32 devices in a mesh: grp: 2 (over x), dom: 16 (over z, y, core).
Axes of the slice: x: 2, y: 2, z: 4, core: 2. Of those that a mesh axis runs over, the one named last changes fastest.
Arguments:
- slabs: bfloat16 [32, 2, 1024, 384], P(('grp', 'dom')), parts along dimension 0, may hold values from -1 to 1
- pair_blocks: int32 [32, 3], P(('grp', 'dom')), parts along dimension 0, may hold values from 0 to 15, as said below
- occ_energy: float32 [32, 2], P('grp'), parts along dimension 0, may hold values from -1.5 to -0.3
- virt_energy: float32 [16384], P('grp'), parts along dimension 0, may hold values from 0.2 to 3
- domain_map: int32 [32, 384], P('grp'), parts along dimension 0, may hold values from 0 to 8191
Outputs:
- residual_slabs: float32 [32, 2, 1024, 384], P(('grp', 'dom')), parts along dimension 0
- metric_gradient: float32 [2048, 1024], P('grp'), parts along dimension 0
The draws below stay inside these ranges and needn't reach their ends.
There are 2 independent parts, one for each index of `grp`. The reference program is written for one: setup_inputs(seed, part) draws one part's arguments, and reference() takes and returns one part's arrays. A program takes and returns all parts, laid end to end along the dimension named above; each array names one. Nothing has to cross between parts.
Inputs may be any that keep to these rules, and one draw needn't show every extreme that they name: `pair_blocks`: each block lists 3 distinct blocks whose index differs from its own by at most 2, possibly itself (a self-pair adds both back-contractions to that block); the first block lists the block 2 above it and the last block the one 2 below it.
All inputs are finite; a program needn't handle non-finite values.
Results may differ from the reference program's by a relative error of at most 0.0015.
Values may be sent and summed in bfloat16 or wider, within the bound.
No kernel may reach another device: no remote copies, remote signals or barrier semaphores. Data moves between devices by JAX's collectives and lax.ppermute only.
A program may use at most 128 MiB of HBM per device.

```python
import jax
import jax.numpy as jnp
from jax import lax

OB = 2
NAUX = 1024
NVIR = 384
NVG = 8192
SLOTS = 3
REACH = 2
BLOCKS = 16


def draw_pair_blocks(key, part):
    key = jax.random.fold_in(key, 11)
    offsets = jnp.arange(-REACH, REACH + 1, dtype=jnp.int32)
    width = 2 * REACH + 1
    candidate = jnp.arange(BLOCKS, dtype=jnp.int32)[:, None] + offsets[None, :]
    allowed = (candidate >= 0) & (candidate < BLOCKS)
    scores = jax.random.randint(key, (BLOCKS, width), 0, 1000, dtype=jnp.int32) * width
    scores = scores + jnp.arange(width, dtype=jnp.int32)[None, :]
    scores = jnp.where(allowed, scores, scores + 1000000)
    ranking = jnp.argsort(scores, axis=1, stable=True)
    chosen = ranking[:, :SLOTS]
    return jnp.take_along_axis(candidate, chosen, axis=1).astype(jnp.int32)


def plant(drawn, key, smallest, high):
    extent = drawn.shape
    index_at = [jax.random.randint(jax.random.fold_in(key, axis), (), 0, extent[axis]) for axis in range(len(extent))]
    drawn = drawn.at[tuple(index_at)].set(smallest)
    longest = extent.index(max(extent))
    index_at[longest] = (index_at[longest] + 1) % extent[longest]
    return drawn.at[tuple(index_at)].set(high)


def shard_levels(rng, shape, split, smallest, high):
    level = 1.0
    for axis_at, blocks in split:
        steps = jax.random.uniform(jax.random.fold_in(jax.random.fold_in(rng, 6), axis_at), (blocks,), jnp.float32, smallest / len(split), high / len(split))
        level = level * jnp.repeat(jnp.exp(steps), shape[axis_at] // blocks).reshape((-1,) + (1,) * (len(shape) - 1 - axis_at))
    return level


def normal_values(own_key, extent, scale, reach, shards=(), kind=jnp.bfloat16):
    gain = shard_levels(own_key, extent, shards, -0.22, 0.18) if shards else 1.0
    array = jax.random.normal(own_key, extent, jnp.float32) * scale * gain
    return jnp.minimum(jnp.maximum(array, -reach), reach).astype(kind)


def setup_inputs(seed: int = 0, part: int = 0) -> dict:
    key_of = jax.random.split(jax.random.key(seed), 6)
    part_keys = jax.random.split(jax.random.fold_in(key_of[5], part), 6)
    return {
        "slabs": normal_values(part_keys[0], (BLOCKS, OB, NAUX, NVIR), 0.18, 1.0, ((0, 16),)),
        "pair_blocks": draw_pair_blocks(jax.random.fold_in(jax.random.fold_in(key_of[5], part), 71), part),
        "occ_energy": jnp.clip(jax.random.uniform(part_keys[2], (BLOCKS, OB), jnp.float32, -1.5, -0.3), -1.5, -0.3),
        "virt_energy": jnp.clip(jax.random.uniform(part_keys[3], (NVG,), jnp.float32, 0.2, 3.0), 0.2, 3.0),
        "domain_map": plant(jax.random.randint(part_keys[4], (BLOCKS, NVIR), 0, NVG), jax.random.fold_in(part_keys[4], 1), 0, NVG - 1).astype(jnp.int32),
    }


def pair_amplitude(slab_first, slab_partner, energy_first, energy_partner, virt_first, virt_partner):
    integrals = jnp.einsum('ipa,jpb->iajb', slab_first.astype(jnp.float32), slab_partner.astype(jnp.float32))
    denominator = (virt_first[None, :, None, None] + virt_partner[None, None, None, :]
                   - energy_first[:, None, None, None] - energy_partner[None, None, :, None])
    return (-integrals / denominator).astype(jnp.bfloat16)


def reference(slabs, pair_blocks, occ_energy, virt_energy, domain_map):
    domain_energy = virt_energy[domain_map]
    flat_pairs = pair_blocks.reshape(-1).astype(jnp.int32)

    def one_pair(pair_index, back_sum):
        first = (pair_index // SLOTS).astype(jnp.int32)
        partner = flat_pairs[pair_index]
        slab_first = slabs[first]
        slab_partner = slabs[partner]
        amplitude = pair_amplitude(slab_first, slab_partner, occ_energy[first], occ_energy[partner],
                                   domain_energy[first], domain_energy[partner])
        widened = amplitude.astype(jnp.float32)
        to_first = jnp.einsum('iajb,jpb->ipa', widened, slab_partner.astype(jnp.float32))
        to_partner = jnp.einsum('iajb,ipa->jpb', widened, slab_first.astype(jnp.float32))
        back_sum = back_sum.at[first].add(to_first)
        back_sum = back_sum.at[partner].add(to_partner)
        return back_sum

    start = jnp.zeros(slabs.shape, jnp.float32)
    back_sum = lax.fori_loop(0, BLOCKS * SLOTS, one_pair, start)
    gradient = jnp.einsum('kipa,kiqa->pq', back_sum, slabs.astype(jnp.float32),
                          precision=lax.Precision.HIGHEST) / BLOCKS
    return back_sum, gradient
```

```python
import functools

import jax
import jax.numpy as jnp
from jax import lax
from jax.experimental import pallas as pl
from jax.experimental.pallas import tpu as pltpu
from jax.sharding import PartitionSpec as P

VMEM_LIMIT = 60 * 1024 * 1024
TILE = 128
NT = (((1,), (1,)), ((), ()))


def move(x, pairs):
    return lax.ppermute(x, "dom", pairs)


def swapped(x, bit):
    return move(x, [(d, d ^ bit) for d in range(lax.axis_size("dom"))])


def shifted(x, distance):
    devices = range(lax.axis_size("dom"))
    return move(x, [(d, d + distance) for d in devices if d + distance in devices])


def forwarded(x):
    devices = range(lax.axis_size("dom"))
    route = [(d, d - 4 if d & 2 else d + 4) for d in devices]
    return move(x, [(a, b) for a, b in route if b in devices])


def to_sibling(x, own_first):
    devices = range(lax.axis_size("dom"))
    return move(x, [(d, d ^ 1) for d in devices if ((d >> 1) ^ d) & 1 == own_first])


def load(copies, sem):
    started = []
    for at, (src, dst) in enumerate(copies):
        copy = pltpu.make_async_copy(src, dst, sem.at[at])
        copy.start()
        started.append(copy)
    return started


def add_pair(own_t, other, amp, total, own_level, other_level, weight, first):
    integrals = jnp.dot(own_t[...], other[...], preferred_element_type=jnp.float32)
    amp[...] = (integrals * weight / (own_level + other_level)).astype(jnp.bfloat16)
    part = lax.dot_general(other[...], amp[...], NT, preferred_element_type=jnp.float32)
    if first:
        total[...] = part
    else:
        total[...] += part


def near_kernel(own, sib, own_level, levels, weights, own_t_out, total_out, sem, own_s, other, own_t, amp, total):
    virt = own.shape[2]
    copies = load(
        [(x.at[j], s.at[:, pl.ds(j * virt, virt)]) for x, s in ((own, own_s), (sib, other)) for j in range(2)],
        sem,
    )
    for c in copies[:2]:
        c.wait()
    own_t[...] = own_s[...].T
    add_pair(own_t, own_s, amp, total, own_level[...], levels[0:1, :], weights[0:1, :], True)
    for c in copies[2:]:
        c.wait()
    add_pair(own_t, other, amp, total, own_level[...], levels[1:2, :], weights[1:2, :], False)
    own_t_out[...] = own_t[...]
    total_out[...] = total[...]


def far_kernel(pick, own_t, total_in, y00, y01, y10, y11, z00, z01, xy0, xz0, own_level, levels, weights, total_out,
               sem, first, second, amp, total):
    half, virt = y00.shape
    a, b = pl.ds(0, virt), pl.ds(virt, virt)
    top, low = pl.ds(0, half), pl.ds(half, half)
    copies = load(
        [
            (y00, first.at[top, a]), (y01, first.at[low, a]),
            (y10, first.at[top, b]), (y11, first.at[low, b]),
            (z00, second.at[top, a]), (z01, second.at[low, a]),
            (total_in, total),
        ],
        sem,
    )

    @pl.when(pick[0] == 1)
    def _():
        pltpu.make_async_copy(xy0, second.at[:, b], sem.at[7]).start()

    @pl.when(pick[0] != 1)
    def _():
        pltpu.make_async_copy(xz0, second.at[:, b], sem.at[7]).start()

    for c in copies[:4]:
        c.wait()
    copies[6].wait()
    add_pair(own_t, first, amp, total, own_level[...], levels[2:3, :], weights[2:3, :], False)
    for c in copies[4:6]:
        c.wait()
    pltpu.make_async_copy(xz0, second.at[:, b], sem.at[7]).wait()
    add_pair(own_t, second, amp, total, own_level[...], levels[3:4, :], weights[3:4, :], False)
    total_out[...] = total[...]


def last_kernel(pick, own_t, total_in, own, z10, z11, xy1, xz1, own_level, levels, weights, residual, metric,
                sem, own_s, second, amp, total):
    half, virt = z10.shape
    a, b = pl.ds(0, virt), pl.ds(virt, virt)
    top, low = pl.ds(0, half), pl.ds(half, half)

    @pl.when(pick[0] == 1)
    def _():
        pltpu.make_async_copy(xy1, second.at[:, b], sem.at[5]).start()

    @pl.when(pick[0] != 1)
    def _():
        pltpu.make_async_copy(xz1, second.at[:, b], sem.at[5]).start()

    copies = load(
        [
            (z10, second.at[top, a]), (z11, second.at[low, a]), (total_in, total),
            (own.at[0], own_s.at[:, a]), (own.at[1], own_s.at[:, b]),
        ],
        sem,
    )
    copies[0].wait()
    copies[1].wait()
    copies[2].wait()
    pltpu.make_async_copy(xz1, second.at[:, b], sem.at[5]).wait()
    add_pair(own_t, second, amp, total, own_level[...], levels[4:5, :], weights[4:5, :], False)
    outs = load([(total.at[:, a], residual.at[0]), (total.at[:, b], residual.at[1])], sem.at[pl.ds(6, 2)])
    copies[3].wait()
    copies[4].wait()
    high = total[...].astype(jnp.bfloat16)
    rest = (total[...] - high.astype(jnp.float32)).astype(jnp.bfloat16)
    metric[...] = lax.dot_general(high, own_s[...], NT, preferred_element_type=jnp.float32) + lax.dot_general(
        rest, own_s[...], NT, preferred_element_type=jnp.float32
    )
    for c in outs:
        c.wait()


def shards(slabs, pair_blocks, occ_energy, virt_energy, domain_map):
    me = lax.axis_index("dom")
    blocks = lax.axis_size("dom")
    own = slabs[0]
    orbitals, aux, virt = own.shape
    half, wide = aux // 2, orbitals * virt

    sib = swapped(own, 1)
    y = [[swapped(own[j, h * half:(h + 1) * half], 2) for h in range(2)] for j in range(2)]
    near_pairs = {step: shifted(pair_blocks[0], -step) for step in (1, -1, 2, -2)}
    z = [[forwarded(c) for c in row] for row in y]
    from_y = [to_sibling(jnp.concatenate(row), 0) for row in y]
    from_z = [to_sibling(jnp.concatenate(row), 1) for row in z]

    parity, core = (me >> 1) & 1, me & 1
    pick = (parity ^ core).astype(jnp.int32)[None]
    offsets = jnp.stack([0 * me, 1 - 2 * core, 2 - 4 * parity, 4 * parity - 2, 2 * core - 1])
    who = me + offsets
    inside = (who >= 0) & (who < blocks)
    who = jnp.clip(who, 0, blocks - 1)
    listed = jnp.any(pair_blocks[0][None, :] == who[:, None], axis=1) & inside
    theirs = jnp.stack([pair_blocks[0]] + [near_pairs[s] for s in (1, -1, 2, -2)])
    row_at = jnp.stack([0 * me, 1 + core, 3 + parity, 4 - parity, 2 - core])
    lists = jnp.any(theirs[row_at] == me, axis=1) & inside
    count = -(listed.astype(jnp.float32) + lists.astype(jnp.float32))
    level = (virt_energy[domain_map[who]][:, None, :] - occ_energy[who][:, :, None])
    weight = jnp.broadcast_to(count[:, None, None], level.shape)

    def rows(x):
        return jnp.stack([
            x[0].reshape(wide), x[1].reshape(wide), x[2].reshape(wide),
            jnp.concatenate([x[3, 0], x[4, 0]]), jnp.concatenate([x[3, 1], x[4, 1]]),
        ])

    levels, weights = rows(level), rows(weight)
    own_level = level[0].reshape(wide, 1)

    hbm = pl.BlockSpec(memory_space=pl.ANY)
    vmem = pl.BlockSpec(memory_space=pltpu.VMEM)
    smem = pl.BlockSpec(memory_space=pltpu.SMEM)
    f32, bf16 = jnp.float32, jnp.bfloat16
    total_s = pltpu.VMEM((aux, wide), f32)
    slab_s = pltpu.VMEM((aux, wide), bf16)
    amp_s = pltpu.VMEM((wide, wide), bf16)
    params = pltpu.CompilerParams(vmem_limit_bytes=VMEM_LIMIT)
    total_t = jax.ShapeDtypeStruct((aux, wide), f32)
    pair_flops = 4 * aux * wide * wide

    def cost(flops, moved):
        return pl.CostEstimate(flops=flops, bytes_accessed=moved, transcendentals=0)

    own_t, total = pl.pallas_call(
        near_kernel,
        out_shape=(jax.ShapeDtypeStruct((wide, aux), bf16), total_t),
        in_specs=[hbm, hbm, vmem, vmem, vmem],
        out_specs=(vmem, vmem),
        scratch_shapes=[pltpu.SemaphoreType.DMA((4,)), slab_s, slab_s, pltpu.VMEM((wide, aux), bf16), amp_s, total_s],
        compiler_params=params,
        cost_estimate=cost(2 * pair_flops, 10 * aux * wide),
        name="near",
    )(own, sib, own_level, levels, weights)
    total = pl.pallas_call(
        far_kernel,
        out_shape=total_t,
        in_specs=[smem, vmem] + [hbm] * 9 + [vmem] * 3,
        out_specs=vmem,
        scratch_shapes=[pltpu.SemaphoreType.DMA((8,)), slab_s, slab_s, amp_s, total_s],
        compiler_params=params,
        cost_estimate=cost(2 * pair_flops, 14 * aux * wide),
        name="far",
    )(pick, own_t, total, y[0][0], y[0][1], y[1][0], y[1][1], z[0][0], z[0][1], from_y[0], from_z[0],
      own_level, levels, weights)
    residual, partial_metric = pl.pallas_call(
        last_kernel,
        out_shape=(jax.ShapeDtypeStruct(own.shape, f32), jax.ShapeDtypeStruct((aux, aux), f32)),
        in_specs=[smem, vmem] + [hbm] * 6 + [vmem] * 3,
        out_specs=(hbm, vmem),
        scratch_shapes=[pltpu.SemaphoreType.DMA((8,)), slab_s, slab_s, amp_s, total_s],
        compiler_params=params,
        cost_estimate=cost(2 * pair_flops, 14 * aux * wide),
        name="last",
    )(pick, own_t, total, own, z[1][0], z[1][1], from_y[1], from_z[1], own_level, levels, weights)
    gradient = lax.psum(partial_metric, "dom") / blocks
    return residual[None], gradient


def solution(mesh):
    return jax.shard_map(
        shards,
        mesh=mesh,
        in_specs=(
            P(("grp", "dom"), None, None, None),
            P(("grp", "dom"), None),
            P("grp", None),
            P("grp"),
            P("grp", None),
        ),
        out_specs=(P(("grp", "dom"), None, None, None), P("grp", None)),
        check_vma=False,
    )
```

```python
import functools

import jax
import jax.numpy as jnp
from jax import lax
from jax.experimental import pallas as pl
from jax.experimental.pallas import tpu as pltpu
from jax.sharding import PartitionSpec as P

VMEM_LIMIT = 60 * 1024 * 1024
LANES = 128
BLOCK = 256
PAD = 16
BITS = 14
NT = (((1,), (1,)), ((), ()))
TN = (((0,), (0,)), ((), ()))
F32, BF16, I16, I32 = jnp.float32, jnp.bfloat16, jnp.int16, jnp.int32


def move(x, pairs):
    return lax.ppermute(x, "dom", pairs)


def swapped(x, bits):
    return move(x, [(d, d ^ bits) for d in range(lax.axis_size("dom"))])


def shifted(x, distance):
    devices = range(lax.axis_size("dom"))
    return move(x, [(d, d + distance) for d in devices if d + distance in devices])


def forwarded(x):
    devices = range(lax.axis_size("dom"))
    route = [(d, d - 4 if d & 2 else d + 4) for d in devices]
    return move(x, [(a, b) for a, b in route if b in devices])


def to_sibling(x, kind):
    devices = range(lax.axis_size("dom"))
    return move(x, [(d, d ^ 1) for d in devices if ((d >> 1) ^ d) & 1 == kind])


def begin(copies, sem, at=0):
    started = [pltpu.make_async_copy(a, b, sem.at[at + i]) for i, (a, b) in enumerate(copies)]
    for copy in started:
        copy.start()
    return started


def finish(copies):
    for copy in copies:
        copy.wait()


def place_of(me):
    return (me >> 1) & 1, me & 1, (me >> 2) & 3


def prep_kernel(blocks, me_ref, pairs, up, down, up2, down2, occ, energy, maps, levels, weights):
    me = me_ref[0]
    parity, core, _ = place_of(me)
    virt = maps.shape[1]
    table = energy[...]
    parts = []
    for _ in range(3):
        part = table.astype(BF16)
        parts.append(part)
        table = table - part.astype(F32)
    offsets = (0, 1 - 2 * core, 2 - 4 * parity, 4 * parity - 2, 2 * core - 1)
    row_major = lax.broadcasted_iota(I32, (energy.shape[0], virt), 0)
    lane_major = lax.broadcasted_iota(I32, (LANES, virt), 0)
    slots = pairs.shape[1]
    for at, offset in enumerate(offsets):
        other = me + offset
        inside = jnp.logical_and(other >= 0, other < blocks).astype(I32)
        who = jnp.clip(other, 0, blocks - 1)
        count = 0
        for s in range(slots):
            theirs = pairs[0, s]
            for step, ref in ((1, up), (-1, down), (2, up2), (-2, down2)):
                theirs = jnp.where(offset == step, ref[0, s], theirs)
            count = count + (pairs[0, s] == other).astype(I32) + (theirs == me).astype(I32)
        weight = -(count * inside).astype(F32)
        index = maps[pl.ds(who, 1), :]
        pick = (row_major == index // LANES).astype(F32).astype(BF16)
        rows = sum(lax.dot_general(p, pick, TN, preferred_element_type=F32) for p in parts)
        chosen = jnp.sum(jnp.where(lane_major == index % LANES, rows, 0.0), axis=0, keepdims=True)
        for j in range(2):
            row, col = (at, j * virt) if at < 3 else (3 + j, (at - 3) * virt)
            levels[row:row + 1, col:col + virt] = chosen - occ[who, j]
            weights[row:row + 1, col:col + virt] = jnp.full((1, virt), weight, F32)


def add_pair(own_t, other, amp, given, total, own_level, levels, weights, step, after=None):
    wide = own_t.shape[0]
    for t in range(0, wide, BLOCK):
        s = pl.ds(t, BLOCK)
        integrals = jnp.dot(own_t[s, :], other[...], preferred_element_type=F32)
        gap = own_level[t:t + BLOCK, 0:1] + levels[step:step + 1, :]
        amp[s, :] = (integrals * weights[step:step + 1, :] / gap).astype(BF16)
    if given is not None:
        given()
    for t in range(0, wide, BLOCK):
        s = pl.ds(t, BLOCK)
        part = lax.dot_general(other[...], amp[s, :], NT, preferred_element_type=F32)
        total[:, s] = part if given is None else total[:, s] + part
        if after is not None:
            after(t + BLOCK)


def near_kernel(own, sib, levels, weights, own_t, total_out, sem, own_s, other, amp, total):
    virt = own.shape[2]
    copies = begin(
        [(x.at[j], s.at[:, pl.ds(j * virt, virt)]) for x, s in ((own, own_s), (sib, other)) for j in range(2)],
        sem,
    )
    level = levels[...].T
    finish(copies[:2])
    own_t[...] = own_s[...].T
    add_pair(own_t, own_s, amp, None, total, level, levels, weights, 0)
    finish(copies[2:])
    outs = []

    def after(done):
        s = pl.ds(done - BLOCK, BLOCK)
        outs.extend(begin([(total.at[:, s], total_out.at[:, s])], sem, 4 + len(outs)))

    add_pair(own_t, other, amp, lambda: None, total, level, levels, weights, 1, after)
    finish(outs)


def load_extra(pick, from_y, from_z, dst, sem):
    @pl.when(pick == 1)
    def _():
        pltpu.make_async_copy(from_y, dst, sem).start()

    @pl.when(pick != 1)
    def _():
        pltpu.make_async_copy(from_z, dst, sem).start()

    return pltpu.make_async_copy(from_z, dst, sem)


def far_kernel(me_ref, own_t_in, total_in, y00, y01, y10, y11, z00, z01, xy0, xz0, levels, weights, total_out,
               sem, own_t, first, second, amp, total):
    half, virt = y00.shape
    parity, core, _ = place_of(me_ref[0])
    a, b = pl.ds(0, virt), pl.ds(virt, virt)
    top, low = pl.ds(0, half), pl.ds(half, half)
    copies = begin(
        [
            (own_t_in, own_t),
            (y00, first.at[top, a]), (y01, first.at[low, a]), (y10, first.at[top, b]), (y11, first.at[low, b]),
            (total_in, total), (z00, second.at[top, a]), (z01, second.at[low, a]),
        ],
        sem,
    )
    extra = load_extra(parity ^ core, xy0, xz0, second.at[:, b], sem.at[8])
    level = levels[...].T
    finish(copies[:5])
    add_pair(own_t, first, amp, copies[5].wait, total, level, levels, weights, 2)
    finish(copies[6:])
    extra.wait()
    outs = []

    def after(done):
        s = pl.ds(done - BLOCK, BLOCK)
        outs.extend(begin([(total.at[:, s], total_out.at[:, s])], sem, 9 + len(outs)))

    add_pair(own_t, second, amp, lambda: None, total, level, levels, weights, 3, after)
    finish(outs)


def last_kernel(me_ref, own_t_in, total_in, own, z10, z11, xy1, xz1, levels, weights, residual, keep, send,
                sem, own_t, own_s, second, amp, total, high, rest, packed):
    half, virt = z10.shape
    parity, core, _ = place_of(me_ref[0])
    a, b = pl.ds(0, virt), pl.ds(virt, virt)
    top, low = pl.ds(0, half), pl.ds(half, half)
    copies = begin(
        [
            (own_t_in, own_t), (z10, second.at[top, a]), (z11, second.at[low, a]), (total_in, total),
            (own.at[0], own_s.at[:, a]), (own.at[1], own_s.at[:, b]),
        ],
        sem,
    )
    extra = load_extra(parity ^ core, xy1, xz1, second.at[:, b], sem.at[6])
    level = levels[...].T
    finish(copies[:3])
    extra.wait()
    add_pair(own_t, second, amp, copies[3].wait, total, level, levels, weights, 4)
    outs = begin([(total.at[:, a], residual.at[0]), (total.at[:, b], residual.at[1])], sem, 7)
    finish(copies[4:])
    high[...] = total[...].astype(BF16)
    rest[...] = (total[...] - high[...].astype(F32)).astype(BF16)
    at = 0
    for q in range(0, total.shape[0], BLOCK):
        rows = q + BLOCK
        slab = own_s[q:q + BLOCK, :]
        block = lax.dot_general(high[:rows, :], slab, NT, preferred_element_type=F32)
        block += lax.dot_general(rest[:rows, :], slab, NT, preferred_element_type=F32)
        for c in range(0, BLOCK, LANES):
            upper = q + c + LANES
            packed[at:at + upper, :] = block[:upper, c:c + LANES]
            at += upper
    size = keep.shape[0]
    outs += begin(
        [(packed.at[pl.ds(core * size, size)], keep), (packed.at[pl.ds((1 - core) * size, size)], send)], sem, 9
    )
    finish(outs)


def encode(x, out, row):
    rows = x.shape[0]
    largest = jnp.max(jnp.abs(x), axis=0, keepdims=True)
    power = jnp.floor(jnp.log2(jnp.maximum(largest, 1e-30))) + 1.0
    out[pl.ds(row, rows), :] = jnp.round(x * jnp.exp2(BITS - power)).astype(I32).astype(I16)
    out[pl.ds(row + rows, PAD), :] = jnp.broadcast_to(power, (PAD, LANES)).astype(I32).astype(I16)


def decode(coded):
    rows = coded.shape[0] - PAD
    wide = coded.astype(I32).astype(F32)
    return wide[:rows] * jnp.exp2(wide[rows:rows + 1] - BITS)


def chip_kernel(me_ref, mine, theirs, keep, send):
    parity, _, _ = place_of(me_ref[0])
    size = keep.shape[0]
    piece = size // 4
    at = pl.ds(pl.multiple_of(parity * size, 16), size)
    keep[...] = mine[at, :] + theirs[at, :]
    for t in range(4):
        at = pl.ds(pl.multiple_of((1 - parity) * size + t * piece, 16), piece)
        encode(mine[at, :] + theirs[at, :], send, t * (piece + PAD))


def column_kernel(me_ref, mine, theirs, keep, *sends):
    _, _, z = place_of(me_ref[0])
    piece = keep.shape[0]
    for t in range(4):
        at = pl.ds(pl.multiple_of((z ^ t) * piece, 16), piece)
        coded = theirs[pl.ds(pl.multiple_of((z ^ t) * (piece + PAD), 16), piece + PAD), :]
        value = mine[at, :] + decode(coded)
        if t:
            encode(value, sends[t - 1], 0)
        else:
            keep[...] = value


def sum_kernel(mine, a, b, c, out):
    out[...] = mine[...] + decode(a[...]) + decode(b[...]) + decode(c[...])


def code_kernel(scale, x, out):
    encode(x[...] * scale, out, 0)


def sum_code_kernel(scale, mine, a, b, c, out):
    encode((mine[...] + decode(a[...]) + decode(b[...]) + decode(c[...])) * scale, out, 0)


def spread_kernel(me_ref, a, b, sib_a, sib_b, out, packed):
    parity, core, z = place_of(me_ref[0])
    rows = a.shape[1] - PAD
    for src, half, side in ((a, core, parity), (b, core, 1 - parity), (sib_a, 1 - core, parity), (sib_b, 1 - core, 1 - parity)):
        for t in range(4):
            row = ((half * 2 + side) * 4 + (z ^ t)) * rows
            packed[pl.ds(pl.multiple_of(row, 16), rows), :] = decode(src[t])
    at = 0
    for c in range(0, out.shape[1], LANES):
        out[0:c + LANES, c:c + LANES] = packed[at:at + c + LANES, :]
        for r in range(0, c, LANES):
            out[c:c + LANES, r:r + LANES] = packed[at + r:at + r + LANES, :].T
        at += c + LANES


def shards(slabs, pair_blocks, occ_energy, virt_energy, domain_map):
    blocks = lax.axis_size("dom")
    me = lax.axis_index("dom").astype(I32)[None]
    own = slabs[0]
    orbitals, aux, virt = own.shape
    half, wide = aux // 2, orbitals * virt
    upper = aux * (aux + LANES) // 2 // LANES
    piece = upper // 16

    hbm = pl.BlockSpec(memory_space=pl.ANY)
    vmem = pl.BlockSpec(memory_space=pltpu.VMEM)
    smem = pl.BlockSpec(memory_space=pltpu.SMEM)
    total_s = pltpu.VMEM((aux, wide), F32)
    slab_s = pltpu.VMEM((aux, wide), BF16)
    amp_s = pltpu.VMEM((wide, wide), BF16)
    own_t_s = pltpu.VMEM((wide, aux), BF16)
    total_t = jax.ShapeDtypeStruct((aux, wide), F32)
    pair_flops = 4 * aux * wide * wide

    def kernel(body, name, ins, outs, out_specs, scratch=(), flops=0, moved=0):
        return pl.pallas_call(
            body,
            out_shape=outs,
            in_specs=ins,
            out_specs=out_specs,
            scratch_shapes=scratch,
            compiler_params=pltpu.CompilerParams(vmem_limit_bytes=VMEM_LIMIT),
            cost_estimate=pl.CostEstimate(flops=flops, bytes_accessed=moved, transcendentals=0),
            name=name,
        )

    def dma(n):
        return pltpu.SemaphoreType.DMA((n,))

    def coded(n):
        return jax.ShapeDtypeStruct((n, LANES), I16)

    def plain(n):
        return jax.ShapeDtypeStruct((n, LANES), F32)

    sib = swapped(own, 1)
    y = [[swapped(own[j, h * half:(h + 1) * half], 2) for h in range(2)] for j in range(2)]
    near_pairs = [shifted(pair_blocks, -step) for step in (1, -1, 2, -2)]

    small = jax.ShapeDtypeStruct((8, wide), F32)
    levels, weights = kernel(
        functools.partial(prep_kernel, blocks), "prep", [smem] * 7 + [vmem] * 2, (small, small), (vmem, vmem),
        flops=1000, moved=100000,
    )(me, pair_blocks, *near_pairs, occ_energy, virt_energy.reshape(-1, LANES), domain_map)
    own_t, total = kernel(
        near_kernel, "near", [hbm, hbm, vmem, vmem], (jax.ShapeDtypeStruct((wide, aux), BF16), total_t), (vmem, hbm),
        [dma(7), slab_s, slab_s, amp_s, total_s], 2 * pair_flops, 10 * aux * wide,
    )(own, sib, levels, weights)

    y[0][1], total, own_t = lax.optimization_barrier((y[0][1], total, own_t))
    z = [[forwarded(c) for c in row] for row in y]
    from_y = [to_sibling(jnp.concatenate(row), 0) for row in y]
    from_z = to_sibling(jnp.concatenate(z[0]), 1)
    total = kernel(
        far_kernel, "far", [smem] + [hbm] * 10 + [vmem] * 2, total_t, hbm,
        [dma(12), own_t_s, slab_s, slab_s, amp_s, total_s], 2 * pair_flops, 14 * aux * wide,
    )(me, own_t, total, y[0][0], y[0][1], y[1][0], y[1][1], z[0][0], z[0][1], from_y[0], from_z, levels, weights)
    z[1][0], z[1][1], total = lax.optimization_barrier((z[1][0], z[1][1], total))
    from_z = to_sibling(jnp.concatenate(z[1]), 1)
    residual, keep, send = kernel(
        last_kernel, "last", [smem] + [hbm] * 7 + [vmem] * 2,
        (jax.ShapeDtypeStruct(own.shape, F32), plain(upper // 2), plain(upper // 2)), (hbm,) * 3,
        [dma(11), own_t_s, slab_s, slab_s, amp_s, total_s, slab_s, slab_s, pltpu.VMEM((upper, LANES), F32)],
        2 * pair_flops, 14 * aux * wide,
    )(me, own_t, total, own, z[1][0], z[1][1], from_y[1], from_z, levels, weights)

    got = swapped(send, 1)
    keep, send = kernel(
        chip_kernel, "chip", [smem, vmem, vmem], (plain(upper // 4), coded(4 * (piece + PAD))), (vmem, vmem),
        moved=upper * LANES * 6,
    )(me, keep, got)
    got = swapped(send, 2)
    keep, *sends = kernel(
        column_kernel, "column", [smem, vmem, vmem], (plain(piece),) + (coded(piece + PAD),) * 3, (vmem,) * 4,
        moved=upper * LANES * 2,
    )(me, keep, got)
    got = [swapped(send, 4 * t) for t, send in zip((1, 2, 3), sends)]
    if blocks == 16:
        mine = kernel(
            functools.partial(sum_code_kernel, 1.0 / blocks), "sum_code", [vmem] * 4, coded(piece + PAD), vmem,
            moved=upper * LANES,
        )(keep, *got)
    else:
        value = kernel(sum_kernel, "sum", [vmem] * 4, plain(piece), vmem)(keep, *got)
        bit = 16
        while bit < blocks:
            value = value + swapped(value, bit)
            bit *= 2
        mine = kernel(functools.partial(code_kernel, 1.0 / blocks), "code", [vmem], coded(piece + PAD), vmem)(value)

    column = [mine] + [swapped(mine, 4 * t) for t in (1, 2, 3)]
    across = [swapped(c, 2) for c in column]
    a, b = jnp.stack(column), jnp.stack(across)
    gradient = kernel(
        spread_kernel, "spread", [smem] + [vmem] * 4, jax.ShapeDtypeStruct((aux, aux), F32), vmem,
        [pltpu.VMEM((upper, LANES), F32)], moved=aux * aux * 6,
    )(me, a, b, swapped(a, 1), swapped(b, 1))
    return residual[None], gradient


def solution(mesh):
    return jax.shard_map(
        shards,
        mesh=mesh,
        in_specs=(
            P(("grp", "dom"), None, None, None),
            P(("grp", "dom"), None),
            P("grp", None),
            P("grp"),
            P("grp", None),
        ),
        out_specs=(P(("grp", "dom"), None, None, None), P("grp", None)),
        check_vma=False,
    )
```

```python
import functools

import jax
import jax.numpy as jnp
from jax import lax
from jax.experimental import pallas as pl
from jax.experimental.pallas import tpu as pltpu
from jax.sharding import PartitionSpec as P

LARGE_LIMIT = 28 * 1024 * 1024
SMALL_LIMIT = 16 * 1024 * 1024
LANES = 128
BLOCK = 256
PAD = 16
GROUP = 32
BITS = 14
NT = (((1,), (1,)), ((), ()))
TN = (((0,), (0,)), ((), ()))
F32, BF16, I16, I32 = jnp.float32, jnp.bfloat16, jnp.int16, jnp.int32


def move(x, pairs):
    return lax.ppermute(x, "dom", pairs)


def swapped(x, bits):
    return move(x, [(d, d ^ bits) for d in range(lax.axis_size("dom"))])


def forwarded(x):
    devices = range(lax.axis_size("dom"))
    route = [(d, d - 4 if d & 2 else d + 4) for d in devices]
    return move(x, [(a, b) for a, b in route if b in devices])


def to_sibling(x, kind):
    devices = range(lax.axis_size("dom"))
    return move(x, [(d, d ^ 1) for d in devices if ((d >> 1) ^ d) & 1 == kind])


def begin(copies, sem, at=0):
    started = [pltpu.make_async_copy(a, b, sem.at[at + i]) for i, (a, b) in enumerate(copies)]
    for copy in started:
        copy.start()
    return started


def finish(copies):
    for copy in copies:
        copy.wait()


def place_of(me):
    return (me >> 1) & 1, me & 1, (me >> 2) & 3


def offsets_of(me):
    parity, core, _ = place_of(me)
    return 0, 1 - 2 * core, 2 - 4 * parity, 4 * parity - 2, 2 * core - 1


OWN, SIB, Y, Z, X = range(5)
STEPS = (((OWN, 0), (OWN, 1)), ((SIB, 0), (SIB, 1)), ((Y, 0), (Z, 0)), ((X, 0), (Y, 1)), ((Z, 1), (X, 1)))


def prep_kernel(blocks, me_ref, pairs, sib_pairs, occ, energy, maps, levels, weights):
    me = me_ref[0]
    virt = maps.shape[1]
    table = energy[...]
    parts = []
    for _ in range(3):
        part = table.astype(BF16)
        parts.append(part)
        table = table - part.astype(F32)
    row_major = lax.broadcasted_iota(I32, (energy.shape[0], virt), 0)
    lane_major = lax.broadcasted_iota(I32, (LANES, virt), 0)
    for block, offset in enumerate(offsets_of(me)):
        other = me + offset
        who = jnp.clip(other, 0, blocks - 1)
        count = 0
        for s in range(pairs.shape[1]):
            count = count + (pairs[0, s] == other).astype(I32)
            if block in (OWN, SIB):
                count = count + ((pairs, sib_pairs)[block][0, s] == me).astype(I32)
        index = maps[pl.ds(who, 1), :]
        pick = (row_major == index // LANES).astype(F32).astype(BF16)
        rows = sum(lax.dot_general(p, pick, TN, preferred_element_type=F32) for p in parts)
        chosen = jnp.sum(jnp.where(lane_major == index % LANES, rows, 0.0), axis=0, keepdims=True)
        for step, halves in enumerate(STEPS):
            for side, (which, j) in enumerate(halves):
                if which == block:
                    at = pl.ds(side * virt, virt)
                    levels[step:step + 1, at] = chosen - occ[who, j]
                    weights[step:step + 1, at] = jnp.full((1, virt), -count.astype(F32), F32)


def add_pair(own_t, other, amp, total, own_level, level, weight, first):
    wide = own_t.shape[0]
    for t in range(0, wide, BLOCK):
        s = pl.ds(t, BLOCK)
        integrals = jnp.dot(own_t[s, :], other[...], preferred_element_type=F32)
        amp[s, :] = (integrals * weight / (own_level[t:t + BLOCK, 0:1] + level)).astype(BF16)
    for t in range(0, wide, BLOCK):
        s = pl.ds(t, BLOCK)
        part = lax.dot_general(other[...], amp[s, :], NT, preferred_element_type=F32)
        total[:, s] = part if first else total[:, s] + part


def split_kernel(me_ref, pairs, own, *rest):
    parts, sem = rest[:-1], rest[-1]
    per = len(parts) // 2
    rows, virt = parts[1].shape
    copies = begin(
        [(own.at[i // per, pl.ds(i % per * rows, rows)], part.at[pl.ds(0, rows)]) for i, part in enumerate(parts)], sem
    )
    lane = lax.broadcasted_iota(I32, (PAD, virt), 1)
    listed = jnp.full((PAD, virt), 100, I32)
    for s in range(pairs.shape[1]):
        listed = jnp.where(lane == s, pairs[0, s] - me_ref[0], listed)
    parts[0][rows:, :] = listed.astype(F32).astype(BF16)
    finish(copies)


def near_kernel(own, sib, levels, weights, own_t, total, sem, own_s, other, amp):
    virt = own.shape[2]
    copies = begin(
        [(x.at[j], s.at[:, pl.ds(j * virt, virt)]) for x, s in ((own, own_s), (sib, other)) for j in range(2)],
        sem,
    )
    level = levels[...].T
    finish(copies[:2])
    own_t[...] = own_s[...].T
    add_pair(own_t, own_s, amp, total, level, levels[0:1, :], weights[0:1, :], True)
    finish(copies[2:])
    add_pair(own_t, other, amp, total, level, levels[1:2, :], weights[1:2, :], False)


def fetch(plan, step, me, refs, other):
    parity, core, _ = place_of(me)
    along_y = (parity ^ core) == 1
    counts = []
    for side, (rows, (name, at)) in enumerate(plan):
        virt = other.shape[1] // 2
        columns = slice(side * virt, (side + 1) * virt)

        def copy(ref_name, first, n, to):
            other[to:to + n, columns] = refs[ref_name][first:first + n, :]

        for source, first, n, to in rows:
            if isinstance(source, str):
                copy(source, first, n, to)
            else:
                pl.when(along_y)(functools.partial(copy, source[0][0], source[0][1], n, to))
                pl.when(jnp.logical_not(along_y))(functools.partial(copy, source[1][0], source[1][1], n, to))
        if isinstance(name, str):
            listed = refs[name][at:at + PAD, :].astype(F32)
        else:
            listed = jnp.where(
                along_y, refs[name[0]][at:at + PAD, :].astype(F32), refs[name[1]][at:at + PAD, :].astype(F32)
            )
        wanted = -offsets_of(me)[STEPS[step][side][0]]
        hits = jnp.where(listed[0:1, :] == wanted.astype(F32), 1.0, 0.0)
        counts.append(jnp.broadcast_to(jnp.sum(hits, axis=1, keepdims=True), (1, virt)))
    return jnp.concatenate(counts, axis=1)


def far_kernel(plan, names, step, me_ref, own_t, total_in, levels, weights, *rest):
    refs = dict(zip(names, rest))
    total, other, amp = rest[len(names):]
    weight = weights[step:step + 1, :] - fetch(plan, step, me_ref[0], refs, other)
    add_pair(own_t, other, amp, total, levels[...].T, levels[step:step + 1, :], weight, False)


def last_kernel(plan, names, step, me_ref, own_t, total_in, levels, weights, own, *rest):
    refs = dict(zip(names, rest))
    total, residual, keep, send, sem, other, amp, own_s, high, low, packed = rest[len(names):]
    me = me_ref[0]
    core = me & 1
    virt = own.shape[2]
    a, b = pl.ds(0, virt), pl.ds(virt, virt)
    copies = begin([(own.at[0], own_s.at[:, a]), (own.at[1], own_s.at[:, b])], sem)
    weight = weights[step:step + 1, :] - fetch(plan, step, me, refs, other)
    add_pair(own_t, other, amp, total, levels[...].T, levels[step:step + 1, :], weight, False)
    outs = begin([(total.at[:, a], residual.at[0]), (total.at[:, b], residual.at[1])], sem, 2)
    finish(copies)
    high[...] = total[...].astype(BF16)
    low[...] = (total[...] - high[...].astype(F32)).astype(BF16)
    at = 0
    for q in range(0, total.shape[0], BLOCK):
        rows = q + BLOCK
        slab = own_s[q:q + BLOCK, :]
        block = lax.dot_general(high[:rows, :], slab, NT, preferred_element_type=F32)
        block += lax.dot_general(low[:rows, :], slab, NT, preferred_element_type=F32)
        for c in range(0, BLOCK, LANES):
            upper = q + c + LANES
            packed[at:at + upper, :] = block[:upper, c:c + LANES]
            at += upper
    size = keep.shape[0]
    keep[...] = packed[pl.ds(pl.multiple_of(core * size, 16), size), :]
    send[...] = packed[pl.ds(pl.multiple_of((1 - core) * size, 16), size), :]
    finish(outs)


def encode(x, out, row):
    rows = x.shape[0]
    groups = x.reshape(rows // GROUP, GROUP, LANES)
    largest = jnp.max(jnp.abs(groups), axis=1)
    power = jnp.floor(jnp.log2(jnp.maximum(largest, 1e-30))) + 1.0
    unit = jnp.exp2(BITS - power)
    for g in range(rows // GROUP):
        whole = jnp.round(groups[g] * unit[g:g + 1, :]).astype(I32)
        out[pl.ds(row + g * GROUP, GROUP), :] = whole.astype(I16)
    pad = jnp.zeros((PAD - rows // GROUP, LANES), F32)
    out[pl.ds(row + rows, PAD), :] = jnp.concatenate([power, pad]).astype(I32).astype(I16)


def decode(coded):
    rows = coded.shape[0] - PAD
    wide = coded.astype(I32).astype(F32)
    unit = jnp.exp2(wide[rows:] - BITS)
    return jnp.concatenate(
        [wide[g * GROUP:(g + 1) * GROUP] * unit[g:g + 1, :] for g in range(rows // GROUP)]
    )


def chip_kernel(me_ref, mine, theirs, keep, send):
    parity, _, _ = place_of(me_ref[0])
    size = keep.shape[0]
    piece = size // 4
    at = pl.ds(pl.multiple_of(parity * size, 16), size)
    keep[...] = mine[at, :] + theirs[at, :]
    for t in range(4):
        at = pl.ds(pl.multiple_of((1 - parity) * size + t * piece, 16), piece)
        encode(mine[at, :] + theirs[at, :], send, t * (piece + PAD))


def column_kernel(me_ref, mine, theirs, keep, *sends):
    _, _, z = place_of(me_ref[0])
    piece = keep.shape[0]
    for t in range(4):
        at = pl.ds(pl.multiple_of((z ^ t) * piece, 16), piece)
        coded = theirs[pl.ds(pl.multiple_of((z ^ t) * (piece + PAD), 16), piece + PAD), :]
        value = mine[at, :] + decode(coded)
        if t:
            encode(value, sends[t - 1], 0)
        else:
            keep[...] = value


def sum_kernel(mine, a, b, c, out):
    out[...] = mine[...] + decode(a[...]) + decode(b[...]) + decode(c[...])


def code_kernel(scale, x, out):
    encode(x[...] * scale, out, 0)


def sum_code_kernel(scale, mine, a, b, c, out):
    encode((mine[...] + decode(a[...]) + decode(b[...]) + decode(c[...])) * scale, out, 0)


def spread_kernel(me_ref, a, b, sib_a, sib_b, out, sem, packed, square):
    parity, core, z = place_of(me_ref[0])
    rows = a.shape[1] - PAD
    for src, half, side in ((a, core, parity), (b, core, 1 - parity), (sib_a, 1 - core, parity), (sib_b, 1 - core, 1 - parity)):
        for t in range(4):
            row = ((half * 2 + side) * 4 + (z ^ t)) * rows
            packed[pl.ds(pl.multiple_of(row, 16), rows), :] = decode(src[t])
    copies = []
    at = packed.shape[0]
    for c in range(out.shape[1] - LANES, -1, -LANES):
        at -= c + LANES
        square[0:c + LANES, c:c + LANES] = packed[at:at + c + LANES, :]
        for r in range(0, c, LANES):
            square[c:c + LANES, r:r + LANES] = packed[at + r:at + r + LANES, :].T
        done = pl.ds(c, LANES)
        copies += begin([(square.at[done], out.at[done])], sem, len(copies))
    finish(copies)


def shards(slabs, pair_blocks, occ_energy, virt_energy, domain_map):
    blocks = lax.axis_size("dom")
    me = lax.axis_index("dom").astype(I32)[None]
    own = slabs[0]
    orbitals, aux, virt = own.shape
    wide = orbitals * virt
    upper = aux * (aux + LANES) // 2 // LANES
    piece = upper // 16

    hbm = pl.BlockSpec(memory_space=pl.ANY)
    vmem = pl.BlockSpec(memory_space=pltpu.VMEM)
    smem = pl.BlockSpec(memory_space=pltpu.SMEM)
    slab_s = pltpu.VMEM((aux, wide), BF16)
    amp_s = pltpu.VMEM((wide, wide), BF16)
    total_t = jax.ShapeDtypeStruct((aux, wide), F32)

    def kernel(body, name, ins, outs, out_specs, scratch=(), limit=SMALL_LIMIT, aliases={}, flops=1):
        return pl.pallas_call(
            body,
            out_shape=outs,
            in_specs=ins,
            out_specs=out_specs,
            scratch_shapes=scratch,
            compiler_params=pltpu.CompilerParams(vmem_limit_bytes=limit),
            cost_estimate=pl.CostEstimate(flops=flops, bytes_accessed=1, transcendentals=0),
            input_output_aliases=aliases,
            name=name,
        )

    def dma(n):
        return pltpu.SemaphoreType.DMA((n,))

    def coded(n):
        return jax.ShapeDtypeStruct((n, LANES), I16)

    def plain(n):
        return jax.ShapeDtypeStruct((n, LANES), F32)

    half = aux // 2
    sib, sib_pairs = swapped(own, 1), swapped(pair_blocks, 1)
    parts = kernel(
        split_kernel, "split", [smem, smem, hbm],
        [jax.ShapeDtypeStruct((half + (0 if i else PAD), virt), BF16) for i in range(4)], [vmem] * 4, [dma(4)],
    )(me, pair_blocks, own)
    y = [swapped(parts[0], 2)]
    sib, part = lax.optimization_barrier((sib, parts[1]))
    y.append(swapped(part, 2))

    small = jax.ShapeDtypeStruct((8, wide), F32)
    levels, weights = kernel(
        functools.partial(prep_kernel, blocks), "prep", [smem] * 4 + [vmem] * 2, (small, small), (vmem, vmem),
    )(me, pair_blocks, sib_pairs, occ_energy, virt_energy.reshape(-1, LANES), domain_map)
    own_t, total = kernel(
        near_kernel, "near", [hbm, hbm, vmem, vmem], (jax.ShapeDtypeStruct((wide, aux), BF16), total_t), (vmem, vmem),
        [dma(4), slab_s, slab_s, amp_s], LARGE_LIMIT, flops=int(5e10),
    )(own, sib, levels, weights)
    y[0], total, own_t, part = lax.optimization_barrier((y[0], total, own_t, parts[2]))
    y.append(swapped(part, 2))
    y[1], part = lax.optimization_barrier((y[1], parts[3]))
    y.append(swapped(part, 2))

    z = [forwarded(part) for part in y]
    z[0], z[1], y[2], y[3] = lax.optimization_barrier((z[0], z[1], y[2], y[3]))
    arrays = {f"y{i}": part for i, part in enumerate(y)}
    arrays |= {f"z{i}": part for i, part in enumerate(z)}
    arrays["sy0"] = to_sibling(jnp.concatenate(y[:2]), 0)
    arrays["sz0"] = to_sibling(jnp.concatenate(z[:2]), 1)
    arrays["sy2"] = to_sibling(jnp.concatenate(y[2:]), 0)

    def own_core(name, j):
        return [(f"{name}{2 * j + h}", 0, half, h * half) for h in range(2)], (f"{name}0", half)

    def other_core(j):
        if j:
            rows = [((("sy2", h * half), (f"sz{2 + h}", 0)), 0, half, h * half) for h in range(2)]
        else:
            rows = [((("sy0", at), ("sz0", at)), 0, half, to) for at, to in ((0, 0), (half + PAD, half))]
        return rows, (("sy0", "sz0"), half)

    def names_in(plan):
        names = []
        for rows, (name, _) in plan:
            for source in [r[0] for r in rows]:
                names += [source] if isinstance(source, str) else [n for n, _ in source]
            names += [name] if isinstance(name, str) else name
        return list(dict.fromkeys(names))

    def pair_step(body, name, step, given=(), outs=(), out_specs=(), scratch=()):
        plan = [other_core(j) if which == X else own_core("y" if which == Y else "z", j) for which, j in STEPS[step]]
        names = names_in(plan)
        return kernel(
            functools.partial(body, plan, names, step), name,
            [smem] + [vmem] * 4 + [hbm] * len(given) + [vmem] * len(names),
            (total_t, *outs), (vmem, *out_specs), scratch, LARGE_LIMIT, {2: 0}, int(1e10),
        )(me, own_t, total, levels, weights, *given, *[arrays[n] for n in names])

    (total,) = pair_step(far_kernel, "far2", 2, scratch=[slab_s, amp_s])
    (total,) = pair_step(far_kernel, "far3", 3, scratch=[slab_s, amp_s])
    z[2], z[3], total = lax.optimization_barrier((z[2], z[3], total))
    arrays["z2"], arrays["z3"] = z[2], z[3]
    arrays["sz2"], arrays["sz3"] = to_sibling(z[2], 1), to_sibling(z[3], 1)
    _, residual, keep, send = pair_step(
        last_kernel, "last", 4, (own,),
        (jax.ShapeDtypeStruct(own.shape, F32), plain(upper // 2), plain(upper // 2)), (hbm, vmem, vmem),
        [dma(4), slab_s, amp_s, slab_s, slab_s, slab_s, pltpu.VMEM((upper, LANES), F32)],
    )

    got = swapped(send, 1)
    keep, send = kernel(
        chip_kernel, "chip", [smem, vmem, vmem], (plain(upper // 4), coded(4 * (piece + PAD))), (vmem, vmem),
    )(me, keep, got)
    got = swapped(send, 2)
    keep, *sends = kernel(
        column_kernel, "column", [smem, vmem, vmem], (plain(piece),) + (coded(piece + PAD),) * 3, (vmem,) * 4,
    )(me, keep, got)
    got = [swapped(send, 4 * t) for t, send in zip((1, 2, 3), sends)]
    if blocks == 16:
        mine = kernel(
            functools.partial(sum_code_kernel, 1.0 / blocks), "sum_code", [vmem] * 4, coded(piece + PAD), vmem,
        )(keep, *got)
    else:
        value = kernel(sum_kernel, "sum", [vmem] * 4, plain(piece), vmem)(keep, *got)
        bit = 16
        while bit < blocks:
            value = value + swapped(value, bit)
            bit *= 2
        mine = kernel(functools.partial(code_kernel, 1.0 / blocks), "code", [vmem], coded(piece + PAD), vmem)(value)

    column = [mine] + [swapped(mine, 4 * t) for t in (1, 2, 3)]
    across = [swapped(c, 2) for c in column]
    a, b = jnp.stack(column), jnp.stack(across)
    gradient = kernel(
        spread_kernel, "spread", [smem] + [vmem] * 4, jax.ShapeDtypeStruct((aux, aux), F32), hbm,
        [dma(aux // LANES), pltpu.VMEM((upper, LANES), F32), pltpu.VMEM((aux, aux), F32)],
    )(me, a, b, swapped(a, 1), swapped(b, 1))
    return residual[None], gradient


def solution(mesh):
    return jax.shard_map(
        shards,
        mesh=mesh,
        in_specs=(
            P(("grp", "dom"), None, None, None),
            P(("grp", "dom"), None),
            P("grp", None),
            P("grp"),
            P("grp", None),
        ),
        out_specs=(P(("grp", "dom"), None, None, None), P("grp", None)),
        check_vma=False,
    )
```

```python
import functools

import jax
import jax.numpy as jnp
from jax import lax
from jax.experimental import pallas as pl
from jax.experimental.pallas import tpu as pltpu
from jax.sharding import PartitionSpec as P

LARGE_LIMIT = 28 * 1024 * 1024
SMALL_LIMIT = 16 * 1024 * 1024
LANES = 128
BLOCK = 256
PAD = 16
PER = 2
GROUP = 32
BITS = 14
NT = (((1,), (1,)), ((), ()))
TN = (((0,), (0,)), ((), ()))
F32, BF16, I16, I32 = jnp.float32, jnp.bfloat16, jnp.int16, jnp.int32


def move(x, pairs):
    return lax.ppermute(x, "dom", pairs)


def swapped(x, bits):
    return move(x, [(d, d ^ bits) for d in range(lax.axis_size("dom"))])


def forwarded(x):
    devices = range(lax.axis_size("dom"))
    route = [(d, d - 4 if d & 2 else d + 4) for d in devices]
    return move(x, [(a, b) for a, b in route if b in devices])


def to_sibling(x, kind):
    devices = range(lax.axis_size("dom"))
    return move(x, [(d, d ^ 1) for d in devices if ((d >> 1) ^ d) & 1 == kind])


def begin(copies, sem, at=0):
    started = [pltpu.make_async_copy(a, b, sem.at[at + i]) for i, (a, b) in enumerate(copies)]
    for copy in started:
        copy.start()
    return started


def finish(copies):
    for copy in copies:
        copy.wait()


def place_of(me):
    return (me >> 1) & 1, me & 1, (me >> 2) & 3


def offsets_of(me):
    parity, core, _ = place_of(me)
    return 0, 1 - 2 * core, 2 - 4 * parity, 4 * parity - 2, 2 * core - 1


OWN, SIB, Y, Z, X = range(5)
STEPS = (((OWN, 0), (OWN, 1)), ((SIB, 0), (SIB, 1)), ((Y, 0), (Z, 0)), ((X, 0), (Y, 1)), ((Z, 1), (X, 1)))


def prep_kernel(blocks, me_ref, pairs, sib_pairs, occ_in, energy_in, maps_in, levels, weights, sem, occ, energy, maps):
    copies = begin([(occ_in, occ), (energy_in, energy), (maps_in, maps)], sem)
    me = me_ref[0]
    virt = maps.shape[1]
    finish(copies)
    table = energy[...]
    parts = []
    for _ in range(3):
        part = table.astype(BF16)
        parts.append(part)
        table = table - part.astype(F32)
    block_major = lax.broadcasted_iota(I32, occ.shape, 1)
    row_major = lax.broadcasted_iota(I32, (energy.shape[0], virt), 0)
    lane_major = lax.broadcasted_iota(I32, (LANES, virt), 0)
    for block, offset in enumerate(offsets_of(me)):
        other = me + offset
        who = jnp.clip(other, 0, blocks - 1)
        count = 0
        for s in range(pairs.shape[1]):
            count = count + (pairs[0, s] == other).astype(I32)
            if block in (OWN, SIB):
                count = count + ((pairs, sib_pairs)[block][0, s] == me).astype(I32)
        occupied = jnp.sum(jnp.where(block_major == who, occ[...], 0.0), axis=1, keepdims=True)
        index = maps[pl.ds(who, 1), :]
        pick = (row_major == index // LANES).astype(F32).astype(BF16)
        rows = sum(lax.dot_general(p, pick, TN, preferred_element_type=F32) for p in parts)
        chosen = jnp.sum(jnp.where(lane_major == index % LANES, rows, 0.0), axis=0, keepdims=True)
        for step, halves in enumerate(STEPS):
            for side, (which, j) in enumerate(halves):
                if which == block:
                    at = pl.ds(side * virt, virt)
                    levels[step:step + 1, at] = chosen - occupied[j:j + 1, :]
                    weights[step:step + 1, at] = jnp.full((1, virt), -count.astype(F32), F32)


def add_pair(own_t, other, amp, total, own_level, level, weight, first, halves=None):
    wide = own_t.shape[0]
    for t in range(0, wide, BLOCK):
        s = pl.ds(t, BLOCK)
        integrals = jnp.dot(own_t[s, :], other[...], preferred_element_type=F32)
        amp[s, :] = (integrals * weight / (own_level[t:t + BLOCK, 0:1] + level)).astype(BF16)
    for t in range(0, wide, BLOCK):
        s = pl.ds(t, BLOCK)
        part = lax.dot_general(other[...], amp[s, :], NT, preferred_element_type=F32)
        value = part if first else total[:, s] + part
        total[:, s] = value
        if halves is not None:
            high = value.astype(BF16)
            halves[0][:, s] = high
            halves[1][:, s] = (value - high.astype(F32)).astype(BF16)


def split_kernel(places, me_ref, pairs, own, *rest):
    parts, sem = rest[:-1], rest[-1]
    copies = begin(
        [(own.at[j, pl.ds(a, n)], part.at[pl.ds(0, n)]) for (j, a, n), part in zip(places, parts)], sem
    )
    rows, virt = parts[0].shape[0] - PAD, parts[0].shape[1]
    lane = lax.broadcasted_iota(I32, (PAD, virt), 1)
    listed = jnp.full((PAD, virt), 100, I32)
    for s in range(pairs.shape[1]):
        listed = jnp.where(lane == s, pairs[0, s] - me_ref[0], listed)
    parts[0][rows:, :] = listed.astype(F32).astype(BF16)
    finish(copies)


def own_kernel(own, levels, weights, own_t, total, sem, own_s, amp):
    virt = own.shape[2]
    copies = begin([(own.at[j], own_s.at[:, pl.ds(j * virt, virt)]) for j in range(2)], sem)
    level = levels[...].T
    finish(copies)
    own_t[...] = own_s[...].T
    add_pair(own_t, own_s, amp, total, level, levels[0:1, :], weights[0:1, :], True)


def sib_kernel(own_t, total_in, sib, levels, weights, total, sem, other, amp):
    virt = sib.shape[2]
    copies = begin([(sib.at[j], other.at[:, pl.ds(j * virt, virt)]) for j in range(2)], sem)
    level = levels[...].T
    finish(copies)
    add_pair(own_t, other, amp, total, level, levels[1:2, :], weights[1:2, :], False)


def fetch(plan, step, me, refs, other):
    parity, core, _ = place_of(me)
    along_y = (parity ^ core) == 1
    counts = []
    for side, (rows, (name, at)) in enumerate(plan):
        virt = other.shape[1] // 2
        columns = slice(side * virt, (side + 1) * virt)

        def copy(ref_name, first, n, to):
            other[to:to + n, columns] = refs[ref_name][first:first + n, :]

        for source, first, n, to in rows:
            if isinstance(source, str):
                copy(source, first, n, to)
            else:
                pl.when(along_y)(functools.partial(copy, source[0][0], source[0][1], n, to))
                pl.when(jnp.logical_not(along_y))(functools.partial(copy, source[1][0], source[1][1], n, to))
        if isinstance(name, str):
            listed = refs[name][at:at + PAD, :].astype(F32)
        else:
            listed = jnp.where(
                along_y, refs[name[0]][at:at + PAD, :].astype(F32), refs[name[1]][at:at + PAD, :].astype(F32)
            )
        wanted = -offsets_of(me)[STEPS[step][side][0]]
        hits = jnp.where(listed[0:1, :] == wanted.astype(F32), 1.0, 0.0)
        counts.append(jnp.broadcast_to(jnp.sum(hits, axis=1, keepdims=True), (1, virt)))
    return jnp.concatenate(counts, axis=1)


def far_kernel(plan, names, step, me_ref, own_t, total_in, levels, weights, *rest):
    refs = dict(zip(names, rest))
    total, other, amp = rest[len(names):]
    weight = weights[step:step + 1, :] - fetch(plan, step, me_ref[0], refs, other)
    add_pair(own_t, other, amp, total, levels[...].T, levels[step:step + 1, :], weight, False)


def last_kernel(plan, names, step, me_ref, own_t, total_in, levels, weights, own, *rest):
    refs = dict(zip(names, rest))
    total, residual, *quarters, sem, other, amp, own_s, high, low, packed = rest[len(names):]
    me = me_ref[0]
    parity, core, _ = place_of(me)
    virt = own.shape[2]
    a, b = pl.ds(0, virt), pl.ds(virt, virt)
    for j, at in enumerate((a, b)):
        own_s[:, at] = own[j]
    weight = weights[step:step + 1, :] - fetch(plan, step, me, refs, other)
    add_pair(own_t, other, amp, total, levels[...].T, levels[step:step + 1, :], weight, False, (high, low))
    outs = begin([(total.at[:, a], residual.at[0]), (total.at[:, b], residual.at[1])], sem)
    at = 0
    for q in range(0, total.shape[0], BLOCK):
        rows = q + BLOCK
        slab = own_s[q:q + BLOCK, :]
        block = lax.dot_general(high[:rows, :], slab, NT, preferred_element_type=F32)
        block += lax.dot_general(low[:rows, :], slab, NT, preferred_element_type=F32)
        for c in range(0, BLOCK, LANES):
            upper = q + c + LANES
            packed[at:at + upper, :] = block[:upper, c:c + LANES]
            at += upper
    size = quarters[0].shape[0]
    where = ((core, 1 - parity), (core, parity), (1 - core, 1 - parity), (1 - core, parity))
    for out, (half, side) in zip(quarters, where):
        out[...] = packed[pl.ds(pl.multiple_of((2 * half + side) * size, 16), size), :]
    finish(outs)


def encode(x, out, row):
    rows = x.shape[0]
    groups = x.reshape(rows // GROUP, GROUP, LANES)
    largest = jnp.max(jnp.abs(groups), axis=1)
    power = jnp.floor(jnp.log2(jnp.maximum(largest, 1e-30))) + 1.0
    unit = jnp.exp2(BITS - power)
    for g in range(rows // GROUP):
        whole = jnp.round(groups[g] * unit[g:g + 1, :]).astype(I32)
        out[pl.ds(row + g * GROUP, GROUP), :] = whole.astype(I16)
    pad = jnp.zeros((PAD - rows // GROUP, LANES), F32)
    out[pl.ds(row + rows, PAD), :] = jnp.concatenate([power, pad]).astype(I32).astype(I16)


def decode(coded):
    rows = coded.shape[0] - PAD
    wide = coded.astype(I32).astype(F32)
    unit = jnp.exp2(wide[rows:] - BITS)
    return jnp.concatenate(
        [wide[g * GROUP:(g + 1) * GROUP] * unit[g:g + 1, :] for g in range(rows // GROUP)]
    )


def chip_kernel(mine, theirs, send):
    piece = mine.shape[0] // 4
    for t in range(4):
        at = pl.ds(t * piece, piece)
        encode(mine[at, :] + theirs[at, :], send, t * (piece + PAD))


def column_kernel(me_ref, mine, theirs, across, keep, *sends):
    _, _, z = place_of(me_ref[0])
    piece = keep.shape[0]
    for t in range(4):
        at = pl.ds(pl.multiple_of((z ^ t) * piece, 16), piece)
        coded = across[pl.ds(pl.multiple_of((z ^ t) * (piece + PAD), 16), piece + PAD), :]
        value = mine[at, :] + theirs[at, :] + decode(coded)
        if t:
            encode(value, sends[t - 1], 0)
        else:
            keep[...] = value


def sum_kernel(mine, a, b, c, out):
    out[...] = mine[...] + decode(a[...]) + decode(b[...]) + decode(c[...])


def code_kernel(scale, x, out):
    encode(x[...] * scale, out, 0)


def sum_code_kernel(scale, mine, a, b, c, out):
    encode((mine[...] + decode(a[...]) + decode(b[...]) + decode(c[...])) * scale, out, 0)


def spread_kernel(me_ref, a, b, sib_a, sib_b, out, sem, packed, square):
    parity, core, z = place_of(me_ref[0])
    rows = a.shape[1] - PAD
    for src, half, side in ((a, core, parity), (b, core, 1 - parity), (sib_a, 1 - core, parity), (sib_b, 1 - core, 1 - parity)):
        for t in range(4):
            row = ((half * 2 + side) * 4 + (z ^ t)) * rows
            packed[pl.ds(pl.multiple_of(row, 16), rows), :] = decode(src[t])
    copies = []
    at = packed.shape[0]
    for c in range(out.shape[1] - LANES, -1, -LANES):
        at -= c + LANES
        square[0:c + LANES, c:c + LANES] = packed[at:at + c + LANES, :]
        for r in range(0, c, LANES):
            square[c:c + LANES, r:r + LANES] = packed[at + r:at + r + LANES, :].T
        done = pl.ds(c, LANES)
        copies += begin([(square.at[done], out.at[done])], sem, len(copies))
    finish(copies)


def shards(slabs, pair_blocks, occ_energy, virt_energy, domain_map):
    blocks = lax.axis_size("dom")
    me = lax.axis_index("dom").astype(I32)[None]
    own = slabs[0]
    orbitals, aux, virt = own.shape
    wide = orbitals * virt
    upper = aux * (aux + LANES) // 2 // LANES
    piece = upper // 16

    hbm = pl.BlockSpec(memory_space=pl.ANY)
    vmem = pl.BlockSpec(memory_space=pltpu.VMEM)
    smem = pl.BlockSpec(memory_space=pltpu.SMEM)
    slab_s = pltpu.VMEM((aux, wide), BF16)
    amp_s = pltpu.VMEM((wide, wide), BF16)
    total_t = jax.ShapeDtypeStruct((aux, wide), F32)

    def kernel(body, name, ins, outs, out_specs, scratch=(), limit=SMALL_LIMIT, aliases={}, flops=1):
        return pl.pallas_call(
            body,
            out_shape=outs,
            in_specs=ins,
            out_specs=out_specs,
            scratch_shapes=scratch,
            compiler_params=pltpu.CompilerParams(vmem_limit_bytes=limit),
            cost_estimate=pl.CostEstimate(flops=flops, bytes_accessed=1, transcendentals=0),
            input_output_aliases=aliases,
            name=name,
        )

    def dma(n):
        return pltpu.SemaphoreType.DMA((n,))

    def coded(n):
        return jax.ShapeDtypeStruct((n, LANES), I16)

    def plain(n):
        return jax.ShapeDtypeStruct((n, LANES), F32)

    cuts = [[at * aux // PER + (PAD if at and at < PER and not j else 0) for at in range(PER + 1)] for j in range(orbitals)]
    places = [(j, a, b - a) for j in range(orbitals) for a, b in zip(cuts[j], cuts[j][1:])]
    count = len(places)
    part = own[0, :places[0][2]]
    y = [swapped(part, 2)]
    sib_pairs = swapped(pair_blocks, 1)
    later, part = lax.optimization_barrier((own, part))
    sib = swapped(later, 1)
    parts = [None, *kernel(
        functools.partial(split_kernel, places[1:]), "split", [smem, smem, hbm],
        [jax.ShapeDtypeStruct((n + (0 if i else PAD), virt), BF16) for i, (_, _, n) in enumerate(places[1:])],
        [vmem] * (count - 1), [dma(count - 1)],
    )(me, pair_blocks, later)]

    small = jax.ShapeDtypeStruct((8, wide), F32)
    energy = virt_energy.reshape(-1, LANES)
    levels, weights = kernel(
        functools.partial(prep_kernel, blocks), "prep", [smem] * 3 + [hbm] * 3, (small, small), (vmem, vmem),
        [dma(3), pltpu.VMEM((orbitals, blocks), F32), pltpu.VMEM(energy.shape, F32), pltpu.VMEM(domain_map.shape, I32)],
    )(me, pair_blocks, sib_pairs, occ_energy.T, energy, domain_map)
    sib, near_own = lax.optimization_barrier((sib, own))
    own_t, total = kernel(
        own_kernel, "own", [hbm, vmem, vmem], (jax.ShapeDtypeStruct((wide, aux), BF16), total_t), (vmem, vmem),
        [dma(2), slab_s, amp_s], LARGE_LIMIT, flops=int(2e10),
    )(near_own, levels, weights)
    sib, part = lax.optimization_barrier((sib, parts[1]))
    y.append(swapped(part, 2))
    y[0], total, own_t, sib, part = lax.optimization_barrier((y[0], total, own_t, sib, parts[2]))
    y.append(swapped(part, 2))
    z = [forwarded(y[0])]
    total = kernel(
        sib_kernel, "sib", [vmem, vmem, hbm, vmem, vmem], total_t, vmem, [dma(2), slab_s, amp_s], LARGE_LIMIT, {1: 0},
        int(1e10),
    )(own_t, total, sib, levels, weights)
    y[1], total, part = lax.optimization_barrier((y[1], total, parts[3]))
    y.append(swapped(part, 2))
    z.append(forwarded(y[1]))
    for i in range(4, count):
        y[i - 2], part, _ = lax.optimization_barrier((y[i - 2], parts[i], y[i - 3]))
        y.append(swapped(part, 2))
        z.append(forwarded(y[i - 2]))
    y[-2], z[0] = lax.optimization_barrier((y[-2], z[0]))
    z.append(forwarded(y[-2]))

    arrays = {f"y{i}": part for i, part in enumerate(y)}
    arrays |= {f"z{i}": part for i, part in enumerate(z)}
    arrays["sy0"] = to_sibling(jnp.concatenate(y[:PER]), 0)
    arrays["sz0"] = to_sibling(jnp.concatenate(z[:PER]), 1)

    def own_core(name, j):
        rows = [(f"{name}{i}", 0, n, to) for i, (k, to, n) in enumerate(places) if k == j]
        return rows, (f"{name}1", places[1][2])

    def other_core(j):
        rows = []
        for h, (_, to, n) in enumerate(places[j * PER:(j + 1) * PER]):
            if not j:
                at = to + (PAD if h > 1 else 0)
                rows.append(((("sy0", at), ("sz0", at)), 0, n, to))
            elif h < PER - 1:
                rows.append(((("sy1", to), ("sz1", to)), 0, n, to))
            else:
                rows.append(((("sy1", to), ("sz2", 0)), 0, n, to))
        return rows, (("sy0", "sz0"), places[0][2] + places[1][2])

    def names_in(plan):
        names = []
        for rows, (name, _) in plan:
            for source in [r[0] for r in rows]:
                names += [source] if isinstance(source, str) else [n for n, _ in source]
            names += [name] if isinstance(name, str) else name
        return list(dict.fromkeys(names))

    def pair_step(body, name, step, given=(), outs=(), out_specs=(), scratch=(), flops=1):
        plan = [other_core(j) if which == X else own_core("y" if which == Y else "z", j) for which, j in STEPS[step]]
        names = names_in(plan)
        return kernel(
            functools.partial(body, plan, names, step), name,
            [smem] + [vmem] * (4 + len(given) + len(names)),
            (total_t, *outs), (vmem, *out_specs), scratch, LARGE_LIMIT, {2: 0}, flops,
        )(me, own_t, total, levels, weights, *given, *[arrays[n] for n in names])

    z.append(forwarded(y[-1]))
    y[-1], total = lax.optimization_barrier((y[-1], total))
    arrays[f"y{count - 1}"] = y[-1]
    (total,) = pair_step(far_kernel, "far2", 2, scratch=[slab_s, amp_s], flops=int(1e10))
    (total,) = pair_step(far_kernel, "far3", 3, scratch=[slab_s, amp_s], flops=1)
    total, *late = lax.optimization_barrier((total, *y[PER:], *z[PER:-1]))
    y[PER:], z[PER:-1] = late[:PER], late[PER:]
    arrays["sy1"] = to_sibling(jnp.concatenate(y[PER:]), 0)
    arrays["sz1"] = to_sibling(jnp.concatenate(z[PER:-1]), 1)
    z[-1], total, arrays["sz1"] = lax.optimization_barrier((z[-1], total, arrays["sz1"]))
    arrays["sz2"] = to_sibling(z[-1], 1)
    arrays |= {f"z{i}": part for i, part in enumerate(z)}
    _, residual, *quarters = pair_step(
        last_kernel, "last", 4, (own,),
        (jax.ShapeDtypeStruct(own.shape, F32),) + (plain(upper // 4),) * 4, (hbm,) + (vmem,) * 4,
        [dma(2), slab_s, amp_s, slab_s, slab_s, slab_s, pltpu.VMEM((upper, LANES), F32)],
    )

    got = swapped(quarters[2], 1)
    got, send = lax.optimization_barrier((got, quarters[3]))
    got_own = swapped(send, 1)
    send = kernel(chip_kernel, "chip", [vmem, vmem], coded(4 * (piece + PAD)), vmem)(quarters[0], got)
    across = swapped(send, 2)
    keep, *sends = kernel(
        column_kernel, "column", [smem, vmem, vmem, vmem], (plain(piece),) + (coded(piece + PAD),) * 3, (vmem,) * 4,
    )(me, quarters[1], got_own, across)
    got = [swapped(send, 4 * t) for t, send in zip((1, 2, 3), sends)]
    if blocks == 16:
        mine = kernel(
            functools.partial(sum_code_kernel, 1.0 / blocks), "sum_code", [vmem] * 4, coded(piece + PAD), vmem,
        )(keep, *got)
    else:
        value = kernel(sum_kernel, "sum", [vmem] * 4, plain(piece), vmem)(keep, *got)
        bit = 16
        while bit < blocks:
            value = value + swapped(value, bit)
            bit *= 2
        mine = kernel(functools.partial(code_kernel, 1.0 / blocks), "code", [vmem], coded(piece + PAD), vmem)(value)

    column = [mine] + [swapped(mine, 4 * t) for t in (1, 2, 3)]
    across = [swapped(c, 2) for c in column]
    a, b = jnp.stack(column), jnp.stack(across)
    gradient = kernel(
        spread_kernel, "spread", [smem] + [vmem] * 4, jax.ShapeDtypeStruct((aux, aux), F32), hbm,
        [dma(aux // LANES), pltpu.VMEM((upper, LANES), F32), pltpu.VMEM((aux, aux), F32)],
    )(me, a, b, swapped(a, 1), swapped(b, 1))
    return residual[None], gradient


def solution(mesh):
    return jax.shard_map(
        shards,
        mesh=mesh,
        in_specs=(
            P(("grp", "dom"), None, None, None),
            P(("grp", "dom"), None),
            P("grp", None),
            P("grp"),
            P("grp", None),
        ),
        out_specs=(P(("grp", "dom"), None, None, None), P("grp", None)),
        check_vma=False,
    )
```

```python
import functools

import jax
import jax.numpy as jnp
from jax import lax
from jax.experimental import pallas as pl
from jax.experimental.pallas import tpu as pltpu
from jax.sharding import PartitionSpec as P

LARGE_LIMIT = 28 * 1024 * 1024
SMALL_LIMIT = 16 * 1024 * 1024
LANES = 128
BLOCK = 256
PAD = 16
PER = 2
GROUP = 32
BITS = 14
NT = (((1,), (1,)), ((), ()))
TN = (((0,), (0,)), ((), ()))
F32, BF16, I16, I32 = jnp.float32, jnp.bfloat16, jnp.int16, jnp.int32


def move(x, pairs):
    return lax.ppermute(x, "dom", pairs)


def swapped(x, bits):
    return move(x, [(d, d ^ bits) for d in range(lax.axis_size("dom"))])


def forwarded(x):
    devices = range(lax.axis_size("dom"))
    route = [(d, d - 4 if d & 2 else d + 4) for d in devices]
    return move(x, [(a, b) for a, b in route if b in devices])


def begin(copies, sem, at=0):
    started = [pltpu.make_async_copy(a, b, sem.at[at + i]) for i, (a, b) in enumerate(copies)]
    for copy in started:
        copy.start()
    return started


def finish(copies):
    for copy in copies:
        copy.wait()


def place_of(me):
    return (me >> 1) & 1, me & 1, (me >> 2) & 3


def offsets_of(me):
    parity, core, _ = place_of(me)
    return 0, 1 - 2 * core, 2 - 4 * parity, 4 * parity - 2, 2 * core - 1


OWN, SIB, Y, Z, X = range(5)
STEPS = (((OWN, 0), (OWN, 1)), ((SIB, 0), (SIB, 1)), ((Y, 0), (Y, 1)), ((Z, 0), (X, 0)), ((Z, 1), (X, 1)))


def prep_kernel(blocks, me_ref, pairs, sib_pairs, occ_in, energy_in, maps_in, levels, weights, sem, occ, energy, maps):
    copies = begin([(occ_in, occ), (energy_in, energy), (maps_in, maps)], sem)
    me = me_ref[0]
    virt = maps.shape[1]
    finish(copies)
    table = energy[...]
    parts = []
    for _ in range(3):
        part = table.astype(BF16)
        parts.append(part)
        table = table - part.astype(F32)
    block_major = lax.broadcasted_iota(I32, occ.shape, 1)
    row_major = lax.broadcasted_iota(I32, (energy.shape[0], virt), 0)
    lane_major = lax.broadcasted_iota(I32, (LANES, virt), 0)
    for block, offset in enumerate(offsets_of(me)):
        other = me + offset
        who = jnp.clip(other, 0, blocks - 1)
        count = 0
        for s in range(pairs.shape[1]):
            count = count + (pairs[0, s] == other).astype(I32)
            if block in (OWN, SIB):
                count = count + ((pairs, sib_pairs)[block][0, s] == me).astype(I32)
        occupied = jnp.sum(jnp.where(block_major == who, occ[...], 0.0), axis=1, keepdims=True)
        index = maps[pl.ds(who, 1), :]
        pick = (row_major == index // LANES).astype(F32).astype(BF16)
        rows = sum(lax.dot_general(p, pick, TN, preferred_element_type=F32) for p in parts)
        chosen = jnp.sum(jnp.where(lane_major == index % LANES, rows, 0.0), axis=0, keepdims=True)
        for step, halves in enumerate(STEPS):
            for side, (which, j) in enumerate(halves):
                if which == block:
                    at = pl.ds(side * virt, virt)
                    levels[step:step + 1, at] = chosen - occupied[j:j + 1, :]
                    weights[step:step + 1, at] = jnp.full((1, virt), -count.astype(F32), F32)


def add_pair(own_t, other, amp, total, own_level, level, weight, first, halves=None, near=None):
    wide = own_t.shape[0]
    for t in range(0, wide, BLOCK):
        s = pl.ds(t, BLOCK)
        integrals = jnp.dot(own_t[s, :], other[...], preferred_element_type=F32)
        amp[s, :] = (integrals * weight / (own_level[t:t + BLOCK, 0:1] + level)).astype(BF16)
    for t in range(0, wide, BLOCK):
        s = pl.ds(t, BLOCK)
        part = lax.dot_general(other[...], amp[s, :], NT, preferred_element_type=F32)
        value = part if first else total[:, s] + part
        total[:, s] = value if near is None else value + near[:, s]
        if halves is not None:
            high = value.astype(BF16)
            halves[0][:, s] = high
            halves[1][:, s] = (value - high.astype(F32)).astype(BF16)


def split_kernel(places, me_ref, pairs, own, *rest):
    parts, sem = rest[:-1], rest[-1]
    copies = begin(
        [(own.at[j, pl.ds(a, n)], part.at[pl.ds(0, n)]) for (j, a, n), part in zip(places, parts)], sem
    )
    rows, virt = parts[0].shape[0] - PAD, parts[0].shape[1]
    lane = lax.broadcasted_iota(I32, (PAD, virt), 1)
    listed = jnp.full((PAD, virt), 100, I32)
    for s in range(pairs.shape[1]):
        listed = jnp.where(lane == s, pairs[0, s] - me_ref[0], listed)
    parts[0][rows:, :] = listed.astype(F32).astype(BF16)
    finish(copies)


def own_kernel(own, levels, weights, own_t, own_s, total, sem, amp):
    virt = own.shape[2]
    copies = begin([(own.at[j], own_s.at[:, pl.ds(j * virt, virt)]) for j in range(2)], sem)
    level = levels[...].T
    finish(copies)
    own_t[...] = own_s[...].T
    add_pair(own_t, own_s, amp, total, level, levels[0:1, :], weights[0:1, :], True)


def sib_kernel(own_t, total_in, sib, levels, weights, total, sem, other, amp):
    virt = sib.shape[2]
    copies = begin([(sib.at[j], other.at[:, pl.ds(j * virt, virt)]) for j in range(2)], sem)
    level = levels[...].T
    finish(copies)
    add_pair(own_t, other, amp, total, level, levels[1:2, :], weights[1:2, :], False)


def fetch(plan, step, me, refs, other):
    counts = []
    for side, (rows, (name, at)) in enumerate(plan):
        virt = other.shape[1] // 2
        for source, first, n, to in rows:
            other[to:to + n, side * virt:(side + 1) * virt] = refs[source][first:first + n, :]
        wanted = -offsets_of(me)[STEPS[step][side][0]]
        hits = jnp.where(refs[name][at:at + PAD, :].astype(F32)[0:1, :] == wanted.astype(F32), 1.0, 0.0)
        counts.append(jnp.broadcast_to(jnp.sum(hits, axis=1, keepdims=True), (1, virt)))
    return jnp.concatenate(counts, axis=1)


def first_far_kernel(plan, names, step, me_ref, own_t, levels, weights, *rest):
    refs = dict(zip(names, rest))
    total, other, amp = rest[len(names):]
    weight = weights[step:step + 1, :] - fetch(plan, step, me_ref[0], refs, other)
    add_pair(own_t, other, amp, total, levels[...].T, levels[step:step + 1, :], weight, True)


def far_kernel(plan, names, step, me_ref, own_t, levels, weights, total_in, *rest):
    refs = dict(zip(names, rest))
    total, other, amp = rest[len(names):]
    weight = weights[step:step + 1, :] - fetch(plan, step, me_ref[0], refs, other)
    add_pair(own_t, other, amp, total, levels[...].T, levels[step:step + 1, :], weight, False)


def near_metric_kernel(me_ref, total, own_s, keep, away, *rest):
    *sends, high, low, packed = rest
    parity, core, _ = place_of(me_ref[0])
    high[...] = total[...].astype(BF16)
    low[...] = (total[...] - high[...].astype(F32)).astype(BF16)
    aux = total.shape[0]
    half, quarter = aux // 2, aux // 4
    plane = packed.shape[0] // 2
    square = plane - half // LANES * quarter
    for q in range(0, aux, BLOCK):
        rows = q + BLOCK
        slab = own_s[q:q + BLOCK, :]
        block = lax.dot_general(high[:rows, :], slab, NT, preferred_element_type=F32)
        block += lax.dot_general(low[:rows, :], slab, NT, preferred_element_type=F32)
        for c in range(q, q + BLOCK, LANES):
            column = block[:, c - q:c - q + LANES]
            base, side = (half, 1) if c >= half else (0, 0)
            k = (c - base) // LANES
            at = side * plane + k * (k + 1) // 2 * LANES
            packed[at:at + (k + 1) * LANES, :] = column[base:c + LANES, :]
            if side:
                for s in range(2):
                    at = s * plane + square + k * quarter
                    packed[at:at + quarter, :] = column[s * quarter:(s + 1) * quarter, :]
    size = plane // 2

    def part(side, which):
        return packed[pl.ds(pl.multiple_of((2 * side + which) * size, 16), size), :]

    keep[...] = part(parity, core)
    away[...] = part(1 - parity, core)
    given = [part(1 - parity, 1 - core), part(parity, 1 - core)]
    piece = size // 4
    for send, x in zip(sends, given):
        for t in range(4):
            encode(x[t * piece:(t + 1) * piece, :], send, t * (piece + PAD))


def last_kernel(plan, names, step, me_ref, own_t, levels, weights, total_in, own_s, near, *rest):
    refs = dict(zip(names, rest))
    total, residual, keep, send, sem, other, amp, high, low, packed = rest[len(names):]
    me = me_ref[0]
    parity, core, _ = place_of(me)
    aux, wide = total.shape
    virt = wide // 2
    weight = weights[step:step + 1, :] - fetch(plan, step, me, refs, other)
    add_pair(own_t, other, amp, total, levels[...].T, levels[step:step + 1, :], weight, False, (high, low), near)
    copies = begin([(total.at[:, pl.ds(j * virt, virt)], residual.at[j]) for j in range(2)], sem)
    half, quarter = aux // 2, aux // 4

    def both(first, n, q):
        rows, columns = pl.ds(pl.multiple_of(first, 16), n), pl.ds(pl.multiple_of(q, 16), BLOCK)
        pairs = ((high, own_s), (low, own_s), (own_s, high), (own_s, low))
        return sum(
            lax.dot_general(a[rows, :], b[columns, :], NT, preferred_element_type=F32) for a, b in pairs
        )

    at = 0
    for q in range(0, half, BLOCK):
        block = both(parity * half, q + BLOCK, parity * half + q)
        for c in range(0, BLOCK, LANES):
            upper = q + c + LANES
            packed[at:at + upper, :] = block[:upper, c:c + LANES]
            at += upper
    for q in range(half, aux, BLOCK):
        block = both(parity * quarter, quarter, q)
        for c in range(0, BLOCK, LANES):
            packed[at:at + quarter, :] = block[:, c:c + LANES]
            at += quarter
    size = keep.shape[0]
    keep[...] = packed[pl.ds(pl.multiple_of(core * size, 16), size), :]
    send[...] = packed[pl.ds(pl.multiple_of((1 - core) * size, 16), size), :]
    finish(copies)


def encode(x, out, row):
    rows = x.shape[0]
    groups = x.reshape(rows // GROUP, GROUP, LANES)
    largest = jnp.max(jnp.abs(groups), axis=1)
    power = jnp.floor(jnp.log2(jnp.maximum(largest, 1e-30))) + 1.0
    unit = jnp.exp2(BITS - power)
    for g in range(rows // GROUP):
        whole = jnp.round(groups[g] * unit[g:g + 1, :]).astype(I32)
        out[pl.ds(row + g * GROUP, GROUP), :] = whole.astype(I16)
    pad = jnp.zeros((PAD - rows // GROUP, LANES), F32)
    out[pl.ds(row + rows, PAD), :] = jnp.concatenate([power, pad]).astype(I32).astype(I16)


def decode(coded):
    rows = coded.shape[0] - PAD
    wide = coded.astype(I32).astype(F32)
    unit = jnp.exp2(wide[rows:] - BITS)
    return jnp.concatenate(
        [wide[g * GROUP:(g + 1) * GROUP] * unit[g:g + 1, :] for g in range(rows // GROUP)]
    )


def chip_kernel(keep_in, away, got_away, got_keep, keep, send):
    piece = keep.shape[0] // 4
    for t in range(4):
        at, coded = pl.ds(t * piece, piece), pl.ds(t * (piece + PAD), piece + PAD)
        encode(away[at, :] + decode(got_away[coded, :]), send, t * (piece + PAD))
        keep[at, :] = keep_in[at, :] + decode(got_keep[coded, :])


def column_kernel(me_ref, mine, theirs, near, across, keep, *sends):
    _, _, z = place_of(me_ref[0])
    piece = keep.shape[0]
    for t in range(4):
        at = pl.ds(pl.multiple_of((z ^ t) * piece, 16), piece)
        coded = across[pl.ds(pl.multiple_of((z ^ t) * (piece + PAD), 16), piece + PAD), :]
        value = (mine[at, :] + theirs[at, :]) + (near[at, :] + decode(coded))
        if t:
            encode(value, sends[t - 1], 0)
        else:
            keep[...] = value


def sum_kernel(mine, a, b, c, out):
    out[...] = mine[...] + decode(a[...]) + decode(b[...]) + decode(c[...])


def code_kernel(scale, x, out):
    encode(x[...] * scale, out, 0)


def sum_code_kernel(scale, mine, a, b, c, out):
    encode((mine[...] + decode(a[...]) + decode(b[...]) + decode(c[...])) * scale, out, 0)


def spread_kernel(me_ref, a, b, sib_a, sib_b, out, sem, packed, square):
    parity, core, z = place_of(me_ref[0])
    rows = a.shape[1] - PAD
    aux = out.shape[1]
    half, quarter = aux // 2, aux // 4
    plane = packed.shape[0] // 2
    sources = ((a, core, parity), (b, core, 1 - parity), (sib_a, 1 - core, parity), (sib_b, 1 - core, 1 - parity))
    for src, which, side in sources:
        for t in range(4):
            row = ((side * 2 + which) * 4 + (z ^ t)) * rows
            packed[pl.ds(pl.multiple_of(row, 16), rows), :] = decode(src[t])
    for side in range(2):
        at = side * plane + plane - half // LANES * quarter
        for c in range(half, aux, LANES):
            first = side * quarter
            square[first:first + quarter, c:c + LANES] = packed[at:at + quarter, :]
            for r in range(0, quarter, LANES):
                square[c:c + LANES, first + r:first + r + LANES] = packed[at + r:at + r + LANES, :].T
            at += quarter
    copies = []
    for side in range(2):
        at = side * plane + plane - half // LANES * quarter
        base = side * half
        for c in range(half - LANES, -1, -LANES):
            at -= c + LANES
            columns = slice(base + c, base + c + LANES)
            square[base:base + c + LANES, columns] = packed[at:at + c + LANES, :]
            for r in range(0, c, LANES):
                square[columns, base + r:base + r + LANES] = packed[at + r:at + r + LANES, :].T
            done = pl.ds(base + c, LANES)
            copies += begin([(square.at[done], out.at[done])], sem, len(copies))
    finish(copies)


def shards(slabs, pair_blocks, occ_energy, virt_energy, domain_map):
    blocks = lax.axis_size("dom")
    me = lax.axis_index("dom").astype(I32)[None]
    own = slabs[0]
    orbitals, aux, virt = own.shape
    wide = orbitals * virt
    upper = aux * (aux + LANES) // 2 // LANES
    piece = upper // 16

    hbm = pl.BlockSpec(memory_space=pl.ANY)
    vmem = pl.BlockSpec(memory_space=pltpu.VMEM)
    smem = pl.BlockSpec(memory_space=pltpu.SMEM)
    slab_s = pltpu.VMEM((aux, wide), BF16)
    amp_s = pltpu.VMEM((wide, wide), BF16)
    total_t = jax.ShapeDtypeStruct((aux, wide), F32)

    def kernel(body, name, ins, outs, out_specs, scratch=(), limit=SMALL_LIMIT, aliases={}, flops=1):
        return pl.pallas_call(
            body,
            out_shape=outs,
            in_specs=ins,
            out_specs=out_specs,
            scratch_shapes=scratch,
            compiler_params=pltpu.CompilerParams(vmem_limit_bytes=limit),
            cost_estimate=pl.CostEstimate(flops=flops, bytes_accessed=1, transcendentals=0),
            input_output_aliases=aliases,
            name=name,
        )

    def dma(n):
        return pltpu.SemaphoreType.DMA((n,))

    def coded(n):
        return jax.ShapeDtypeStruct((n, LANES), I16)

    def plain(n):
        return jax.ShapeDtypeStruct((n, LANES), F32)

    cuts = [[at * aux // PER + (PAD if at and at < PER and not j else 0) for at in range(PER + 1)] for j in range(orbitals)]
    places = [(j, a, b - a) for j in range(orbitals) for a, b in zip(cuts[j], cuts[j][1:])]
    count = len(places)
    part = own[0, :places[0][2]]
    y = [swapped(part, 2)]
    sib_pairs = swapped(pair_blocks, 1)
    later, part = lax.optimization_barrier((own, part))
    sib = swapped(later, 1)
    parts = [None, *kernel(
        functools.partial(split_kernel, places[1:]), "split", [smem, smem, hbm],
        [jax.ShapeDtypeStruct((n + (0 if i else PAD), virt), BF16) for i, (_, _, n) in enumerate(places[1:])],
        [vmem] * (count - 1), [dma(count - 1)],
    )(me, pair_blocks, later)]

    small = jax.ShapeDtypeStruct((8, wide), F32)
    energy = virt_energy.reshape(-1, LANES)
    levels, weights = kernel(
        functools.partial(prep_kernel, blocks), "prep", [smem] * 3 + [hbm] * 3, (small, small), (vmem, vmem),
        [dma(3), pltpu.VMEM((orbitals, blocks), F32), pltpu.VMEM(energy.shape, F32), pltpu.VMEM(domain_map.shape, I32)],
    )(me, pair_blocks, sib_pairs, occ_energy.T, energy, domain_map)
    sib, near_own = lax.optimization_barrier((sib, own))
    own_t, own_s, total = kernel(
        own_kernel, "own", [hbm, vmem, vmem],
        (jax.ShapeDtypeStruct((wide, aux), BF16), jax.ShapeDtypeStruct((aux, wide), BF16), total_t), (vmem,) * 3,
        [dma(2), amp_s], LARGE_LIMIT, flops=int(2e10),
    )(near_own, levels, weights)
    sib, part = lax.optimization_barrier((sib, parts[1]))
    y.append(swapped(part, 2))
    y[0], total, own_t, sib, part = lax.optimization_barrier((y[0], total, own_t, sib, parts[2]))
    y.append(swapped(part, 2))
    z = [forwarded(y[0])]
    total = kernel(
        sib_kernel, "sib", [vmem, vmem, hbm, vmem, vmem], total_t, vmem, [dma(2), slab_s, amp_s], LARGE_LIMIT, {1: 0},
        int(1e10),
    )(own_t, total, sib, levels, weights)
    y[1], total, part = lax.optimization_barrier((y[1], total, parts[3]))
    y.append(swapped(part, 2))
    z.append(forwarded(y[1]))
    for i in range(4, count):
        y[i - 2], part, _ = lax.optimization_barrier((y[i - 2], parts[i], y[i - 3]))
        y.append(swapped(part, 2))
        z.append(forwarded(y[i - 2]))
    y[-2], z[0] = lax.optimization_barrier((y[-2], z[0]))
    z.append(forwarded(y[-2]))

    y[-2], near = lax.optimization_barrier((y[-2], total))
    keep, away, *sends = kernel(
        near_metric_kernel, "near_metric", [smem, vmem, vmem], (plain(upper // 4),) * 2 + (coded(4 * (piece + PAD)),) * 2,
        (vmem,) * 4, [slab_s, slab_s, pltpu.VMEM((upper, LANES), F32)], LARGE_LIMIT, flops=int(1e10),
    )(me, near, own_s)
    got = [swapped(send, 1) for send in sends]
    y[-1], *got = lax.optimization_barrier((y[-1], *got))
    z.append(forwarded(y[-1]))
    keep, send = kernel(
        chip_kernel, "chip", [vmem] * 4, (plain(upper // 4), coded(4 * (piece + PAD))), (vmem, vmem),
    )(keep, away, *got)
    across = swapped(send, 2)
    y[-1], own_t, keep = lax.optimization_barrier((y[-1], own_t, keep))

    gives_y = ((me[0] >> 1) ^ me[0]) & 1 == 0

    def given(rows_y, rows_z):
        return swapped(jnp.where(gives_y, jnp.concatenate(rows_y), jnp.concatenate(rows_z)), 1)

    arrays = {f"y{i}": part for i, part in enumerate(y)}
    arrays |= {f"z{i}": part for i, part in enumerate(z)}
    arrays["x0"] = given(y[:PER], z[:PER])

    def half_of(which, j):
        name = "y" if which == Y else "z"
        if which != X:
            rows = [(f"{name}{i}", 0, n, to) for i, (k, to, n) in enumerate(places) if k == j]
            return rows, (f"{name}1", places[1][2])
        if j:
            cut = places[-1][1]
            rows = [("x1", 0, cut // 2, 0), ("x2", 0, cut // 2, cut // 2), ("x3", 0, aux - cut, cut)]
        else:
            cut = places[0][2] + places[1][2]
            rows = [("x0", 0, cut, 0)] + ([("x0", cut + PAD, aux - cut, cut)] if cut < aux else [])
        return rows, ("x0", places[0][2] + places[1][2])

    def pair_step(body, name, step, before=(), outs=(), out_specs=(), scratch=(), flops=1):
        plan = [half_of(*half) for half in STEPS[step]]
        names = list(dict.fromkeys(n for rows, (at, _) in plan for n in [r[0] for r in rows] + [at]))
        return kernel(
            functools.partial(body, plan, names, step), name,
            [smem] + [vmem] * (3 + len(before) + len(names)),
            (total_t, *outs), (vmem, *out_specs), scratch, LARGE_LIMIT, {4: 0} if before else {}, flops,
        )(me, own_t, levels, weights, *before, *[arrays[n] for n in names])

    (total,) = pair_step(first_far_kernel, "far2", 2, scratch=[slab_s, amp_s], flops=int(1e10))
    (total,) = pair_step(far_kernel, "far3", 3, (total,), scratch=[slab_s, amp_s], flops=1)
    total, *late = lax.optimization_barrier((total, *y[PER:-1], *z[PER:-1]))
    early = [jnp.where(gives_y, a, b) for a, b in zip(late[:PER - 1], late[PER - 1:])]
    early = jnp.concatenate(early)
    middle = early.shape[0] // 2
    arrays["x1"], arrays["x2"] = swapped(early[:middle], 1), swapped(early[middle:], 1)
    z[-1], total, arrays["x1"], arrays["x2"], across = lax.optimization_barrier(
        (z[-1], total, arrays["x1"], arrays["x2"], across)
    )
    arrays[f"z{count - 1}"] = z[-1]
    arrays["x3"] = given(y[-1:], z[-1:])
    _, residual, mine, send = pair_step(
        last_kernel, "last", 4, (total, own_s, near),
        (jax.ShapeDtypeStruct(own.shape, F32), plain(upper // 4), plain(upper // 4)), (hbm, vmem, vmem),
        [dma(2), slab_s, amp_s, slab_s, slab_s, pltpu.VMEM((upper // 2, LANES), F32)],
    )

    got = swapped(send, 1)
    keep, *sends = kernel(
        column_kernel, "column", [smem] + [vmem] * 4, (plain(piece),) + (coded(piece + PAD),) * 3, (vmem,) * 4,
    )(me, mine, got, keep, across)
    got = [swapped(send, 4 * t) for t, send in zip((1, 2, 3), sends)]
    if blocks == 16:
        mine = kernel(
            functools.partial(sum_code_kernel, 1.0 / blocks), "sum_code", [vmem] * 4, coded(piece + PAD), vmem,
        )(keep, *got)
    else:
        value = kernel(sum_kernel, "sum", [vmem] * 4, plain(piece), vmem)(keep, *got)
        bit = 16
        while bit < blocks:
            value = value + swapped(value, bit)
            bit *= 2
        mine = kernel(functools.partial(code_kernel, 1.0 / blocks), "code", [vmem], coded(piece + PAD), vmem)(value)

    column = [mine] + [swapped(mine, 4 * t) for t in (1, 2, 3)]
    across = [swapped(c, 2) for c in column]
    a, b = jnp.stack(column), jnp.stack(across)
    gradient = kernel(
        spread_kernel, "spread", [smem] + [vmem] * 4, jax.ShapeDtypeStruct((aux, aux), F32), hbm,
        [dma(aux // LANES), pltpu.VMEM((upper, LANES), F32), pltpu.VMEM((aux, aux), F32)],
    )(me, a, b, swapped(a, 1), swapped(b, 1))
    return residual[None], gradient


def solution(mesh):
    return jax.shard_map(
        shards,
        mesh=mesh,
        in_specs=(
            P(("grp", "dom"), None, None, None),
            P(("grp", "dom"), None),
            P("grp", None),
            P("grp"),
            P("grp", None),
        ),
        out_specs=(P(("grp", "dom"), None, None, None), P("grp", None)),
        check_vma=False,
    )
```

```python
import functools

import jax
import jax.numpy as jnp
from jax import lax
from jax.experimental import pallas as pl
from jax.experimental.pallas import tpu as pltpu
from jax.sharding import PartitionSpec as P

LARGE_LIMIT = 16 * 1024 * 1024
SMALL_LIMIT = 8 * 1024 * 1024
LANES = 128
BLOCK = 256
PAD = 16
PER = 2
GROUP = 32
BITS = 14
NT = (((1,), (1,)), ((), ()))
TN = (((0,), (0,)), ((), ()))
F32, BF16, I16, I32 = jnp.float32, jnp.bfloat16, jnp.int16, jnp.int32


def move(x, pairs):
    return lax.ppermute(x, "dom", pairs)


def swapped(x, bits):
    return move(x, [(d, d ^ bits) for d in range(lax.axis_size("dom"))])


def forwarded(x):
    devices = range(lax.axis_size("dom"))
    route = [(d, d - 4 if d & 2 else d + 4) for d in devices]
    return move(x, [(a, b) for a, b in route if b in devices])


def begin(copies, sem, at=0):
    started = [pltpu.make_async_copy(a, b, sem.at[at + i]) for i, (a, b) in enumerate(copies)]
    for copy in started:
        copy.start()
    return started


def finish(copies):
    for copy in copies:
        copy.wait()


def place_of(me):
    return (me >> 1) & 1, me & 1, (me >> 2) & 3


def offsets_of(me):
    parity, core, _ = place_of(me)
    return 0, 1 - 2 * core, 2 - 4 * parity, 4 * parity - 2, 2 * core - 1


OWN, SIB, Y, Z, X = range(5)
STEPS = (((OWN, 0), (OWN, 1)), ((SIB, 0), (SIB, 1)), ((Y, 0), (Y, 1)), ((Z, 0), (X, 0)), ((Z, 1), (X, 1)))


def prep_kernel(blocks, me_ref, pairs, sib_pairs, occ_in, energy_in, maps_in, levels, weights, sem, occ, energy, maps):
    copies = begin([(occ_in, occ), (energy_in, energy), (maps_in, maps)], sem)
    me = me_ref[0]
    virt = maps.shape[1]
    finish(copies)
    table = energy[...]
    parts = []
    for _ in range(3):
        part = table.astype(BF16)
        parts.append(part)
        table = table - part.astype(F32)
    block_major = lax.broadcasted_iota(I32, occ.shape, 1)
    row_major = lax.broadcasted_iota(I32, (energy.shape[0], virt), 0)
    lane_major = lax.broadcasted_iota(I32, (LANES, virt), 0)
    for block, offset in enumerate(offsets_of(me)):
        other = me + offset
        who = jnp.clip(other, 0, blocks - 1)
        count = 0
        for s in range(pairs.shape[1]):
            count = count + (pairs[0, s] == other).astype(I32)
            if block in (OWN, SIB):
                count = count + ((pairs, sib_pairs)[block][0, s] == me).astype(I32)
        occupied = jnp.sum(jnp.where(block_major == who, occ[...], 0.0), axis=1, keepdims=True)
        index = maps[pl.ds(who, 1), :]
        pick = (row_major == index // LANES).astype(F32).astype(BF16)
        rows = sum(lax.dot_general(p, pick, TN, preferred_element_type=F32) for p in parts)
        chosen = jnp.sum(jnp.where(lane_major == index % LANES, rows, 0.0), axis=0, keepdims=True)
        for step, halves in enumerate(STEPS):
            for side, (which, j) in enumerate(halves):
                if which == block:
                    at = pl.ds(side * virt, virt)
                    levels[step:step + 1, at] = chosen - occupied[j:j + 1, :]
                    weights[step:step + 1, at] = jnp.full((1, virt), -count.astype(F32), F32)


def add_pair(own_t, other, amp, total, own_level, level, weight, first, halves=None, near=None):
    wide = own_t.shape[0]
    for t in range(0, wide, BLOCK):
        s = pl.ds(t, BLOCK)
        integrals = jnp.dot(own_t[s, :], other[...], preferred_element_type=F32)
        amp[s, :] = (integrals * weight / (own_level[t:t + BLOCK, 0:1] + level)).astype(BF16)
    for t in range(0, wide, BLOCK):
        s = pl.ds(t, BLOCK)
        part = lax.dot_general(other[...], amp[s, :], NT, preferred_element_type=F32)
        value = part if first else total[:, s] + part
        total[:, s] = value if near is None else value + near[:, s]
        if halves is not None:
            high = value.astype(BF16)
            halves[0][:, s] = high
            halves[1][:, s] = (value - high.astype(F32)).astype(BF16)


def split_kernel(places, me_ref, pairs, own, *rest):
    parts, sem = rest[:-1], rest[-1]
    copies = begin(
        [(own.at[j, pl.ds(a, n)], part.at[pl.ds(0, n)]) for (j, a, n), part in zip(places, parts)], sem
    )
    rows, virt = parts[0].shape[0] - PAD, parts[0].shape[1]
    lane = lax.broadcasted_iota(I32, (PAD, virt), 1)
    listed = jnp.full((PAD, virt), 100, I32)
    for s in range(pairs.shape[1]):
        listed = jnp.where(lane == s, pairs[0, s] - me_ref[0], listed)
    parts[0][rows:, :] = listed.astype(F32).astype(BF16)
    finish(copies)


def own_kernel(own, levels, weights, own_t, own_s, total, sem, amp):
    virt = own.shape[2]
    copies = begin([(own.at[j], own_s.at[:, pl.ds(j * virt, virt)]) for j in range(2)], sem)
    level = levels[...].T
    finish(copies)
    own_t[...] = own_s[...].T
    add_pair(own_t, own_s, amp, total, level, levels[0:1, :], weights[0:1, :], True)


def sib_kernel(own_t, total_in, sib, levels, weights, total, sem, other, amp):
    virt = sib.shape[2]
    copies = begin([(sib.at[j], other.at[:, pl.ds(j * virt, virt)]) for j in range(2)], sem)
    level = levels[...].T
    finish(copies)
    add_pair(own_t, other, amp, total, level, levels[1:2, :], weights[1:2, :], False)


def fetch(plan, step, me, refs, other):
    counts = []
    for side, (rows, (name, at)) in enumerate(plan):
        virt = other.shape[1] // 2
        for source, first, n, to in rows:
            other[to:to + n, side * virt:(side + 1) * virt] = refs[source][first:first + n, :]
        wanted = -offsets_of(me)[STEPS[step][side][0]]
        hits = jnp.where(refs[name][at:at + PAD, :].astype(F32)[0:1, :] == wanted.astype(F32), 1.0, 0.0)
        counts.append(jnp.broadcast_to(jnp.sum(hits, axis=1, keepdims=True), (1, virt)))
    return jnp.concatenate(counts, axis=1)


def first_far_kernel(plan, names, step, me_ref, own_t, levels, weights, *rest):
    refs = dict(zip(names, rest))
    total, other, amp = rest[len(names):]
    weight = weights[step:step + 1, :] - fetch(plan, step, me_ref[0], refs, other)
    add_pair(own_t, other, amp, total, levels[...].T, levels[step:step + 1, :], weight, True)


def far_kernel(plan, names, step, me_ref, own_t, levels, weights, total_in, *rest):
    refs = dict(zip(names, rest))
    total, other, amp = rest[len(names):]
    weight = weights[step:step + 1, :] - fetch(plan, step, me_ref[0], refs, other)
    add_pair(own_t, other, amp, total, levels[...].T, levels[step:step + 1, :], weight, False)


def near_metric_kernel(me_ref, total, own_s, keep, away, *rest):
    *sends, high, low, packed = rest
    parity, core, _ = place_of(me_ref[0])
    high[...] = total[...].astype(BF16)
    low[...] = (total[...] - high[...].astype(F32)).astype(BF16)
    aux = total.shape[0]
    half, quarter = aux // 2, aux // 4
    plane = packed.shape[0] // 2
    square = plane - half // LANES * quarter
    for q in range(0, aux, BLOCK):
        rows = q + BLOCK
        slab = own_s[q:q + BLOCK, :]
        block = lax.dot_general(high[:rows, :], slab, NT, preferred_element_type=F32)
        block += lax.dot_general(low[:rows, :], slab, NT, preferred_element_type=F32)
        for c in range(q, q + BLOCK, LANES):
            column = block[:, c - q:c - q + LANES]
            base, side = (half, 1) if c >= half else (0, 0)
            k = (c - base) // LANES
            at = side * plane + k * (k + 1) // 2 * LANES
            packed[at:at + (k + 1) * LANES, :] = column[base:c + LANES, :]
            if side:
                for s in range(2):
                    at = s * plane + square + k * quarter
                    packed[at:at + quarter, :] = column[s * quarter:(s + 1) * quarter, :]
    size = plane // 2

    def part(side, which):
        return packed[pl.ds(pl.multiple_of((2 * side + which) * size, 16), size), :]

    keep[...] = part(parity, core)
    away[...] = part(1 - parity, core)
    given = [part(1 - parity, 1 - core), part(parity, 1 - core)]
    piece = size // 4
    for send, x in zip(sends, given):
        for t in range(4):
            encode(x[t * piece:(t + 1) * piece, :], send, t * (piece + PAD))


def last_kernel(plan, names, step, me_ref, own_t, levels, weights, total_in, own_s, near, *rest):
    refs = dict(zip(names, rest))
    total, residual, keep, send, sem, other, amp, high, low, packed = rest[len(names):]
    me = me_ref[0]
    parity, core, _ = place_of(me)
    aux, wide = total.shape
    virt = wide // 2
    weight = weights[step:step + 1, :] - fetch(plan, step, me, refs, other)
    add_pair(own_t, other, amp, total, levels[...].T, levels[step:step + 1, :], weight, False, (high, low), near)
    copies = begin([(total.at[:, pl.ds(j * virt, virt)], residual.at[j]) for j in range(2)], sem)
    half, quarter = aux // 2, aux // 4

    def both(first, n, q):
        rows, columns = pl.ds(pl.multiple_of(first, 16), n), pl.ds(pl.multiple_of(q, 16), BLOCK)
        pairs = ((high, own_s), (low, own_s), (own_s, high), (own_s, low))
        return sum(
            lax.dot_general(a[rows, :], b[columns, :], NT, preferred_element_type=F32) for a, b in pairs
        )

    at = 0
    for q in range(0, half, BLOCK):
        block = both(parity * half, q + BLOCK, parity * half + q)
        for c in range(0, BLOCK, LANES):
            upper = q + c + LANES
            packed[at:at + upper, :] = block[:upper, c:c + LANES]
            at += upper
    for q in range(half, aux, BLOCK):
        block = both(parity * quarter, quarter, q)
        for c in range(0, BLOCK, LANES):
            packed[at:at + quarter, :] = block[:, c:c + LANES]
            at += quarter
    size = keep.shape[0]
    keep[...] = packed[pl.ds(pl.multiple_of(core * size, 16), size), :]
    send[...] = packed[pl.ds(pl.multiple_of((1 - core) * size, 16), size), :]
    finish(copies)


def encode(x, out, row):
    rows = x.shape[0]
    groups = x.reshape(rows // GROUP, GROUP, LANES)
    largest = jnp.max(jnp.abs(groups), axis=1)
    power = jnp.floor(jnp.log2(jnp.maximum(largest, 1e-30))) + 1.0
    unit = jnp.exp2(BITS - power)
    for g in range(rows // GROUP):
        whole = jnp.round(groups[g] * unit[g:g + 1, :]).astype(I32)
        out[pl.ds(row + g * GROUP, GROUP), :] = whole.astype(I16)
    pad = jnp.zeros((PAD - rows // GROUP, LANES), F32)
    out[pl.ds(row + rows, PAD), :] = jnp.concatenate([power, pad]).astype(I32).astype(I16)


def decode(coded):
    rows = coded.shape[0] - PAD
    wide = coded.astype(I32).astype(F32)
    unit = jnp.exp2(wide[rows:] - BITS)
    return jnp.concatenate(
        [wide[g * GROUP:(g + 1) * GROUP] * unit[g:g + 1, :] for g in range(rows // GROUP)]
    )


def chip_kernel(keep_in, away, got_away, got_keep, keep, send):
    piece = keep.shape[0] // 4
    for t in range(4):
        at, coded = pl.ds(t * piece, piece), pl.ds(t * (piece + PAD), piece + PAD)
        encode(away[at, :] + decode(got_away[coded, :]), send, t * (piece + PAD))
        keep[at, :] = keep_in[at, :] + decode(got_keep[coded, :])


def column_kernel(me_ref, mine, theirs, near, across, keep, *sends):
    _, _, z = place_of(me_ref[0])
    piece = keep.shape[0]
    for t in range(4):
        at = pl.ds(pl.multiple_of((z ^ t) * piece, 16), piece)
        coded = across[pl.ds(pl.multiple_of((z ^ t) * (piece + PAD), 16), piece + PAD), :]
        value = (mine[at, :] + theirs[at, :]) + (near[at, :] + decode(coded))
        if t:
            encode(value, sends[t - 1], 0)
        else:
            keep[...] = value


def sum_kernel(mine, a, b, c, out):
    out[...] = mine[...] + decode(a[...]) + decode(b[...]) + decode(c[...])


def code_kernel(scale, x, out):
    encode(x[...] * scale, out, 0)


def sum_code_kernel(scale, mine, a, b, c, out):
    encode((mine[...] + decode(a[...]) + decode(b[...]) + decode(c[...])) * scale, out, 0)


def spread_kernel(me_ref, a, b, sib_a, sib_b, out, sem, packed, square):
    parity, core, z = place_of(me_ref[0])
    rows = a.shape[1] - PAD
    aux = out.shape[1]
    half, quarter = aux // 2, aux // 4
    plane = packed.shape[0] // 2
    sources = ((a, core, parity), (b, core, 1 - parity), (sib_a, 1 - core, parity), (sib_b, 1 - core, 1 - parity))
    for src, which, side in sources:
        for t in range(4):
            row = ((side * 2 + which) * 4 + (z ^ t)) * rows
            packed[pl.ds(pl.multiple_of(row, 16), rows), :] = decode(src[t])
    for side in range(2):
        at = side * plane + plane - half // LANES * quarter
        for c in range(half, aux, LANES):
            first = side * quarter
            square[first:first + quarter, c:c + LANES] = packed[at:at + quarter, :]
            for r in range(0, quarter, LANES):
                square[c:c + LANES, first + r:first + r + LANES] = packed[at + r:at + r + LANES, :].T
            at += quarter
    copies = []
    for side in range(2):
        at = side * plane + plane - half // LANES * quarter
        base = side * half
        for c in range(half - LANES, -1, -LANES):
            at -= c + LANES
            columns = slice(base + c, base + c + LANES)
            square[base:base + c + LANES, columns] = packed[at:at + c + LANES, :]
            for r in range(0, c, LANES):
                square[columns, base + r:base + r + LANES] = packed[at + r:at + r + LANES, :].T
            done = pl.ds(base + c, LANES)
            copies += begin([(square.at[done], out.at[done])], sem, len(copies))
    finish(copies)


def shards(slabs, pair_blocks, occ_energy, virt_energy, domain_map):
    blocks = lax.axis_size("dom")
    me = lax.axis_index("dom").astype(I32)[None]
    own = slabs[0]
    orbitals, aux, virt = own.shape
    wide = orbitals * virt
    upper = aux * (aux + LANES) // 2 // LANES
    piece = upper // 16

    hbm = pl.BlockSpec(memory_space=pl.ANY)
    vmem = pl.BlockSpec(memory_space=pltpu.VMEM)
    smem = pl.BlockSpec(memory_space=pltpu.SMEM)
    slab_s = pltpu.VMEM((aux, wide), BF16)
    amp_s = pltpu.VMEM((wide, wide), BF16)
    total_t = jax.ShapeDtypeStruct((aux, wide), F32)

    def kernel(body, name, ins, outs, out_specs, scratch=(), limit=SMALL_LIMIT, aliases={}, flops=1):
        return pl.pallas_call(
            body,
            out_shape=outs,
            in_specs=ins,
            out_specs=out_specs,
            scratch_shapes=scratch,
            compiler_params=pltpu.CompilerParams(vmem_limit_bytes=limit),
            cost_estimate=pl.CostEstimate(flops=flops, bytes_accessed=1, transcendentals=0),
            input_output_aliases=aliases,
            name=name,
        )

    def dma(n):
        return pltpu.SemaphoreType.DMA((n,))

    def coded(n):
        return jax.ShapeDtypeStruct((n, LANES), I16)

    def plain(n):
        return jax.ShapeDtypeStruct((n, LANES), F32)

    cuts = [[at * aux // PER + (PAD if at and at < PER and not j else 0) for at in range(PER + 1)] for j in range(orbitals)]
    places = [(j, a, b - a) for j in range(orbitals) for a, b in zip(cuts[j], cuts[j][1:])]
    count = len(places)
    part = own[0, :places[0][2]]
    y = [swapped(part, 2)]
    sib_pairs = swapped(pair_blocks, 1)
    gives_y = ((me[0] >> 1) ^ me[0]) & 1 == 0
    later, part, gives_y = lax.optimization_barrier((own, part, gives_y))
    sib = swapped(later, 1)
    parts = [None, *kernel(
        functools.partial(split_kernel, places[1:]), "split", [smem, smem, hbm],
        [jax.ShapeDtypeStruct((n + (0 if i else PAD), virt), BF16) for i, (_, _, n) in enumerate(places[1:])],
        [vmem] * (count - 1), [dma(count - 1)],
    )(me, pair_blocks, later)]

    small = jax.ShapeDtypeStruct((8, wide), F32)
    energy = virt_energy.reshape(-1, LANES)
    levels, weights = kernel(
        functools.partial(prep_kernel, blocks), "prep", [smem] * 3 + [hbm] * 3, (small, small), (vmem, vmem),
        [dma(3), pltpu.VMEM((orbitals, blocks), F32), pltpu.VMEM(energy.shape, F32), pltpu.VMEM(domain_map.shape, I32)],
    )(me, pair_blocks, sib_pairs, occ_energy.T, energy, domain_map)
    sib, near_own = lax.optimization_barrier((sib, own))
    own_t, own_s, total = kernel(
        own_kernel, "own", [hbm, vmem, vmem],
        (jax.ShapeDtypeStruct((wide, aux), BF16), jax.ShapeDtypeStruct((aux, wide), BF16), total_t), (vmem,) * 3,
        [dma(2), amp_s], LARGE_LIMIT, flops=int(2e10),
    )(near_own, levels, weights)
    sib, part = lax.optimization_barrier((sib, parts[1]))
    y.append(swapped(part, 2))
    y[0], total, own_t, sib, part = lax.optimization_barrier((y[0], total, own_t, sib, parts[2]))
    y.append(swapped(part, 2))
    z = [forwarded(y[0])]
    total = kernel(
        sib_kernel, "sib", [vmem, vmem, hbm, vmem, vmem], total_t, vmem, [dma(2), slab_s, amp_s], LARGE_LIMIT, {1: 0},
        int(1e10),
    )(own_t, total, sib, levels, weights)
    y[1], total, part = lax.optimization_barrier((y[1], total, parts[3]))
    y.append(swapped(part, 2))
    z.append(forwarded(y[1]))
    for i in range(4, count):
        y[i - 2], part, _ = lax.optimization_barrier((y[i - 2], parts[i], y[i - 3]))
        y.append(swapped(part, 2))
        z.append(forwarded(y[i - 2]))
    y[-2], z[0] = lax.optimization_barrier((y[-2], z[0]))
    z.append(forwarded(y[-2]))

    y[-2], near = lax.optimization_barrier((y[-2], total))
    keep, away, *sends = kernel(
        near_metric_kernel, "near_metric", [smem, vmem, vmem], (plain(upper // 4),) * 2 + (coded(4 * (piece + PAD)),) * 2,
        (vmem,) * 4, [slab_s, slab_s, pltpu.VMEM((upper, LANES), F32)], LARGE_LIMIT, flops=int(1e10),
    )(me, near, own_s)
    got = [swapped(send, 1) for send in sends]
    y[-1], *got = lax.optimization_barrier((y[-1], *got))
    z.append(forwarded(y[-1]))
    y[-1], keep, away = lax.optimization_barrier((y[-1], keep, away))
    keep, send = kernel(
        chip_kernel, "chip", [vmem] * 4, (plain(upper // 4), coded(4 * (piece + PAD))), (vmem, vmem),
    )(keep, away, *got)
    across = swapped(send, 2)
    (y[-1], own_t, keep), z[PER:-1] = lax.optimization_barrier(((y[-1], own_t, keep), z[PER:-1]))

    def given(rows_y, rows_z):
        return swapped(jnp.where(gives_y, jnp.concatenate(rows_y), jnp.concatenate(rows_z)), 1)

    arrays = {f"y{i}": part for i, part in enumerate(y)}
    arrays |= {f"z{i}": part for i, part in enumerate(z)}
    arrays["x0"] = given(y[:PER], z[:PER])

    def half_of(which, j):
        name = "y" if which == Y else "z"
        if which != X:
            rows = [(f"{name}{i}", 0, n, to) for i, (k, to, n) in enumerate(places) if k == j]
            return rows, (f"{name}1", places[1][2])
        if j:
            cut = places[-1][1]
            rows = [("x1", 0, cut // 2, 0), ("x2", 0, cut // 2, cut // 2), ("x3", 0, aux - cut, cut)]
        else:
            cut = places[0][2] + places[1][2]
            rows = [("x0", 0, cut, 0)] + ([("x0", cut + PAD, aux - cut, cut)] if cut < aux else [])
        return rows, ("x0", places[0][2] + places[1][2])

    def pair_step(body, name, step, before=(), outs=(), out_specs=(), scratch=(), flops=1):
        plan = [half_of(*half) for half in STEPS[step]]
        names = list(dict.fromkeys(n for rows, (at, _) in plan for n in [r[0] for r in rows] + [at]))
        return kernel(
            functools.partial(body, plan, names, step), name,
            [smem] + [vmem] * (3 + len(before) + len(names)),
            (total_t, *outs), (vmem, *out_specs), scratch, LARGE_LIMIT, {4: 0} if before else {}, flops,
        )(me, own_t, levels, weights, *before, *[arrays[n] for n in names])

    (total,) = pair_step(first_far_kernel, "far2", 2, scratch=[slab_s, amp_s], flops=int(1e10))
    (total,) = pair_step(far_kernel, "far3", 3, (total,), scratch=[slab_s, amp_s], flops=1)
    total, *late = lax.optimization_barrier((total, *y[PER:-1], *z[PER:-1]))
    early = [jnp.where(gives_y, a, b) for a, b in zip(late[:PER - 1], late[PER - 1:])]
    early = jnp.concatenate(early)
    middle = early.shape[0] // 2
    arrays["x1"], arrays["x2"] = swapped(early[:middle], 1), swapped(early[middle:], 1)
    z[-1], total, arrays["x1"], arrays["x2"], across = lax.optimization_barrier(
        (z[-1], total, arrays["x1"], arrays["x2"], across)
    )
    arrays[f"z{count - 1}"] = z[-1]
    arrays["x3"] = given(y[-1:], z[-1:])
    _, residual, mine, send = pair_step(
        last_kernel, "last", 4, (total, own_s, near),
        (jax.ShapeDtypeStruct(own.shape, F32), plain(upper // 4), plain(upper // 4)), (hbm, vmem, vmem),
        [dma(2), slab_s, amp_s, slab_s, slab_s, pltpu.VMEM((upper // 2, LANES), F32)],
    )

    got = swapped(send, 1)
    keep, *sends = kernel(
        column_kernel, "column", [smem] + [vmem] * 4, (plain(piece),) + (coded(piece + PAD),) * 3, (vmem,) * 4,
    )(me, mine, got, keep, across)
    got = [swapped(send, 4 * t) for t, send in zip((1, 2, 3), sends)]
    if blocks == 16:
        mine = kernel(
            functools.partial(sum_code_kernel, 1.0 / blocks), "sum_code", [vmem] * 4, coded(piece + PAD), vmem,
        )(keep, *got)
    else:
        value = kernel(sum_kernel, "sum", [vmem] * 4, plain(piece), vmem)(keep, *got)
        bit = 16
        while bit < blocks:
            value = value + swapped(value, bit)
            bit *= 2
        mine = kernel(functools.partial(code_kernel, 1.0 / blocks), "code", [vmem], coded(piece + PAD), vmem)(value)

    column = [mine] + [swapped(mine, 4 * t) for t in (1, 2, 3)]
    across = [swapped(c, 2) for c in column]
    a, b = jnp.stack(column), jnp.stack(across)
    gradient = kernel(
        spread_kernel, "spread", [smem] + [vmem] * 4, jax.ShapeDtypeStruct((aux, aux), F32), hbm,
        [dma(aux // LANES), pltpu.VMEM((upper, LANES), F32), pltpu.VMEM((aux, aux), F32)],
    )(me, a, b, swapped(a, 1), swapped(b, 1))
    return residual[None], gradient


def solution(mesh):
    return jax.shard_map(
        shards,
        mesh=mesh,
        in_specs=(
            P(("grp", "dom"), None, None, None),
            P(("grp", "dom"), None),
            P("grp", None),
            P("grp"),
            P("grp", None),
        ),
        out_specs=(P(("grp", "dom"), None, None, None), P("grp", None)),
        check_vma=False,
    )
```

```python
import functools

import jax
import jax.numpy as jnp
from jax import lax
from jax.experimental import pallas as pl
from jax.experimental.pallas import tpu as pltpu
from jax.sharding import PartitionSpec as P

LARGE_LIMIT = 16 * 1024 * 1024
SMALL_LIMIT = 8 * 1024 * 1024
LANES = 128
BLOCK = 256
PAD = 16
PARTS = (416, 368, 432, 416, 416)
GROUP = 32
BITS = 14
NT = (((1,), (1,)), ((), ()))
TN = (((0,), (0,)), ((), ()))
F32, BF16, I16, I32 = jnp.float32, jnp.bfloat16, jnp.int16, jnp.int32


def move(x, pairs):
    return lax.ppermute(x, "dom", pairs)


def swapped(x, bits):
    return move(x, [(d, d ^ bits) for d in range(lax.axis_size("dom"))])


def forwarded(x):
    devices = range(lax.axis_size("dom"))
    route = [(d, d - 4 if d & 2 else d + 4) for d in devices]
    return move(x, [(a, b) for a, b in route if b in devices])


def begin(copies, sem, at=0):
    started = [pltpu.make_async_copy(a, b, sem.at[at + i]) for i, (a, b) in enumerate(copies)]
    for copy in started:
        copy.start()
    return started


def finish(copies):
    for copy in copies:
        copy.wait()


def place_of(me):
    return (me >> 1) & 1, me & 1, (me >> 2) & 3


def offsets_of(me):
    parity, core, _ = place_of(me)
    return 0, 1 - 2 * core, 2 - 4 * parity, 4 * parity - 2, 2 * core - 1


OWN, SIB, Y, Z, X = range(5)
STEPS = (((OWN, 0), (OWN, 1)), ((SIB, 0), (SIB, 1)), ((Y, 0), (Y, 1)), ((Z, 0), (X, 0)), ((Z, 1), (X, 1)))


def prep_kernel(blocks, me_ref, pairs, sib_pairs, occ_in, energy_in, maps_in, levels, weights, sem, occ, energy, maps):
    copies = begin([(occ_in, occ), (energy_in, energy), (maps_in, maps)], sem)
    me = me_ref[0]
    virt = maps.shape[1]
    finish(copies)
    table = energy[...]
    parts = []
    for _ in range(3):
        part = table.astype(BF16)
        parts.append(part)
        table = table - part.astype(F32)
    block_major = lax.broadcasted_iota(I32, occ.shape, 1)
    row_major = lax.broadcasted_iota(I32, (energy.shape[0], virt), 0)
    lane_major = lax.broadcasted_iota(I32, (LANES, virt), 0)
    for block, offset in enumerate(offsets_of(me)):
        other = me + offset
        who = jnp.clip(other, 0, blocks - 1)
        count = 0
        for s in range(pairs.shape[1]):
            count = count + (pairs[0, s] == other).astype(I32)
            if block in (OWN, SIB):
                count = count + ((pairs, sib_pairs)[block][0, s] == me).astype(I32)
        occupied = jnp.sum(jnp.where(block_major == who, occ[...], 0.0), axis=1, keepdims=True)
        index = maps[pl.ds(who, 1), :]
        pick = (row_major == index // LANES).astype(F32).astype(BF16)
        rows = sum(lax.dot_general(p, pick, TN, preferred_element_type=F32) for p in parts)
        chosen = jnp.sum(jnp.where(lane_major == index % LANES, rows, 0.0), axis=0, keepdims=True)
        for step, halves in enumerate(STEPS):
            for side, (which, j) in enumerate(halves):
                if which == block:
                    at = pl.ds(side * virt, virt)
                    levels[step:step + 1, at] = chosen - occupied[j:j + 1, :]
                    weights[step:step + 1, at] = jnp.full((1, virt), -count.astype(F32), F32)


def add_pair(own_t, other, amp, total, own_level, level, weight, first, halves=None, near=None):
    wide = own_t.shape[0]
    for t in range(0, wide, BLOCK):
        s = pl.ds(t, BLOCK)
        integrals = jnp.dot(own_t[s, :], other[...], preferred_element_type=F32)
        amp[s, :] = (integrals * weight / (own_level[t:t + BLOCK, 0:1] + level)).astype(BF16)
    for t in range(0, wide, BLOCK):
        s = pl.ds(t, BLOCK)
        part = lax.dot_general(other[...], amp[s, :], NT, preferred_element_type=F32)
        value = part if first else total[:, s] + part
        total[:, s] = value if near is None else value + near[:, s]
        if halves is not None:
            high = value.astype(BF16)
            halves[0][:, s] = high
            halves[1][:, s] = (value - high.astype(F32)).astype(BF16)


def split_kernel(cuts, me_ref, pairs, own, *rest):
    parts, sem = rest[:-1], rest[-1]
    copies = begin(
        [(own.at[pl.ds(a, b)], part.at[pl.ds(0, b)]) for a, b, part in zip(cuts, PARTS[1:], parts)], sem
    )
    rows, virt = parts[0].shape[0] - PAD, parts[0].shape[1]
    lane = lax.broadcasted_iota(I32, (PAD, virt), 1)
    listed = jnp.full((PAD, virt), 100, I32)
    for s in range(pairs.shape[1]):
        listed = jnp.where(lane == s, pairs[0, s] - me_ref[0], listed)
    parts[0][rows:, :] = listed.astype(F32).astype(BF16)
    finish(copies)


def own_kernel(own, levels, weights, own_t, own_s, total, sem, amp):
    aux, virt = own.shape[0] // 2, own.shape[1]
    copies = begin([(own.at[pl.ds(j * aux, aux)], own_s.at[:, pl.ds(j * virt, virt)]) for j in range(2)], sem)
    level = levels[...].T
    finish(copies)
    own_t[...] = own_s[...].T
    add_pair(own_t, own_s, amp, total, level, levels[0:1, :], weights[0:1, :], True)


def sib_kernel(own_t, total_in, sib, levels, weights, total, sem, other, amp):
    aux, virt = sib.shape[0] // 2, sib.shape[1]
    copies = begin([(sib.at[pl.ds(j * aux, aux)], other.at[:, pl.ds(j * virt, virt)]) for j in range(2)], sem)
    level = levels[...].T
    finish(copies)
    add_pair(own_t, other, amp, total, level, levels[1:2, :], weights[1:2, :], False)


def fetch(plan, step, me, refs, other, skip=0):
    counts = []
    for side, (rows, (name, at)) in enumerate(plan):
        virt = other.shape[1] // len(plan)
        for source, first, n, to in rows:
            other[to:to + n, side * virt:(side + 1) * virt] = refs[source][first:first + n, :]
        wanted = -offsets_of(me)[STEPS[step][side + skip][0]]
        hits = jnp.where(refs[name][at:at + PAD, :].astype(F32)[0:1, :] == wanted.astype(F32), 1.0, 0.0)
        counts.append(jnp.broadcast_to(jnp.sum(hits, axis=1, keepdims=True), (1, virt)))
    return jnp.concatenate(counts, axis=1) if len(counts) > 1 else counts[0]


def first_far_kernel(plan, names, step, me_ref, own_t, levels, weights, *rest):
    refs = dict(zip(names, rest))
    total, other, amp = rest[len(names):]
    weight = weights[step:step + 1, :] - fetch(plan, step, me_ref[0], refs, other)
    add_pair(own_t, other, amp, total, levels[...].T, levels[step:step + 1, :], weight, True)


def far_kernel(plan, names, step, me_ref, own_t, levels, weights, total_in, *rest):
    refs = dict(zip(names, rest))
    total, other, amp = rest[len(names):]
    weight = weights[step:step + 1, :] - fetch(plan, step, me_ref[0], refs, other)
    add_pair(own_t, other, amp, total, levels[...].T, levels[step:step + 1, :], weight, False)


def near_metric_kernel(me_ref, total, own_s, keep, away, *rest):
    *sends, high, low, packed = rest
    parity, core, _ = place_of(me_ref[0])
    high[...] = total[...].astype(BF16)
    low[...] = (total[...] - high[...].astype(F32)).astype(BF16)
    aux = total.shape[0]
    half, quarter = aux // 2, aux // 4
    plane = packed.shape[0] // 2
    square = plane - half // LANES * quarter
    for q in range(0, aux, BLOCK):
        rows = q + BLOCK
        slab = own_s[q:q + BLOCK, :]
        block = lax.dot_general(high[:rows, :], slab, NT, preferred_element_type=F32)
        block += lax.dot_general(low[:rows, :], slab, NT, preferred_element_type=F32)
        for c in range(q, q + BLOCK, LANES):
            column = block[:, c - q:c - q + LANES]
            base, side = (half, 1) if c >= half else (0, 0)
            k = (c - base) // LANES
            at = side * plane + k * (k + 1) // 2 * LANES
            packed[at:at + (k + 1) * LANES, :] = column[base:c + LANES, :]
            if side:
                for s in range(2):
                    at = s * plane + square + k * quarter
                    packed[at:at + quarter, :] = column[s * quarter:(s + 1) * quarter, :]
    size = plane // 2

    def part(side, which):
        return packed[pl.ds(pl.multiple_of((2 * side + which) * size, 16), size), :]

    keep[...] = part(parity, core)
    away[...] = part(1 - parity, core)
    given = [part(1 - parity, 1 - core), part(parity, 1 - core)]
    piece = size // 4
    for send, x in zip(sends, given):
        for t in range(4):
            encode(x[t * piece:(t + 1) * piece, :], send, t * (piece + PAD))


def half_kernel(plan, names, step, side, me_ref, own_t, levels, weights, total_in, *rest):
    refs = dict(zip(names, rest))
    total, other, amp = rest[len(names):]
    add_half(plan, refs, step, side, me_ref[0], own_t, levels, weights, total, other, amp)


def add_half(plan, refs, step, side, me, own_t, levels, weights, total, other, amp, halves=None, near=None):
    virt = other.shape[1]
    columns = slice(side * virt, (side + 1) * virt)
    count = fetch([plan[side]], step, me, refs, other, side)
    weight = weights[step:step + 1, columns] - count
    level = levels[step:step + 1, columns]
    add_pair(own_t, other, amp, total, levels[...].T, level, weight, False, halves, near)


def last_kernel(plan, names, step, me_ref, own_t, levels, weights, total_in, own_s, near, *rest):
    refs = dict(zip(names, rest))
    total, residual, keep, send, sem, other, amp, high, low, packed = rest[len(names):]
    me = me_ref[0]
    parity, core, _ = place_of(me)
    aux, wide = total.shape
    virt = wide // 2
    add_half(plan, refs, step, 1, me, own_t, levels, weights, total, other, amp, (high, low), near)
    copies = begin([(total.at[:, pl.ds(j * virt, virt)], residual.at[j]) for j in range(2)], sem)
    half, quarter = aux // 2, aux // 4

    def both(first, n, q):
        rows, columns = pl.ds(pl.multiple_of(first, 16), n), pl.ds(pl.multiple_of(q, 16), BLOCK)
        pairs = ((high, own_s), (low, own_s), (own_s, high), (own_s, low))
        return sum(
            lax.dot_general(a[rows, :], b[columns, :], NT, preferred_element_type=F32) for a, b in pairs
        )

    at = 0
    for q in range(0, half, BLOCK):
        block = both(parity * half, q + BLOCK, parity * half + q)
        for c in range(0, BLOCK, LANES):
            upper = q + c + LANES
            packed[at:at + upper, :] = block[:upper, c:c + LANES]
            at += upper
    for q in range(half, aux, BLOCK):
        block = both(parity * quarter, quarter, q)
        for c in range(0, BLOCK, LANES):
            packed[at:at + quarter, :] = block[:, c:c + LANES]
            at += quarter
    size = keep.shape[0]
    keep[...] = packed[pl.ds(pl.multiple_of(core * size, 16), size), :]
    send[...] = packed[pl.ds(pl.multiple_of((1 - core) * size, 16), size), :]
    finish(copies)


def encode(x, out, row):
    rows = x.shape[0]
    groups = x.reshape(rows // GROUP, GROUP, LANES)
    largest = jnp.max(jnp.abs(groups), axis=1)
    power = jnp.floor(jnp.log2(jnp.maximum(largest, 1e-30))) + 1.0
    unit = jnp.exp2(BITS - power)
    for g in range(rows // GROUP):
        whole = jnp.round(groups[g] * unit[g:g + 1, :]).astype(I32)
        out[pl.ds(row + g * GROUP, GROUP), :] = whole.astype(I16)
    pad = jnp.zeros((PAD - rows // GROUP, LANES), F32)
    out[pl.ds(row + rows, PAD), :] = jnp.concatenate([power, pad]).astype(I32).astype(I16)


def decode(coded):
    rows = coded.shape[0] - PAD
    wide = coded.astype(I32).astype(F32)
    unit = jnp.exp2(wide[rows:] - BITS)
    return jnp.concatenate(
        [wide[g * GROUP:(g + 1) * GROUP] * unit[g:g + 1, :] for g in range(rows // GROUP)]
    )


def chip_kernel(keep_in, away, got_away, got_keep, keep, send):
    piece = keep.shape[0] // 4
    for t in range(4):
        at, coded = pl.ds(t * piece, piece), pl.ds(t * (piece + PAD), piece + PAD)
        encode(away[at, :] + decode(got_away[coded, :]), send, t * (piece + PAD))
        keep[at, :] = keep_in[at, :] + decode(got_keep[coded, :])


def column_kernel(me_ref, mine, theirs, near, across, keep, *sends):
    _, _, z = place_of(me_ref[0])
    piece = keep.shape[0]
    for t in range(4):
        at = pl.ds(pl.multiple_of((z ^ t) * piece, 16), piece)
        coded = across[pl.ds(pl.multiple_of((z ^ t) * (piece + PAD), 16), piece + PAD), :]
        value = (mine[at, :] + theirs[at, :]) + (near[at, :] + decode(coded))
        if t:
            encode(value, sends[t - 1], 0)
        else:
            keep[...] = value


def sum_kernel(mine, a, b, c, out):
    out[...] = mine[...] + decode(a[...]) + decode(b[...]) + decode(c[...])


def code_kernel(scale, x, out):
    encode(x[...] * scale, out, 0)


def sum_code_kernel(scale, mine, a, b, c, out):
    encode((mine[...] + decode(a[...]) + decode(b[...]) + decode(c[...])) * scale, out, 0)


def unpack(src, which, side, z, packed):
    rows = src.shape[1] - PAD
    for t in range(4):
        row = ((side * 2 + which) * 4 + (z ^ t)) * rows
        packed[pl.ds(pl.multiple_of(row, 16), rows), :] = decode(src[t])


def unpack_kernel(me_ref, a, b, sib_a, packed):
    parity, core, z = place_of(me_ref[0])
    for src, which, side in ((a, core, parity), (b, core, 1 - parity), (sib_a, 1 - core, parity)):
        unpack(src, which, side, z, packed)


def spread_kernel(me_ref, packed_in, sib_b, out, packed, sem, square):
    parity, core, z = place_of(me_ref[0])
    aux = out.shape[1]
    half, quarter = aux // 2, aux // 4
    plane = packed.shape[0] // 2
    unpack(sib_b, 1 - core, 1 - parity, z, packed)
    for side in range(2):
        at = side * plane + plane - half // LANES * quarter
        for c in range(half, aux, LANES):
            first = side * quarter
            square[first:first + quarter, c:c + LANES] = packed[at:at + quarter, :]
            for r in range(0, quarter, LANES):
                square[c:c + LANES, first + r:first + r + LANES] = packed[at + r:at + r + LANES, :].T
            at += quarter
    copies = []
    for side in range(2):
        at = side * plane + plane - half // LANES * quarter
        base = side * half
        for c in range(half - LANES, -1, -LANES):
            at -= c + LANES
            columns = slice(base + c, base + c + LANES)
            square[base:base + c + LANES, columns] = packed[at:at + c + LANES, :]
            for r in range(0, c, LANES):
                square[columns, base + r:base + r + LANES] = packed[at + r:at + r + LANES, :].T
            done = pl.ds(base + c, LANES)
            copies += begin([(square.at[done], out.at[done])], sem, len(copies))
    finish(copies)


def shards(slabs, pair_blocks, occ_energy, virt_energy, domain_map):
    blocks = lax.axis_size("dom")
    me = lax.axis_index("dom").astype(I32)[None]
    own = slabs[0]
    orbitals, aux, virt = own.shape
    wide = orbitals * virt
    upper = aux * (aux + LANES) // 2 // LANES
    piece = upper // 16

    hbm = pl.BlockSpec(memory_space=pl.ANY)
    vmem = pl.BlockSpec(memory_space=pltpu.VMEM)
    smem = pl.BlockSpec(memory_space=pltpu.SMEM)
    slab_s = pltpu.VMEM((aux, wide), BF16)
    amp_s = pltpu.VMEM((wide, wide), BF16)
    total_t = jax.ShapeDtypeStruct((aux, wide), F32)

    def kernel(body, name, ins, outs, out_specs, scratch=(), limit=SMALL_LIMIT, aliases={}, flops=1):
        return pl.pallas_call(
            body,
            out_shape=outs,
            in_specs=ins,
            out_specs=out_specs,
            scratch_shapes=scratch,
            compiler_params=pltpu.CompilerParams(vmem_limit_bytes=limit),
            cost_estimate=pl.CostEstimate(flops=flops, bytes_accessed=1, transcendentals=0),
            input_output_aliases=aliases,
            name=name,
        )

    def dma(n):
        return pltpu.SemaphoreType.DMA((n,))

    def coded(n):
        return jax.ShapeDtypeStruct((n, LANES), I16)

    def plain(n):
        return jax.ShapeDtypeStruct((n, LANES), F32)

    flat = own.reshape(orbitals * aux, virt)
    cuts = [sum(PARTS[:i]) for i in range(len(PARTS) + 1)]
    count, early = len(PARTS), len(PARTS) - 2
    part = flat[:PARTS[0]]
    y = [swapped(part, 2)]
    sib_pairs = swapped(pair_blocks, 1)
    gives_y = ((me[0] >> 1) ^ me[0]) & 1 == 0
    later, part, gives_y = lax.optimization_barrier((flat, part, gives_y))
    sib = swapped(later, 1)
    parts = [None, *kernel(
        functools.partial(split_kernel, cuts[1:-1]), "split", [smem, smem, hbm],
        [jax.ShapeDtypeStruct((n + (0 if i else PAD), virt), BF16) for i, n in enumerate(PARTS[1:])],
        [vmem] * (count - 1), [dma(count - 1)],
    )(me, pair_blocks, later)]

    small = jax.ShapeDtypeStruct((8, wide), F32)
    energy = virt_energy.reshape(-1, LANES)
    levels, weights = kernel(
        functools.partial(prep_kernel, blocks), "prep", [smem] * 3 + [hbm] * 3, (small, small), (vmem, vmem),
        [dma(3), pltpu.VMEM((orbitals, blocks), F32), pltpu.VMEM(energy.shape, F32), pltpu.VMEM(domain_map.shape, I32)],
    )(me, pair_blocks, sib_pairs, occ_energy.T, energy, domain_map)
    sib, near_own = lax.optimization_barrier((sib, flat))
    own_t, own_s, total = kernel(
        own_kernel, "own", [hbm, vmem, vmem],
        (jax.ShapeDtypeStruct((wide, aux), BF16), jax.ShapeDtypeStruct((aux, wide), BF16), total_t), (vmem,) * 3,
        [dma(2), amp_s], LARGE_LIMIT, flops=int(2e10),
    )(near_own, levels, weights)
    sib, part = lax.optimization_barrier((sib, parts[1]))
    y.append(swapped(part, 2))
    y[0], total, own_t, sib, part = lax.optimization_barrier((y[0], total, own_t, sib, parts[2]))
    y.append(swapped(part, 2))
    z = [forwarded(y[0])]
    total = kernel(
        sib_kernel, "sib", [vmem, vmem, hbm, vmem, vmem], total_t, vmem, [dma(2), slab_s, amp_s], LARGE_LIMIT, {1: 0},
        int(1e10),
    )(own_t, total, sib, levels, weights)
    y[1], total, part = lax.optimization_barrier((y[1], total, parts[3]))
    y.append(swapped(part, 2))
    z.append(forwarded(y[1]))
    for i in range(4, count):
        y[i - 2], part, _ = lax.optimization_barrier((y[i - 2], parts[i], y[i - 3]))
        y.append(swapped(part, 2))
        z.append(forwarded(y[i - 2]))
    y[-3], near = lax.optimization_barrier((y[-3], total))
    keep, away, *sends = kernel(
        near_metric_kernel, "near_metric", [smem, vmem, vmem], (plain(upper // 4),) * 2 + (coded(4 * (piece + PAD)),) * 2,
        (vmem,) * 4, [slab_s, slab_s, pltpu.VMEM((upper, LANES), F32)], LARGE_LIMIT, flops=int(1e10),
    )(me, near, own_s)
    y[-2], z[0], keep = lax.optimization_barrier((y[-2], z[0], keep))
    z.append(forwarded(y[-2]))
    got = [swapped(send, 1) for send in sends]
    y[-1], *got = lax.optimization_barrier((y[-1], *got))
    z.append(forwarded(y[-1]))
    y[-1], keep, away = lax.optimization_barrier((y[-1], keep, away))
    keep, send = kernel(
        chip_kernel, "chip", [vmem] * 4, (plain(upper // 4), coded(4 * (piece + PAD))), (vmem, vmem),
    )(keep, away, *got)
    across = swapped(send, 2)
    (y[-1], own_t, keep), z[early:-1] = lax.optimization_barrier(((y[-1], own_t, keep), z[early:-1]))

    def given(rows_y, rows_z):
        return swapped(jnp.where(gives_y, jnp.concatenate(rows_y), jnp.concatenate(rows_z)), 1)

    arrays = {f"y{i}": part for i, part in enumerate(y)}
    arrays |= {f"z{i}": part for i, part in enumerate(z)}
    arrays["x0"] = given(y[:early], z[:early])

    def half_of(which, j):
        name = "y" if which == Y else "z"
        rows = []
        for i, (a, b) in enumerate(zip(cuts, cuts[1:])):
            first, last = max(a, j * aux), min(b, (j + 1) * aux)
            if first >= last:
                continue
            to = first - j * aux
            if which != X:
                rows.append((f"{name}{i}", first - a, last - first, to))
            elif i < early:
                rows.append(("x0", first + (PAD if i > 1 else 0), last - first, to))
            elif i == early:
                n = (b - a) // 2
                rows += [("x1", 0, n, to), ("x2", 0, b - a - n, to + n)]
            else:
                rows.append(("x3", 0, b - a, to))
        return rows, ("x0", cuts[2]) if which == X else (f"{name}1", PARTS[1])

    def pair_step(body, name, step, before=(), outs=(), out_specs=(), scratch=(), flops=1, side=None):
        plan = [half_of(*half) for half in STEPS[step]]
        used = plan if side is None else [plan[side]]
        names = list(dict.fromkeys(n for rows, (at, _) in used for n in [r[0] for r in rows] + [at]))
        return kernel(
            functools.partial(body, plan, names, step), name,
            [smem] + [vmem] * (3 + len(before) + len(names)),
            (total_t, *outs), (vmem, *out_specs), scratch, LARGE_LIMIT, {4: 0} if before else {}, flops,
        )(me, own_t, levels, weights, *before, *[arrays[n] for n in names])

    (total,) = pair_step(first_far_kernel, "far2", 2, scratch=[slab_s, amp_s], flops=int(1e10))
    (total,) = pair_step(far_kernel, "far3", 3, (total,), scratch=[slab_s, amp_s], flops=1)
    total, *late = lax.optimization_barrier((total, y[-2], z[-2]))
    late = jnp.where(gives_y, *late)
    middle = late.shape[0] // 2
    arrays["x1"], arrays["x2"] = swapped(late[:middle], 1), swapped(late[middle:], 1)
    z[-1], total, arrays["x1"], arrays["x2"], across = lax.optimization_barrier(
        (z[-1], total, arrays["x1"], arrays["x2"], across)
    )
    arrays[f"z{count - 1}"] = z[-1]
    arrays["x3"] = given(y[-1:], z[-1:])
    half_s = [pltpu.VMEM((aux, virt), BF16), pltpu.VMEM((wide, virt), BF16)]
    (total,) = pair_step(
        lambda *a: half_kernel(*a[:3], 0, *a[3:]), "half", 4, (total,), scratch=half_s, flops=int(1e9), side=0
    )
    _, residual, mine, send = pair_step(
        last_kernel, "last", 4, (total, own_s, near),
        (jax.ShapeDtypeStruct(own.shape, F32), plain(upper // 4), plain(upper // 4)), (hbm, vmem, vmem),
        [dma(2), *half_s, slab_s, slab_s, pltpu.VMEM((upper // 2, LANES), F32)], side=1,
    )

    got = swapped(send, 1)
    keep, *sends = kernel(
        column_kernel, "column", [smem] + [vmem] * 4, (plain(piece),) + (coded(piece + PAD),) * 3, (vmem,) * 4,
    )(me, mine, got, keep, across)
    got = [swapped(send, 4 * t) for t, send in zip((1, 2, 3), sends)]
    if blocks == 16:
        mine = kernel(
            functools.partial(sum_code_kernel, 1.0 / blocks), "sum_code", [vmem] * 4, coded(piece + PAD), vmem,
        )(keep, *got)
    else:
        value = kernel(sum_kernel, "sum", [vmem] * 4, plain(piece), vmem)(keep, *got)
        bit = 16
        while bit < blocks:
            value = value + swapped(value, bit)
            bit *= 2
        mine = kernel(functools.partial(code_kernel, 1.0 / blocks), "code", [vmem], coded(piece + PAD), vmem)(value)

    column = [mine] + [swapped(mine, 4 * t) for t in (1, 2, 3)]
    across = [swapped(c, 2) for c in column]
    a, b = jnp.stack(column), jnp.stack(across)
    sib_a, sib_b = swapped(a, 1), swapped(b, 1)
    packed = kernel(unpack_kernel, "unpack", [smem] + [vmem] * 3, plain(upper), vmem, flops=int(1e9))(me, a, b, sib_a)
    gradient, _ = kernel(
        spread_kernel, "spread", [smem, vmem, vmem], (jax.ShapeDtypeStruct((aux, aux), F32), plain(upper)), (hbm, vmem),
        [dma(aux // LANES), pltpu.VMEM((aux, aux), F32)], aliases={1: 1},
    )(me, packed, sib_b)
    return residual[None], gradient


def solution(mesh):
    return jax.shard_map(
        shards,
        mesh=mesh,
        in_specs=(
            P(("grp", "dom"), None, None, None),
            P(("grp", "dom"), None),
            P("grp", None),
            P("grp"),
            P("grp", None),
        ),
        out_specs=(P(("grp", "dom"), None, None, None), P("grp", None)),
        check_vma=False,
    )
```

```python
import functools

import jax
import jax.numpy as jnp
from jax import lax
from jax.experimental import pallas as pl
from jax.experimental.pallas import tpu as pltpu
from jax.sharding import PartitionSpec as P

LARGE_LIMIT = 16 * 1024 * 1024
SMALL_LIMIT = 8 * 1024 * 1024
LANES = 128
BLOCK = 256
PAD = 16
PARTS = (416, 368, 432, 416, 416)
GROUP = 32
BITS = 14
NT = (((1,), (1,)), ((), ()))
TN = (((0,), (0,)), ((), ()))
F32, BF16, I16, I32 = jnp.float32, jnp.bfloat16, jnp.int16, jnp.int32


def move(x, pairs):
    return lax.ppermute(x, "dom", pairs)


def swapped(x, bits):
    return move(x, [(d, d ^ bits) for d in range(lax.axis_size("dom"))])


def forwarded(x):
    devices = range(lax.axis_size("dom"))
    route = [(d, d - 4 if d & 2 else d + 4) for d in devices]
    return move(x, [(a, b) for a, b in route if b in devices])


def begin(copies, sem, at=0):
    started = [pltpu.make_async_copy(a, b, sem.at[at + i]) for i, (a, b) in enumerate(copies)]
    for copy in started:
        copy.start()
    return started


def finish(copies):
    for copy in copies:
        copy.wait()


def place_of(me):
    return (me >> 1) & 1, me & 1, (me >> 2) & 3


def offsets_of(me):
    parity, core, _ = place_of(me)
    return 0, 1 - 2 * core, 2 - 4 * parity, 4 * parity - 2, 2 * core - 1


OWN, SIB, Y, Z, X = range(5)
STEPS = (((OWN, 0), (OWN, 1)), ((SIB, 0), (SIB, 1)), ((Y, 0), (Y, 1)), ((Z, 0), (X, 0)), ((Z, 1), (X, 1)))


def prep_kernel(blocks, me_ref, pairs, sib_pairs, occ_in, energy_in, maps_in, levels, weights, sem, occ, energy, maps):
    copies = begin([(occ_in, occ), (energy_in, energy), (maps_in, maps)], sem)
    me = me_ref[0]
    virt = maps.shape[1]
    finish(copies)
    table = energy[...]
    parts = []
    for _ in range(3):
        part = table.astype(BF16)
        parts.append(part)
        table = table - part.astype(F32)
    block_major = lax.broadcasted_iota(I32, occ.shape, 1)
    row_major = lax.broadcasted_iota(I32, (energy.shape[0], virt), 0)
    lane_major = lax.broadcasted_iota(I32, (LANES, virt), 0)
    for block, offset in enumerate(offsets_of(me)):
        other = me + offset
        who = jnp.clip(other, 0, blocks - 1)
        count = 0
        for s in range(pairs.shape[1]):
            count = count + (pairs[0, s] == other).astype(I32)
            if block in (OWN, SIB):
                count = count + ((pairs, sib_pairs)[block][0, s] == me).astype(I32)
        occupied = jnp.sum(jnp.where(block_major == who, occ[...], 0.0), axis=1, keepdims=True)
        index = maps[pl.ds(who, 1), :]
        pick = (row_major == index // LANES).astype(F32).astype(BF16)
        rows = sum(lax.dot_general(p, pick, TN, preferred_element_type=F32) for p in parts)
        chosen = jnp.sum(jnp.where(lane_major == index % LANES, rows, 0.0), axis=0, keepdims=True)
        for step, halves in enumerate(STEPS):
            for side, (which, j) in enumerate(halves):
                if which == block:
                    at = pl.ds(side * virt, virt)
                    levels[step:step + 1, at] = chosen - occupied[j:j + 1, :]
                    weights[step:step + 1, at] = jnp.full((1, virt), -count.astype(F32), F32)


def add_pair(own_t, other, amp, total, own_level, level, weight, first, halves=None, near=None):
    wide = own_t.shape[0]
    for t in range(0, wide, BLOCK):
        s = pl.ds(t, BLOCK)
        integrals = jnp.dot(own_t[s, :], other[...], preferred_element_type=F32)
        amp[s, :] = (integrals * weight / (own_level[t:t + BLOCK, 0:1] + level)).astype(BF16)
    for t in range(0, wide, BLOCK):
        s = pl.ds(t, BLOCK)
        part = lax.dot_general(other[...], amp[s, :], NT, preferred_element_type=F32)
        value = part if first else total[:, s] + part
        total[:, s] = value if near is None else value + near[:, s]
        if halves is not None:
            high = value.astype(BF16)
            halves[0][:, s] = high
            halves[1][:, s] = (value - high.astype(F32)).astype(BF16)


def split_kernel(cuts, me_ref, pairs, own, *rest):
    parts, sem = rest[:-1], rest[-1]
    copies = begin(
        [(own.at[pl.ds(a, b)], part.at[pl.ds(0, b)]) for a, b, part in zip(cuts, PARTS[1:], parts)], sem
    )
    rows, virt = parts[0].shape[0] - PAD, parts[0].shape[1]
    lane = lax.broadcasted_iota(I32, (PAD, virt), 1)
    listed = jnp.full((PAD, virt), 100, I32)
    for s in range(pairs.shape[1]):
        listed = jnp.where(lane == s, pairs[0, s] - me_ref[0], listed)
    parts[0][rows:, :] = listed.astype(F32).astype(BF16)
    finish(copies)


def own_kernel(own, levels, weights, own_t, own_s, total, sem, amp):
    aux, virt = own.shape[0] // 2, own.shape[1]
    copies = begin([(own.at[pl.ds(j * aux, aux)], own_s.at[:, pl.ds(j * virt, virt)]) for j in range(2)], sem)
    level = levels[...].T
    finish(copies)
    own_t[...] = own_s[...].T
    add_pair(own_t, own_s, amp, total, level, levels[0:1, :], weights[0:1, :], True)


def sib_kernel(own_t, total_in, sib, levels, weights, total, sem, other, amp):
    aux, virt = sib.shape[0] // 2, sib.shape[1]
    copies = begin([(sib.at[pl.ds(j * aux, aux)], other.at[:, pl.ds(j * virt, virt)]) for j in range(2)], sem)
    level = levels[...].T
    finish(copies)
    add_pair(own_t, other, amp, total, level, levels[1:2, :], weights[1:2, :], False)


def fetch(plan, step, me, refs, other, skip=0):
    counts = []
    for side, (rows, (name, at)) in enumerate(plan):
        virt = other.shape[1] // len(plan)
        for source, first, n, to in rows:
            other[to:to + n, side * virt:(side + 1) * virt] = refs[source][first:first + n, :]
        wanted = -offsets_of(me)[STEPS[step][side + skip][0]]
        hits = jnp.where(refs[name][at:at + PAD, :].astype(F32)[0:1, :] == wanted.astype(F32), 1.0, 0.0)
        counts.append(jnp.broadcast_to(jnp.sum(hits, axis=1, keepdims=True), (1, virt)))
    return jnp.concatenate(counts, axis=1) if len(counts) > 1 else counts[0]


def first_far_kernel(plan, names, step, me_ref, own_t, levels, weights, *rest):
    refs = dict(zip(names, rest))
    total, other, amp = rest[len(names):]
    weight = weights[step:step + 1, :] - fetch(plan, step, me_ref[0], refs, other)
    add_pair(own_t, other, amp, total, levels[...].T, levels[step:step + 1, :], weight, True)


def far_kernel(plan, names, step, me_ref, own_t, levels, weights, total_in, *rest):
    refs = dict(zip(names, rest))
    total, other, amp = rest[len(names):]
    weight = weights[step:step + 1, :] - fetch(plan, step, me_ref[0], refs, other)
    add_pair(own_t, other, amp, total, levels[...].T, levels[step:step + 1, :], weight, False)


def segments(plane, which):
    side = plane // 18
    return (which * side * 5, side * 5), (side * 10 + which * side * 4, side * 4)


def rows_of(packed, base, plane, which):
    return jnp.concatenate(
        [packed[pl.ds(pl.multiple_of(base + a, 16), n), :] for a, n in segments(plane, which)]
    )


def near_metric_kernel(me_ref, total, own_s, keep, away, *rest):
    *sends, high, low, packed = rest
    parity, core, _ = place_of(me_ref[0])
    high[...] = total[...].astype(BF16)
    low[...] = (total[...] - high[...].astype(F32)).astype(BF16)
    aux = total.shape[0]
    half, quarter = aux // 2, aux // 4
    plane = packed.shape[0] // 2
    square = plane - half // LANES * quarter
    for q in range(0, aux, BLOCK):
        rows = q + BLOCK
        slab = own_s[q:q + BLOCK, :]
        block = lax.dot_general(high[:rows, :], slab, NT, preferred_element_type=F32)
        block += lax.dot_general(low[:rows, :], slab, NT, preferred_element_type=F32)
        for c in range(q, q + BLOCK, LANES):
            column = block[:, c - q:c - q + LANES]
            base, side = (half, 1) if c >= half else (0, 0)
            k = (c - base) // LANES
            at = side * plane + k * (k + 1) // 2 * LANES
            packed[at:at + (k + 1) * LANES, :] = column[base:c + LANES, :]
            if side:
                for s in range(2):
                    at = s * plane + square + k * quarter
                    packed[at:at + quarter, :] = column[s * quarter:(s + 1) * quarter, :]
    size = plane // 2

    def part(side, which):
        return rows_of(packed, side * plane, plane, which)

    keep[...] = part(parity, core)
    away[...] = part(1 - parity, core)
    given = [part(1 - parity, 1 - core), part(parity, 1 - core)]
    piece = size // 4
    for send, x in zip(sends, given):
        for t in range(4):
            encode(x[t * piece:(t + 1) * piece, :], send, t * (piece + PAD))


def half_kernel(plan, names, step, side, me_ref, own_t, levels, weights, total_in, *rest):
    refs = dict(zip(names, rest))
    total, other, amp = rest[len(names):]
    add_half(plan, refs, step, side, me_ref[0], own_t, levels, weights, total, other, amp)


def add_half(plan, refs, step, side, me, own_t, levels, weights, total, other, amp, halves=None, near=None):
    virt = other.shape[1]
    columns = slice(side * virt, (side + 1) * virt)
    count = fetch([plan[side]], step, me, refs, other, side)
    weight = weights[step:step + 1, columns] - count
    level = levels[step:step + 1, columns]
    add_pair(own_t, other, amp, total, levels[...].T, level, weight, False, halves, near)


def mirrored(high, low, own_s, first, n, q):
    rows, columns = pl.ds(pl.multiple_of(first, 16), n), pl.ds(pl.multiple_of(q, 16), BLOCK)
    pairs = ((high, own_s), (low, own_s), (own_s, high), (own_s, low))
    return sum(lax.dot_general(a[rows, :], b[columns, :], NT, preferred_element_type=F32) for a, b in pairs)


def last_kernel(plan, names, step, me_ref, own_t, levels, weights, total_in, own_s, near, *rest):
    refs = dict(zip(names, rest))
    total, residual, keep, send, high, low, sem, other, amp, packed = rest[len(names):]
    me = me_ref[0]
    parity, core, _ = place_of(me)
    aux, wide = total.shape
    virt = wide // 2
    add_half(plan, refs, step, 1, me, own_t, levels, weights, total, other, amp, (high, low), near)
    copies = begin([(total.at[:, pl.ds(j * virt, virt)], residual.at[j]) for j in range(2)], sem)
    half = aux // 2

    def both(first, n, q):
        return mirrored(high, low, own_s, first, n, q)

    at = 0
    for q in range(0, half, BLOCK):
        block = both(parity * half, q + BLOCK, parity * half + q)
        for c in range(0, BLOCK, LANES):
            upper = q + c + LANES
            packed[at:at + upper, :] = block[:upper, c:c + LANES]
            at += upper
    share(packed, core, keep, send)
    finish(copies)


def share(packed, core, keep, send):
    size = keep.shape[0]
    keep[...] = packed[pl.ds(pl.multiple_of(core * size, 16), size), :]
    send[...] = packed[pl.ds(pl.multiple_of((1 - core) * size, 16), size), :]


def corner_kernel(me_ref, high, low, own_s, keep, send, packed):
    parity, core, _ = place_of(me_ref[0])
    aux = own_s.shape[0]
    half, quarter = aux // 2, aux // 4
    at = 0
    for q in range(half, aux, BLOCK):
        block = mirrored(high, low, own_s, parity * quarter, quarter, q)
        for c in range(0, BLOCK, LANES):
            packed[at:at + quarter, :] = block[:, c:c + LANES]
            at += quarter
    share(packed, core, keep, send)


def encode(x, out, row):
    rows = x.shape[0]
    groups = x.reshape(rows // GROUP, GROUP, LANES)
    largest = jnp.max(jnp.abs(groups), axis=1)
    power = jnp.floor(jnp.log2(jnp.maximum(largest, 1e-30))) + 1.0
    unit = jnp.exp2(BITS - power)
    for g in range(rows // GROUP):
        whole = jnp.round(groups[g] * unit[g:g + 1, :]).astype(I32)
        out[pl.ds(row + g * GROUP, GROUP), :] = whole.astype(I16)
    pad = jnp.zeros((PAD - rows // GROUP, LANES), F32)
    out[pl.ds(row + rows, PAD), :] = jnp.concatenate([power, pad]).astype(I32).astype(I16)


def decode(coded):
    rows = coded.shape[0] - PAD
    wide = coded.astype(I32).astype(F32)
    unit = jnp.exp2(wide[rows:] - BITS)
    return jnp.concatenate(
        [wide[g * GROUP:(g + 1) * GROUP] * unit[g:g + 1, :] for g in range(rows // GROUP)]
    )


def chip_kernel(keep_in, away, got_away, got_keep, keep, send):
    piece = keep.shape[0] // 4
    for t in range(4):
        at, coded = pl.ds(t * piece, piece), pl.ds(t * (piece + PAD), piece + PAD)
        encode(away[at, :] + decode(got_away[coded, :]), send, t * (piece + PAD))
        keep[at, :] = keep_in[at, :] + decode(got_keep[coded, :])


def column_kernel(first, me_ref, mine, theirs, near, across, keep, *sends):
    _, _, z = place_of(me_ref[0])
    piece = keep.shape[0]
    away = across.shape[0] // 4
    far = jnp.concatenate([decode(across[i * away:(i + 1) * away, :]) for i in range(4)])
    for i in range(4):
        at = slice(i * piece, (i + 1) * piece)
        inner = slice(first + i * piece, first + (i + 1) * piece)
        value = (mine[at, :] + theirs[at, :]) + (near[inner, :] + far[inner, :])

        @pl.when(z == i)
        def _():
            keep[...] = value

        for t in (1, 2, 3):
            pl.when((z ^ t) == i)(functools.partial(encode, value, sends[t - 1], 0))


def sum_of(parts):
    return jnp.concatenate([sum((decode(x[...]) for x in others), mine[...]) for mine, *others in (parts[:4], parts[4:])])


def sum_kernel(*rest):
    rest[-1][...] = sum_of(rest[:-1])


def code_kernel(scale, x, out):
    encode(x[...] * scale, out, 0)


def sum_code_kernel(scale, *rest):
    encode(sum_of(rest[:-1]) * scale, rest[-1], 0)


def unpack(src, which, side, z, packed):
    plane = packed.shape[0] // 2
    for t in range(4):
        value = decode(src[t])
        used = 0
        for first, n in ((which * (plane // 18) * 5, plane // 18 * 5), (plane // 18 * (10 + which * 4), plane // 18 * 4)):
            piece = n // 4
            row = side * plane + first + (z ^ t) * piece
            packed[pl.ds(pl.multiple_of(row, 16), piece), :] = value[used:used + piece, :]
            used += piece


def unpack_kernel(me_ref, a, b, sib_a, packed):
    parity, core, z = place_of(me_ref[0])
    for src, which, side in ((a, core, parity), (b, core, 1 - parity), (sib_a, 1 - core, parity)):
        unpack(src, which, side, z, packed)


def spread_kernel(me_ref, packed_in, sib_b, out, packed, sem, square):
    parity, core, z = place_of(me_ref[0])
    aux = out.shape[1]
    half, quarter = aux // 2, aux // 4
    plane = packed.shape[0] // 2
    unpack(sib_b, 1 - core, 1 - parity, z, packed)
    for side in range(2):
        at = side * plane + plane - half // LANES * quarter
        for c in range(half, aux, LANES):
            first = side * quarter
            square[first:first + quarter, c:c + LANES] = packed[at:at + quarter, :]
            for r in range(0, quarter, LANES):
                square[c:c + LANES, first + r:first + r + LANES] = packed[at + r:at + r + LANES, :].T
            at += quarter
    copies = []
    for side in range(2):
        at = side * plane + plane - half // LANES * quarter
        base = side * half
        for c in range(half - LANES, -1, -LANES):
            at -= c + LANES
            columns = slice(base + c, base + c + LANES)
            square[base:base + c + LANES, columns] = packed[at:at + c + LANES, :]
            for r in range(0, c, LANES):
                square[columns, base + r:base + r + LANES] = packed[at + r:at + r + LANES, :].T
            done = pl.ds(base + c, LANES)
            copies += begin([(square.at[done], out.at[done])], sem, len(copies))
    finish(copies)


def shards(slabs, pair_blocks, occ_energy, virt_energy, domain_map):
    blocks = lax.axis_size("dom")
    me = lax.axis_index("dom").astype(I32)[None]
    own = slabs[0]
    orbitals, aux, virt = own.shape
    wide = orbitals * virt
    upper = aux * (aux + LANES) // 2 // LANES
    piece = upper // 16

    hbm = pl.BlockSpec(memory_space=pl.ANY)
    vmem = pl.BlockSpec(memory_space=pltpu.VMEM)
    smem = pl.BlockSpec(memory_space=pltpu.SMEM)
    slab_s = pltpu.VMEM((aux, wide), BF16)
    amp_s = pltpu.VMEM((wide, wide), BF16)
    total_t = jax.ShapeDtypeStruct((aux, wide), F32)

    def kernel(body, name, ins, outs, out_specs, scratch=(), limit=SMALL_LIMIT, aliases={}, flops=1):
        return pl.pallas_call(
            body,
            out_shape=outs,
            in_specs=ins,
            out_specs=out_specs,
            scratch_shapes=scratch,
            compiler_params=pltpu.CompilerParams(vmem_limit_bytes=limit),
            cost_estimate=pl.CostEstimate(flops=flops, bytes_accessed=1, transcendentals=0),
            input_output_aliases=aliases,
            name=name,
        )

    def dma(n):
        return pltpu.SemaphoreType.DMA((n,))

    def coded(n):
        return jax.ShapeDtypeStruct((n, LANES), I16)

    def plain(n):
        return jax.ShapeDtypeStruct((n, LANES), F32)

    flat = own.reshape(orbitals * aux, virt)
    cuts = [sum(PARTS[:i]) for i in range(len(PARTS) + 1)]
    count, early = len(PARTS), len(PARTS) - 2
    part = flat[:PARTS[0]]
    y = [swapped(part, 2)]
    sib_pairs = swapped(pair_blocks, 1)
    gives_y = ((me[0] >> 1) ^ me[0]) & 1 == 0
    later, part, gives_y = lax.optimization_barrier((flat, part, gives_y))
    sib = swapped(later, 1)
    parts = [None, *kernel(
        functools.partial(split_kernel, cuts[1:-1]), "split", [smem, smem, hbm],
        [jax.ShapeDtypeStruct((n + (0 if i else PAD), virt), BF16) for i, n in enumerate(PARTS[1:])],
        [vmem] * (count - 1), [dma(count - 1)],
    )(me, pair_blocks, later)]

    small = jax.ShapeDtypeStruct((8, wide), F32)
    energy = virt_energy.reshape(-1, LANES)
    levels, weights = kernel(
        functools.partial(prep_kernel, blocks), "prep", [smem] * 3 + [hbm] * 3, (small, small), (vmem, vmem),
        [dma(3), pltpu.VMEM((orbitals, blocks), F32), pltpu.VMEM(energy.shape, F32), pltpu.VMEM(domain_map.shape, I32)],
    )(me, pair_blocks, sib_pairs, occ_energy.T, energy, domain_map)
    sib, near_own = lax.optimization_barrier((sib, flat))
    own_t, own_s, total = kernel(
        own_kernel, "own", [hbm, vmem, vmem],
        (jax.ShapeDtypeStruct((wide, aux), BF16), jax.ShapeDtypeStruct((aux, wide), BF16), total_t), (vmem,) * 3,
        [dma(2), amp_s], LARGE_LIMIT, flops=int(2e10),
    )(near_own, levels, weights)
    sib, part = lax.optimization_barrier((sib, parts[1]))
    y.append(swapped(part, 2))
    y[0], total, own_t, sib, part = lax.optimization_barrier((y[0], total, own_t, sib, parts[2]))
    y.append(swapped(part, 2))
    z = [forwarded(y[0])]
    total = kernel(
        sib_kernel, "sib", [vmem, vmem, hbm, vmem, vmem], total_t, vmem, [dma(2), slab_s, amp_s], LARGE_LIMIT, {1: 0},
        int(1e10),
    )(own_t, total, sib, levels, weights)
    y[1], total, part = lax.optimization_barrier((y[1], total, parts[3]))
    y.append(swapped(part, 2))
    z.append(forwarded(y[1]))
    for i in range(4, count):
        y[i - 2], part, _ = lax.optimization_barrier((y[i - 2], parts[i], y[i - 3]))
        y.append(swapped(part, 2))
        z.append(forwarded(y[i - 2]))
    y[-3], near = lax.optimization_barrier((y[-3], total))
    keep, away, *sends = kernel(
        near_metric_kernel, "near_metric", [smem, vmem, vmem], (plain(upper // 4),) * 2 + (coded(4 * (piece + PAD)),) * 2,
        (vmem,) * 4, [slab_s, slab_s, pltpu.VMEM((upper, LANES), F32)], LARGE_LIMIT, flops=int(1e10),
    )(me, near, own_s)
    y[-2], z[0], keep = lax.optimization_barrier((y[-2], z[0], keep))
    z.append(forwarded(y[-2]))
    got = [swapped(send, 1) for send in sends]
    y[-1], *got = lax.optimization_barrier((y[-1], *got))
    z.append(forwarded(y[-1]))
    y[-1], keep, away = lax.optimization_barrier((y[-1], keep, away))
    keep, send = kernel(
        chip_kernel, "chip", [vmem] * 4, (plain(upper // 4), coded(4 * (piece + PAD))), (vmem, vmem),
    )(keep, away, *got)
    across = swapped(send, 2)
    (y[-1], own_t, keep), z[early:-1] = lax.optimization_barrier(((y[-1], own_t, keep), z[early:-1]))

    def given(rows_y, rows_z):
        return swapped(jnp.where(gives_y, jnp.concatenate(rows_y), jnp.concatenate(rows_z)), 1)

    arrays = {f"y{i}": part for i, part in enumerate(y)}
    arrays |= {f"z{i}": part for i, part in enumerate(z)}
    arrays["x0"] = given(y[:early], z[:early])

    def half_of(which, j):
        name = "y" if which == Y else "z"
        rows = []
        for i, (a, b) in enumerate(zip(cuts, cuts[1:])):
            first, last = max(a, j * aux), min(b, (j + 1) * aux)
            if first >= last:
                continue
            to = first - j * aux
            if which != X:
                rows.append((f"{name}{i}", first - a, last - first, to))
            elif i < early:
                rows.append(("x0", first + (PAD if i > 1 else 0), last - first, to))
            elif i == early:
                n = (b - a) // 2
                rows += [("x1", 0, n, to), ("x2", 0, b - a - n, to + n)]
            else:
                rows.append(("x3", 0, b - a, to))
        return rows, ("x0", cuts[2]) if which == X else (f"{name}1", PARTS[1])

    def pair_step(body, name, step, before=(), outs=(), out_specs=(), scratch=(), flops=1, side=None):
        plan = [half_of(*half) for half in STEPS[step]]
        used = plan if side is None else [plan[side]]
        names = list(dict.fromkeys(n for rows, (at, _) in used for n in [r[0] for r in rows] + [at]))
        return kernel(
            functools.partial(body, plan, names, step), name,
            [smem] + [vmem] * (3 + len(before) + len(names)),
            (total_t, *outs), (vmem, *out_specs), scratch, LARGE_LIMIT, {4: 0} if before else {}, flops,
        )(me, own_t, levels, weights, *before, *[arrays[n] for n in names])

    (total,) = pair_step(first_far_kernel, "far2", 2, scratch=[slab_s, amp_s], flops=int(1e10))
    (total,) = pair_step(far_kernel, "far3", 3, (total,), scratch=[slab_s, amp_s], flops=1)
    total, *late = lax.optimization_barrier((total, y[-2], z[-2]))
    late = jnp.where(gives_y, *late)
    middle = late.shape[0] // 2
    arrays["x1"], arrays["x2"] = swapped(late[:middle], 1), swapped(late[middle:], 1)
    z[-1], total, arrays["x1"], arrays["x2"], across = lax.optimization_barrier(
        (z[-1], total, arrays["x1"], arrays["x2"], across)
    )
    arrays[f"z{count - 1}"] = z[-1]
    arrays["x3"] = given(y[-1:], z[-1:])
    half_s = [pltpu.VMEM((aux, virt), BF16), pltpu.VMEM((wide, virt), BF16)]
    (total,) = pair_step(
        lambda *a: half_kernel(*a[:3], 0, *a[3:]), "half", 4, (total,), scratch=half_s, flops=int(1e9), side=0
    )
    plane = upper // 2
    (_, square), (_, corner) = segments(plane, 0)
    slab_t = jax.ShapeDtypeStruct((aux, wide), BF16)
    _, residual, mine, send, high, low = pair_step(
        last_kernel, "last", 4, (total, own_s, near),
        (jax.ShapeDtypeStruct(own.shape, F32), plain(square), plain(square), slab_t, slab_t), (hbm,) + (vmem,) * 4,
        [dma(2), *half_s, pltpu.VMEM((2 * square, LANES), F32)], side=1,
    )

    def column(first, size, mine, got):
        n = size // 4
        return kernel(
            functools.partial(column_kernel, first), "column", [smem] + [vmem] * 4, (plain(n),) + (coded(n + PAD),) * 3,
            (vmem,) * 4,
        )(me, mine, got, keep, across)

    got = swapped(send, 1)
    mine_b, send_b = kernel(
        corner_kernel, "corner", [smem] + [vmem] * 3, (plain(corner), plain(corner)), (vmem, vmem),
        [pltpu.VMEM((2 * corner, LANES), F32)], LARGE_LIMIT, flops=int(2e9),
    )(me, high, low, own_s)
    got, send_b = lax.optimization_barrier((got, send_b))
    got_b = swapped(send_b, 1)
    keep_a, *sends_a = column(0, square, mine, got)
    summed = [keep_a] + [swapped(sends_a[t - 1], 4 * t) for t in (3, 2, 1)]
    keep_b, *sends_b = column(square, corner, mine_b, got_b)
    summed += [keep_b] + [swapped(sends_b[t - 1], 4 * t) for t in (3, 2, 1)]
    if blocks == 16:
        mine = kernel(
            functools.partial(sum_code_kernel, 1.0 / blocks), "sum_code", [vmem] * 8, coded(piece + PAD), vmem,
        )(*summed)
    else:
        value = kernel(sum_kernel, "sum", [vmem] * 8, plain(piece), vmem)(*summed)
        bit = 16
        while bit < blocks:
            value = value + swapped(value, bit)
            bit *= 2
        mine = kernel(functools.partial(code_kernel, 1.0 / blocks), "code", [vmem], coded(piece + PAD), vmem)(value)

    column = [mine] + [swapped(mine, 4 * t) for t in (1, 2, 3)]
    across = [swapped(c, 2) for c in column]
    a, b = jnp.stack(column), jnp.stack(across)
    sib_a, sib_b = swapped(a, 1), swapped(b, 1)
    packed = kernel(unpack_kernel, "unpack", [smem] + [vmem] * 3, plain(upper), vmem, flops=int(1e9))(me, a, b, sib_a)
    gradient, _ = kernel(
        spread_kernel, "spread", [smem, vmem, vmem], (jax.ShapeDtypeStruct((aux, aux), F32), plain(upper)), (hbm, vmem),
        [dma(aux // LANES), pltpu.VMEM((aux, aux), F32)], aliases={1: 1},
    )(me, packed, sib_b)
    return residual[None], gradient


def solution(mesh):
    return jax.shard_map(
        shards,
        mesh=mesh,
        in_specs=(
            P(("grp", "dom"), None, None, None),
            P(("grp", "dom"), None),
            P("grp", None),
            P("grp"),
            P("grp", None),
        ),
        out_specs=(P(("grp", "dom"), None, None, None), P("grp", None)),
        check_vma=False,
    )
```

```python
import functools

import jax
import jax.numpy as jnp
from jax import lax
from jax.experimental import pallas as pl
from jax.experimental.pallas import tpu as pltpu
from jax.sharding import PartitionSpec as P

LARGE_LIMIT = 16 * 1024 * 1024
SMALL_LIMIT = 8 * 1024 * 1024
LANES = 128
BLOCK = 256
PAD = 16
PARTS = (416, 368, 432, 416, 416)
GROUP = 32
BITS = 14
NT = (((1,), (1,)), ((), ()))
TN = (((0,), (0,)), ((), ()))
F32, BF16, I16, I32 = jnp.float32, jnp.bfloat16, jnp.int16, jnp.int32


def move(x, pairs):
    return lax.ppermute(x, "dom", pairs)


def swapped(x, bits):
    return move(x, [(d, d ^ bits) for d in range(lax.axis_size("dom"))])


def forwarded(x):
    devices = range(lax.axis_size("dom"))
    route = [(d, d - 4 if d & 2 else d + 4) for d in devices]
    return move(x, [(a, b) for a, b in route if b in devices])


def begin(copies, sem, at=0):
    started = [pltpu.make_async_copy(a, b, sem.at[at + i]) for i, (a, b) in enumerate(copies)]
    for copy in started:
        copy.start()
    return started


def finish(copies):
    for copy in copies:
        copy.wait()


def place_of(me):
    return (me >> 1) & 1, me & 1, (me >> 2) & 3


def offsets_of(me):
    parity, core, _ = place_of(me)
    return 0, 1 - 2 * core, 2 - 4 * parity, 4 * parity - 2, 2 * core - 1


OWN, SIB, Y, Z, X = range(5)
STEPS = (((OWN, 0), (OWN, 1)), ((SIB, 0), (SIB, 1)), ((Y, 0), (Y, 1)), ((Z, 0), (X, 0)), ((Z, 1), (X, 1)))


def prep_kernel(blocks, me_ref, pairs, sib_pairs, occ_in, energy_in, maps_in, levels, weights, sem, occ, energy, maps):
    copies = begin([(occ_in, occ), (energy_in, energy), (maps_in, maps)], sem)
    me = me_ref[0]
    virt = maps.shape[1]
    finish(copies)
    table = energy[...]
    parts = []
    for _ in range(3):
        part = table.astype(BF16)
        parts.append(part)
        table = table - part.astype(F32)
    block_major = lax.broadcasted_iota(I32, occ.shape, 1)
    row_major = lax.broadcasted_iota(I32, (energy.shape[0], virt), 0)
    lane_major = lax.broadcasted_iota(I32, (LANES, virt), 0)
    for block, offset in enumerate(offsets_of(me)):
        other = me + offset
        who = jnp.clip(other, 0, blocks - 1)
        count = 0
        for s in range(pairs.shape[1]):
            count = count + (pairs[0, s] == other).astype(I32)
            if block in (OWN, SIB):
                count = count + ((pairs, sib_pairs)[block][0, s] == me).astype(I32)
        occupied = jnp.sum(jnp.where(block_major == who, occ[...], 0.0), axis=1, keepdims=True)
        index = maps[pl.ds(who, 1), :]
        pick = (row_major == index // LANES).astype(F32).astype(BF16)
        rows = sum(lax.dot_general(p, pick, TN, preferred_element_type=F32) for p in parts)
        chosen = jnp.sum(jnp.where(lane_major == index % LANES, rows, 0.0), axis=0, keepdims=True)
        for step, halves in enumerate(STEPS):
            for side, (which, j) in enumerate(halves):
                if which == block:
                    at = pl.ds(side * virt, virt)
                    levels[step:step + 1, at] = chosen - occupied[j:j + 1, :]
                    weights[step:step + 1, at] = jnp.full((1, virt), -count.astype(F32), F32)


def add_pair(own_t, other, amp, total, own_level, level, weight, first, halves=None, near=None):
    wide = own_t.shape[0]
    for t in range(0, wide, BLOCK):
        s = pl.ds(t, BLOCK)
        integrals = jnp.dot(own_t[s, :], other[...], preferred_element_type=F32)
        amp[s, :] = (integrals * weight / (own_level[t:t + BLOCK, 0:1] + level)).astype(BF16)
    for t in range(0, wide, BLOCK):
        s = pl.ds(t, BLOCK)
        part = lax.dot_general(other[...], amp[s, :], NT, preferred_element_type=F32)
        value = part if first else total[:, s] + part
        total[:, s] = value if near is None else value + near[:, s]
        if halves is not None:
            high = value.astype(BF16)
            halves[0][:, s] = high
            halves[1][:, s] = (value - high.astype(F32)).astype(BF16)


def split_kernel(cuts, me_ref, pairs, own, *rest):
    parts, sem = rest[:-1], rest[-1]
    copies = begin(
        [(own.at[pl.ds(a, b)], part.at[pl.ds(0, b)]) for a, b, part in zip(cuts, PARTS[1:], parts)], sem
    )
    rows, virt = parts[0].shape[0] - PAD, parts[0].shape[1]
    lane = lax.broadcasted_iota(I32, (PAD, virt), 1)
    listed = jnp.full((PAD, virt), 100, I32)
    for s in range(pairs.shape[1]):
        listed = jnp.where(lane == s, pairs[0, s] - me_ref[0], listed)
    parts[0][rows:, :] = listed.astype(F32).astype(BF16)
    finish(copies)


def own_kernel(own, levels, weights, own_t, own_s, total, sem, amp):
    aux, virt = own.shape[0] // 2, own.shape[1]
    copies = begin([(own.at[pl.ds(j * aux, aux)], own_s.at[:, pl.ds(j * virt, virt)]) for j in range(2)], sem)
    level = levels[...].T
    finish(copies)
    own_t[...] = own_s[...].T
    add_pair(own_t, own_s, amp, total, level, levels[0:1, :], weights[0:1, :], True)


def sib_kernel(own_t, total_in, sib, levels, weights, total, sem, other, amp):
    aux, virt = sib.shape[0] // 2, sib.shape[1]
    copies = begin([(sib.at[pl.ds(j * aux, aux)], other.at[:, pl.ds(j * virt, virt)]) for j in range(2)], sem)
    level = levels[...].T
    finish(copies)
    add_pair(own_t, other, amp, total, level, levels[1:2, :], weights[1:2, :], False)


def fetch(plan, step, me, refs, other, skip=0):
    counts = []
    for side, (rows, (name, at)) in enumerate(plan):
        virt = other.shape[1] // len(plan)
        for source, first, n, to in rows:
            other[to:to + n, side * virt:(side + 1) * virt] = refs[source][first:first + n, :]
        wanted = -offsets_of(me)[STEPS[step][side + skip][0]]
        hits = jnp.where(refs[name][at:at + PAD, :].astype(F32)[0:1, :] == wanted.astype(F32), 1.0, 0.0)
        counts.append(jnp.broadcast_to(jnp.sum(hits, axis=1, keepdims=True), (1, virt)))
    return jnp.concatenate(counts, axis=1) if len(counts) > 1 else counts[0]


def first_far_kernel(plan, names, step, me_ref, own_t, levels, weights, *rest):
    refs = dict(zip(names, rest))
    total, other, amp = rest[len(names):]
    weight = weights[step:step + 1, :] - fetch(plan, step, me_ref[0], refs, other)
    add_pair(own_t, other, amp, total, levels[...].T, levels[step:step + 1, :], weight, True)


def far_kernel(plan, names, step, me_ref, own_t, levels, weights, total_in, *rest):
    refs = dict(zip(names, rest))
    total, other, amp = rest[len(names):]
    weight = weights[step:step + 1, :] - fetch(plan, step, me_ref[0], refs, other)
    add_pair(own_t, other, amp, total, levels[...].T, levels[step:step + 1, :], weight, False)


def segments(plane, which):
    side = plane // 18
    return (which * side * 5, side * 5), (side * 10 + which * side * 4, side * 4)


def rows_of(packed, base, plane, which):
    return jnp.concatenate(
        [packed[pl.ds(pl.multiple_of(base + a, 16), n), :] for a, n in segments(plane, which)]
    )


def near_metric_kernel(me_ref, total, own_s, keep, away, *rest):
    *sends, high, low, packed = rest
    parity, core, _ = place_of(me_ref[0])
    high[...] = total[...].astype(BF16)
    low[...] = (total[...] - high[...].astype(F32)).astype(BF16)
    aux = total.shape[0]
    half, quarter = aux // 2, aux // 4
    plane = packed.shape[0] // 2
    square = plane - half // LANES * quarter
    for q in range(0, aux, BLOCK):
        rows = q + BLOCK
        slab = own_s[q:q + BLOCK, :]
        block = lax.dot_general(high[:rows, :], slab, NT, preferred_element_type=F32)
        block += lax.dot_general(low[:rows, :], slab, NT, preferred_element_type=F32)
        for c in range(q, q + BLOCK, LANES):
            column = block[:, c - q:c - q + LANES]
            base, side = (half, 1) if c >= half else (0, 0)
            k = (c - base) // LANES
            at = side * plane + k * (k + 1) // 2 * LANES
            packed[at:at + (k + 1) * LANES, :] = column[base:c + LANES, :]
            if side:
                for s in range(2):
                    at = s * plane + square + k * quarter
                    packed[at:at + quarter, :] = column[s * quarter:(s + 1) * quarter, :]
    size = plane // 2

    def part(side, which):
        return rows_of(packed, side * plane, plane, which)

    keep[...] = part(parity, core)
    away[...] = part(1 - parity, core)
    given = [part(1 - parity, 1 - core), part(parity, 1 - core)]
    piece = size // 4
    for send, x in zip(sends, given):
        for t in range(4):
            encode(x[t * piece:(t + 1) * piece, :], send, t * (piece + PAD))


def half_kernel(plan, names, step, side, me_ref, own_t, levels, weights, total_in, *rest):
    refs = dict(zip(names, rest))
    total, other, amp = rest[len(names):]
    add_half(plan, refs, step, side, me_ref[0], own_t, levels, weights, total, other, amp)


def add_half(plan, refs, step, side, me, own_t, levels, weights, total, other, amp, halves=None, near=None):
    virt = other.shape[1]
    columns = slice(side * virt, (side + 1) * virt)
    count = fetch([plan[side]], step, me, refs, other, side)
    weight = weights[step:step + 1, columns] - count
    level = levels[step:step + 1, columns]
    add_pair(own_t, other, amp, total, levels[...].T, level, weight, False, halves, near)


def mirrored(high, low, own_s, first, n, q):
    rows, columns = pl.ds(pl.multiple_of(first, 16), n), pl.ds(pl.multiple_of(q, 16), BLOCK)
    pairs = ((high, own_s), (low, own_s), (own_s, high), (own_s, low))
    return sum(lax.dot_general(a[rows, :], b[columns, :], NT, preferred_element_type=F32) for a, b in pairs)


def last_kernel(plan, names, step, me_ref, own_t, levels, weights, total_in, own_s, near, *rest):
    refs = dict(zip(names, rest))
    total, residual, keep, send, high, low, sem, other, amp, packed = rest[len(names):]
    me = me_ref[0]
    parity, core, _ = place_of(me)
    aux, wide = total.shape
    virt = wide // 2
    add_half(plan, refs, step, 1, me, own_t, levels, weights, total, other, amp, (high, low), near)
    copies = begin([(total.at[:, pl.ds(j * virt, virt)], residual.at[j]) for j in range(2)], sem)
    half = aux // 2

    def both(first, n, q):
        return mirrored(high, low, own_s, first, n, q)

    at = 0
    for q in range(0, half, BLOCK):
        block = both(parity * half, q + BLOCK, parity * half + q)
        for c in range(0, BLOCK, LANES):
            upper = q + c + LANES
            packed[at:at + upper, :] = block[:upper, c:c + LANES]
            at += upper
    share(packed, core, keep, send)
    finish(copies)


def share(packed, core, keep, send):
    size = keep.shape[0]
    keep[...] = packed[pl.ds(pl.multiple_of(core * size, 16), size), :]
    send[...] = packed[pl.ds(pl.multiple_of((1 - core) * size, 16), size), :]


def corner_kernel(me_ref, high, low, own_s, keep, send, packed):
    parity, core, _ = place_of(me_ref[0])
    aux = own_s.shape[0]
    half, quarter = aux // 2, aux // 4
    at = 0
    for q in range(half, aux, BLOCK):
        block = mirrored(high, low, own_s, parity * quarter, quarter, q)
        for c in range(0, BLOCK, LANES):
            packed[at:at + quarter, :] = block[:, c:c + LANES]
            at += quarter
    share(packed, core, keep, send)


def encode(x, out, row):
    rows = x.shape[0]
    groups = x.reshape(rows // GROUP, GROUP, LANES)
    largest = jnp.max(jnp.abs(groups), axis=1)
    power = jnp.floor(jnp.log2(jnp.maximum(largest, 1e-30))) + 1.0
    unit = jnp.exp2(BITS - power)
    for g in range(rows // GROUP):
        whole = jnp.round(groups[g] * unit[g:g + 1, :]).astype(I32)
        out[pl.ds(row + g * GROUP, GROUP), :] = whole.astype(I16)
    pad = jnp.zeros((PAD - rows // GROUP, LANES), F32)
    out[pl.ds(row + rows, PAD), :] = jnp.concatenate([power, pad]).astype(I32).astype(I16)


def decode(coded):
    rows = coded.shape[0] - PAD
    wide = coded.astype(I32).astype(F32)
    unit = jnp.exp2(wide[rows:] - BITS)
    return jnp.concatenate(
        [wide[g * GROUP:(g + 1) * GROUP] * unit[g:g + 1, :] for g in range(rows // GROUP)]
    )


def chip_kernel(keep_in, away, got_away, got_keep, keep, send):
    piece = keep.shape[0] // 4
    for t in range(4):
        at, coded = pl.ds(t * piece, piece), pl.ds(t * (piece + PAD), piece + PAD)
        encode(away[at, :] + decode(got_away[coded, :]), send, t * (piece + PAD))
        keep[at, :] = keep_in[at, :] + decode(got_keep[coded, :])


def column_kernel(first, me_ref, mine, theirs, near, across, keep, *sends):
    _, _, z = place_of(me_ref[0])
    piece = keep.shape[0]
    away = across.shape[0] // 4
    far = jnp.concatenate([decode(across[i * away:(i + 1) * away, :]) for i in range(4)])
    for i in range(4):
        at = slice(i * piece, (i + 1) * piece)
        inner = slice(first + i * piece, first + (i + 1) * piece)
        value = (mine[at, :] + theirs[at, :]) + (near[inner, :] + far[inner, :])

        @pl.when(z == i)
        def _():
            keep[...] = value

        for t in (1, 2, 3):
            pl.when((z ^ t) == i)(functools.partial(encode, value, sends[t - 1], 0))


def sum_of(parts):
    return jnp.concatenate([sum((decode(x[...]) for x in others), mine[...]) for mine, *others in (parts[:4], parts[4:])])


def sum_kernel(*rest):
    rest[-1][...] = sum_of(rest[:-1])


def code_kernel(scale, x, out):
    encode(x[...] * scale, out, 0)


def sum_code_kernel(scale, *rest):
    encode(sum_of(rest[:-1]) * scale, rest[-1], 0)


def unpack(src, which, side, z, packed):
    plane = packed.shape[0] // 2
    for t in range(4):
        value = decode(src[t])
        used = 0
        for first, n in ((which * (plane // 18) * 5, plane // 18 * 5), (plane // 18 * (10 + which * 4), plane // 18 * 4)):
            piece = n // 4
            row = side * plane + first + (z ^ t) * piece
            packed[pl.ds(pl.multiple_of(row, 16), piece), :] = value[used:used + piece, :]
            used += piece


def lay_corner(side, packed, square):
    aux = square.shape[0]
    half, quarter = aux // 2, aux // 4
    at = (side + 1) * (packed.shape[0] // 2) - half // LANES * quarter
    first = side * quarter
    for c in range(half, aux, LANES):
        square[first:first + quarter, c:c + LANES] = packed[at:at + quarter, :]
        for r in range(0, quarter, LANES):
            square[c:c + LANES, first + r:first + r + LANES] = packed[at + r:at + r + LANES, :].T
        at += quarter


def lay_triangle(side, packed, square, after=None):
    aux = square.shape[0]
    half, quarter = aux // 2, aux // 4
    at = (side + 1) * (packed.shape[0] // 2) - half // LANES * quarter
    base = side * half
    for c in range(half - LANES, -1, -LANES):
        at -= c + LANES
        columns = slice(base + c, base + c + LANES)
        square[base:base + c + LANES, columns] = packed[at:at + c + LANES, :]
        for r in range(0, c, LANES):
            square[columns, base + r:base + r + LANES] = packed[at + r:at + r + LANES, :].T
        if after is not None:
            after(base + c)


def write_plane(side, packed, square, out, sem):
    aux = square.shape[0]
    half, quarter = aux // 2, aux // 4
    first, base = side * quarter, side * half

    def copy(at, row, rows, column, columns):
        where = (pl.ds(row, rows), pl.ds(column, columns))
        started = pltpu.make_async_copy(square.at[where], out.at[where], sem.at[at])
        started.start()
        return started

    lay_corner(side, packed, square)
    copies = [copy(0, first, quarter, half, half), copy(1, half, half, first, quarter)]
    lay_triangle(
        side, packed, square, lambda row: copies.append(copy(2 + (row - base) // LANES, row, LANES, base, half))
    )
    finish(copies)


def unpack_kernel(me_ref, a, b, sib_a, out, packed, sem, square):
    parity, core, z = place_of(me_ref[0])
    for src, which, side in ((a, core, parity), (b, core, 1 - parity), (sib_a, 1 - core, parity)):
        unpack(src, which, side, z, packed)
    for side in range(2):
        pl.when(parity == side)(functools.partial(write_plane, side, packed, square, out, sem))


def spread_kernel(me_ref, out_in, packed_in, sib_b, out, packed, sem, square):
    parity, core, z = place_of(me_ref[0])
    unpack(sib_b, 1 - core, 1 - parity, z, packed)
    for side in range(2):
        pl.when(parity != side)(functools.partial(write_plane, side, packed, square, out, sem))


def shards(slabs, pair_blocks, occ_energy, virt_energy, domain_map):
    blocks = lax.axis_size("dom")
    me = lax.axis_index("dom").astype(I32)[None]
    own = slabs[0]
    orbitals, aux, virt = own.shape
    wide = orbitals * virt
    upper = aux * (aux + LANES) // 2 // LANES
    piece = upper // 16

    hbm = pl.BlockSpec(memory_space=pl.ANY)
    vmem = pl.BlockSpec(memory_space=pltpu.VMEM)
    smem = pl.BlockSpec(memory_space=pltpu.SMEM)
    slab_s = pltpu.VMEM((aux, wide), BF16)
    amp_s = pltpu.VMEM((wide, wide), BF16)
    total_t = jax.ShapeDtypeStruct((aux, wide), F32)

    def kernel(body, name, ins, outs, out_specs, scratch=(), limit=SMALL_LIMIT, aliases={}, flops=1):
        return pl.pallas_call(
            body,
            out_shape=outs,
            in_specs=ins,
            out_specs=out_specs,
            scratch_shapes=scratch,
            compiler_params=pltpu.CompilerParams(vmem_limit_bytes=limit),
            cost_estimate=pl.CostEstimate(flops=flops, bytes_accessed=1, transcendentals=0),
            input_output_aliases=aliases,
            name=name,
        )

    def dma(n):
        return pltpu.SemaphoreType.DMA((n,))

    def coded(n):
        return jax.ShapeDtypeStruct((n, LANES), I16)

    def plain(n):
        return jax.ShapeDtypeStruct((n, LANES), F32)

    flat = own.reshape(orbitals * aux, virt)
    cuts = [sum(PARTS[:i]) for i in range(len(PARTS) + 1)]
    count, early = len(PARTS), len(PARTS) - 2
    part = flat[:PARTS[0]]
    y = [swapped(part, 2)]
    sib_pairs = swapped(pair_blocks, 1)
    gives_y = ((me[0] >> 1) ^ me[0]) & 1 == 0
    later, part, gives_y = lax.optimization_barrier((flat, part, gives_y))
    sib = swapped(later, 1)
    parts = [None, *kernel(
        functools.partial(split_kernel, cuts[1:-1]), "split", [smem, smem, hbm],
        [jax.ShapeDtypeStruct((n + (0 if i else PAD), virt), BF16) for i, n in enumerate(PARTS[1:])],
        [vmem] * (count - 1), [dma(count - 1)],
    )(me, pair_blocks, later)]

    small = jax.ShapeDtypeStruct((8, wide), F32)
    energy = virt_energy.reshape(-1, LANES)
    levels, weights = kernel(
        functools.partial(prep_kernel, blocks), "prep", [smem] * 3 + [hbm] * 3, (small, small), (vmem, vmem),
        [dma(3), pltpu.VMEM((orbitals, blocks), F32), pltpu.VMEM(energy.shape, F32), pltpu.VMEM(domain_map.shape, I32)],
    )(me, pair_blocks, sib_pairs, occ_energy.T, energy, domain_map)
    sib, near_own = lax.optimization_barrier((sib, flat))
    own_t, own_s, total = kernel(
        own_kernel, "own", [hbm, vmem, vmem],
        (jax.ShapeDtypeStruct((wide, aux), BF16), jax.ShapeDtypeStruct((aux, wide), BF16), total_t), (vmem,) * 3,
        [dma(2), amp_s], LARGE_LIMIT, flops=int(2e10),
    )(near_own, levels, weights)
    sib, part = lax.optimization_barrier((sib, parts[1]))
    y.append(swapped(part, 2))
    y[0], total, own_t, sib, part = lax.optimization_barrier((y[0], total, own_t, sib, parts[2]))
    y.append(swapped(part, 2))
    z = [forwarded(y[0])]
    total = kernel(
        sib_kernel, "sib", [vmem, vmem, hbm, vmem, vmem], total_t, vmem, [dma(2), slab_s, amp_s], LARGE_LIMIT, {1: 0},
        int(1e10),
    )(own_t, total, sib, levels, weights)
    y[1], total, part = lax.optimization_barrier((y[1], total, parts[3]))
    y.append(swapped(part, 2))
    z.append(forwarded(y[1]))
    for i in range(4, count):
        y[i - 2], part, _ = lax.optimization_barrier((y[i - 2], parts[i], y[i - 3]))
        y.append(swapped(part, 2))
        z.append(forwarded(y[i - 2]))
    y[-3], near = lax.optimization_barrier((y[-3], total))
    keep, away, *sends = kernel(
        near_metric_kernel, "near_metric", [smem, vmem, vmem], (plain(upper // 4),) * 2 + (coded(4 * (piece + PAD)),) * 2,
        (vmem,) * 4, [slab_s, slab_s, pltpu.VMEM((upper, LANES), F32)], LARGE_LIMIT, flops=int(1e10),
    )(me, near, own_s)
    y[-2], z[0], keep = lax.optimization_barrier((y[-2], z[0], keep))
    z.append(forwarded(y[-2]))
    got = [swapped(send, 1) for send in sends]
    y[-1], *got = lax.optimization_barrier((y[-1], *got))
    z.append(forwarded(y[-1]))
    y[-1], keep, away = lax.optimization_barrier((y[-1], keep, away))
    keep, send = kernel(
        chip_kernel, "chip", [vmem] * 4, (plain(upper // 4), coded(4 * (piece + PAD))), (vmem, vmem),
    )(keep, away, *got)
    across = swapped(send, 2)
    (y[-1], own_t, keep), z[early:-1] = lax.optimization_barrier(((y[-1], own_t, keep), z[early:-1]))

    def given(rows_y, rows_z):
        return swapped(jnp.where(gives_y, jnp.concatenate(rows_y), jnp.concatenate(rows_z)), 1)

    arrays = {f"y{i}": part for i, part in enumerate(y)}
    arrays |= {f"z{i}": part for i, part in enumerate(z)}
    arrays["x0"] = given(y[:early], z[:early])

    def half_of(which, j):
        name = "y" if which == Y else "z"
        rows = []
        for i, (a, b) in enumerate(zip(cuts, cuts[1:])):
            first, last = max(a, j * aux), min(b, (j + 1) * aux)
            if first >= last:
                continue
            to = first - j * aux
            if which != X:
                rows.append((f"{name}{i}", first - a, last - first, to))
            elif i < early:
                rows.append(("x0", first + (PAD if i > 1 else 0), last - first, to))
            elif i == early:
                n = (b - a) // 2
                rows += [("x1", 0, n, to), ("x2", 0, b - a - n, to + n)]
            else:
                rows.append(("x3", 0, b - a, to))
        return rows, ("x0", cuts[2]) if which == X else (f"{name}1", PARTS[1])

    def pair_step(body, name, step, before=(), outs=(), out_specs=(), scratch=(), flops=1, side=None):
        plan = [half_of(*half) for half in STEPS[step]]
        used = plan if side is None else [plan[side]]
        names = list(dict.fromkeys(n for rows, (at, _) in used for n in [r[0] for r in rows] + [at]))
        return kernel(
            functools.partial(body, plan, names, step), name,
            [smem] + [vmem] * (3 + len(before) + len(names)),
            (total_t, *outs), (vmem, *out_specs), scratch, LARGE_LIMIT, {4: 0} if before else {}, flops,
        )(me, own_t, levels, weights, *before, *[arrays[n] for n in names])

    (total,) = pair_step(first_far_kernel, "far2", 2, scratch=[slab_s, amp_s], flops=int(1e10))
    (total,) = pair_step(far_kernel, "far3", 3, (total,), scratch=[slab_s, amp_s], flops=1)
    total, *late = lax.optimization_barrier((total, y[-2], z[-2]))
    late = jnp.where(gives_y, *late)
    middle = late.shape[0] // 2
    arrays["x1"], arrays["x2"] = swapped(late[:middle], 1), swapped(late[middle:], 1)
    z[-1], total, arrays["x1"], arrays["x2"], across = lax.optimization_barrier(
        (z[-1], total, arrays["x1"], arrays["x2"], across)
    )
    arrays[f"z{count - 1}"] = z[-1]
    arrays["x3"] = given(y[-1:], z[-1:])
    half_s = [pltpu.VMEM((aux, virt), BF16), pltpu.VMEM((wide, virt), BF16)]
    (total,) = pair_step(
        lambda *a: half_kernel(*a[:3], 0, *a[3:]), "half", 4, (total,), scratch=half_s, flops=int(1e9), side=0
    )
    plane = upper // 2
    (_, square), (_, corner) = segments(plane, 0)
    slab_t = jax.ShapeDtypeStruct((aux, wide), BF16)
    _, residual, mine, send, high, low = pair_step(
        last_kernel, "last", 4, (total, own_s, near),
        (jax.ShapeDtypeStruct(own.shape, F32), plain(square), plain(square), slab_t, slab_t), (hbm,) + (vmem,) * 4,
        [dma(2), *half_s, pltpu.VMEM((2 * square, LANES), F32)], side=1,
    )

    def column(first, size, mine, got):
        n = size // 4
        return kernel(
            functools.partial(column_kernel, first), "column", [smem] + [vmem] * 4, (plain(n),) + (coded(n + PAD),) * 3,
            (vmem,) * 4,
        )(me, mine, got, keep, across)

    got = swapped(send, 1)
    mine_b, send_b = kernel(
        corner_kernel, "corner", [smem] + [vmem] * 3, (plain(corner), plain(corner)), (vmem, vmem),
        [pltpu.VMEM((2 * corner, LANES), F32)], LARGE_LIMIT, flops=int(2e9),
    )(me, high, low, own_s)
    got, send_b = lax.optimization_barrier((got, send_b))
    got_b = swapped(send_b, 1)
    keep_a, *sends_a = column(0, square, mine, got)
    summed = [keep_a] + [swapped(sends_a[t - 1], 4 * t) for t in (3, 2, 1)]
    keep_b, *sends_b = column(square, corner, mine_b, got_b)
    summed += [keep_b] + [swapped(sends_b[t - 1], 4 * t) for t in (3, 2, 1)]
    if blocks == 16:
        mine = kernel(
            functools.partial(sum_code_kernel, 1.0 / blocks), "sum_code", [vmem] * 8, coded(piece + PAD), vmem,
        )(*summed)
    else:
        value = kernel(sum_kernel, "sum", [vmem] * 8, plain(piece), vmem)(*summed)
        bit = 16
        while bit < blocks:
            value = value + swapped(value, bit)
            bit *= 2
        mine = kernel(functools.partial(code_kernel, 1.0 / blocks), "code", [vmem], coded(piece + PAD), vmem)(value)

    column = [mine] + [swapped(mine, 4 * t) for t in (1, 2, 3)]
    across = [swapped(c, 2) for c in column]
    a, b = jnp.stack(column), jnp.stack(across)
    sib_a, sib_b = swapped(a, 1), swapped(b, 1)
    whole = jax.ShapeDtypeStruct((aux, aux), F32)
    scratch = [dma(2 + aux // 2 // LANES), pltpu.VMEM((aux, aux), F32)]
    gradient, packed = kernel(
        unpack_kernel, "unpack", [smem] + [vmem] * 3, (whole, plain(upper)), (hbm, vmem), scratch, flops=int(1e9),
    )(me, a, b, sib_a)
    gradient, _ = kernel(
        spread_kernel, "spread", [smem, hbm, vmem, vmem], (whole, plain(upper)), (hbm, vmem), scratch,
        aliases={1: 0, 2: 1},
    )(me, gradient, packed, sib_b)
    return residual[None], gradient


def solution(mesh):
    return jax.shard_map(
        shards,
        mesh=mesh,
        in_specs=(
            P(("grp", "dom"), None, None, None),
            P(("grp", "dom"), None),
            P("grp", None),
            P("grp"),
            P("grp", None),
        ),
        out_specs=(P(("grp", "dom"), None, None, None), P("grp", None)),
        check_vma=False,
    )
```

```python
import functools

import jax
import jax.numpy as jnp
from jax import lax
from jax.experimental import pallas as pl
from jax.experimental.pallas import tpu as pltpu
from jax.sharding import PartitionSpec as P

LARGE_LIMIT = 16 * 1024 * 1024
SMALL_LIMIT = 8 * 1024 * 1024
LANES = 128
BLOCK = 256
PAD = 16
PARTS = (416, 368, 432, 416, 416)
GROUP = 32
BITS = 14
NT = (((1,), (1,)), ((), ()))
TN = (((0,), (0,)), ((), ()))
F32, BF16, I16, I32 = jnp.float32, jnp.bfloat16, jnp.int16, jnp.int32


def move(x, pairs):
    return lax.ppermute(x, "dom", pairs)


def swapped(x, bits):
    return move(x, [(d, d ^ bits) for d in range(lax.axis_size("dom"))])


def forwarded(x):
    devices = range(lax.axis_size("dom"))
    route = [(d, d - 4 if d & 2 else d + 4) for d in devices]
    return move(x, [(a, b) for a, b in route if b in devices])


def begin(copies, sem, at=0):
    started = [pltpu.make_async_copy(a, b, sem.at[at + i]) for i, (a, b) in enumerate(copies)]
    for copy in started:
        copy.start()
    return started


def finish(copies):
    for copy in copies:
        copy.wait()


def place_of(me):
    return (me >> 1) & 1, me & 1, (me >> 2) & 3


def offsets_of(me):
    parity, core, _ = place_of(me)
    return 0, 1 - 2 * core, 2 - 4 * parity, 4 * parity - 2, 2 * core - 1


OWN, SIB, Y, Z, X = range(5)
STEPS = (((OWN, 0), (OWN, 1)), ((SIB, 0), (SIB, 1)), ((Y, 0), (Y, 1)), ((Z, 0), (X, 0)), ((Z, 1), (X, 1)))


def prep_kernel(blocks, me_ref, pairs, sib_pairs, occ_in, energy_in, maps_in, levels, weights, sem, occ, energy, maps):
    copies = begin([(occ_in, occ), (energy_in, energy), (maps_in, maps)], sem)
    me = me_ref[0]
    virt = maps.shape[1]
    finish(copies)
    table = energy[...]
    parts = []
    for _ in range(3):
        part = table.astype(BF16)
        parts.append(part)
        table = table - part.astype(F32)
    block_major = lax.broadcasted_iota(I32, occ.shape, 1)
    row_major = lax.broadcasted_iota(I32, (energy.shape[0], virt), 0)
    lane_major = lax.broadcasted_iota(I32, (LANES, virt), 0)
    for block, offset in enumerate(offsets_of(me)):
        other = me + offset
        who = jnp.clip(other, 0, blocks - 1)
        count = 0
        for s in range(pairs.shape[1]):
            count = count + (pairs[0, s] == other).astype(I32)
            if block in (OWN, SIB):
                count = count + ((pairs, sib_pairs)[block][0, s] == me).astype(I32)
        occupied = jnp.sum(jnp.where(block_major == who, occ[...], 0.0), axis=1, keepdims=True)
        index = maps[pl.ds(who, 1), :]
        pick = (row_major == index // LANES).astype(F32).astype(BF16)
        rows = sum(lax.dot_general(p, pick, TN, preferred_element_type=F32) for p in parts)
        chosen = jnp.sum(jnp.where(lane_major == index % LANES, rows, 0.0), axis=0, keepdims=True)
        for step, halves in enumerate(STEPS):
            for side, (which, j) in enumerate(halves):
                if which == block:
                    at = pl.ds(side * virt, virt)
                    levels[step:step + 1, at] = chosen - occupied[j:j + 1, :]
                    weights[step:step + 1, at] = jnp.full((1, virt), -count.astype(F32), F32)


def add_pair(own_t, other, amp, total, own_level, level, weight, first, halves=None, near=None):
    wide = own_t.shape[0]
    for t in range(0, wide, BLOCK):
        s = pl.ds(t, BLOCK)
        integrals = jnp.dot(own_t[s, :], other[...], preferred_element_type=F32)
        amp[s, :] = (integrals * weight / (own_level[t:t + BLOCK, 0:1] + level)).astype(BF16)
    for t in range(0, wide, BLOCK):
        s = pl.ds(t, BLOCK)
        part = lax.dot_general(other[...], amp[s, :], NT, preferred_element_type=F32)
        value = part if first else total[:, s] + part
        total[:, s] = value if near is None else value + near[:, s]
        if halves is not None:
            high = value.astype(BF16)
            halves[0][:, s] = high
            halves[1][:, s] = (value - high.astype(F32)).astype(BF16)


def split_kernel(cuts, me_ref, pairs, own, *rest):
    parts, sem = rest[:-1], rest[-1]
    copies = begin(
        [(own.at[pl.ds(a, b)], part.at[pl.ds(0, b)]) for a, b, part in zip(cuts, PARTS[1:], parts)], sem
    )
    rows, virt = parts[0].shape[0] - PAD, parts[0].shape[1]
    lane = lax.broadcasted_iota(I32, (PAD, virt), 1)
    listed = jnp.full((PAD, virt), 100, I32)
    for s in range(pairs.shape[1]):
        listed = jnp.where(lane == s, pairs[0, s] - me_ref[0], listed)
    parts[0][rows:, :] = listed.astype(F32).astype(BF16)
    finish(copies)


def own_kernel(own, levels, weights, own_t, own_s, total, sem, amp):
    aux, virt = own.shape[0] // 2, own.shape[1]
    copies = begin([(own.at[pl.ds(j * aux, aux)], own_s.at[:, pl.ds(j * virt, virt)]) for j in range(2)], sem)
    level = levels[...].T
    finish(copies)
    own_t[...] = own_s[...].T
    add_pair(own_t, own_s, amp, total, level, levels[0:1, :], weights[0:1, :], True)


def sib_kernel(own_t, total_in, sib, levels, weights, total, sem, other, amp):
    aux, virt = sib.shape[0] // 2, sib.shape[1]
    copies = begin([(sib.at[pl.ds(j * aux, aux)], other.at[:, pl.ds(j * virt, virt)]) for j in range(2)], sem)
    level = levels[...].T
    finish(copies)
    add_pair(own_t, other, amp, total, level, levels[1:2, :], weights[1:2, :], False)


def fetch(plan, step, me, refs, other, skip=0):
    counts = []
    for side, (rows, (name, at)) in enumerate(plan):
        virt = other.shape[1] // len(plan)
        for source, first, n, to in rows:
            other[to:to + n, side * virt:(side + 1) * virt] = refs[source][first:first + n, :]
        wanted = -offsets_of(me)[STEPS[step][side + skip][0]]
        hits = jnp.where(refs[name][at:at + PAD, :].astype(F32)[0:1, :] == wanted.astype(F32), 1.0, 0.0)
        counts.append(jnp.broadcast_to(jnp.sum(hits, axis=1, keepdims=True), (1, virt)))
    return jnp.concatenate(counts, axis=1) if len(counts) > 1 else counts[0]


def first_far_kernel(plan, names, step, me_ref, own_t, levels, weights, *rest):
    refs = dict(zip(names, rest))
    total, other, amp = rest[len(names):]
    weight = weights[step:step + 1, :] - fetch(plan, step, me_ref[0], refs, other)
    add_pair(own_t, other, amp, total, levels[...].T, levels[step:step + 1, :], weight, True)


def far_kernel(plan, names, step, me_ref, own_t, levels, weights, total_in, *rest):
    refs = dict(zip(names, rest))
    total, other, amp = rest[len(names):]
    weight = weights[step:step + 1, :] - fetch(plan, step, me_ref[0], refs, other)
    add_pair(own_t, other, amp, total, levels[...].T, levels[step:step + 1, :], weight, False)


def segments(plane, which):
    side = plane // 18
    return (which * side * 5, side * 5), (side * 10 + which * side * 4, side * 4)


def rows_of(packed, base, plane, which):
    return jnp.concatenate(
        [packed[pl.ds(pl.multiple_of(base + a, 16), n), :] for a, n in segments(plane, which)]
    )


def near_metric_kernel(me_ref, total, own_s, keep, away, *rest):
    *sends, high, low, packed = rest
    parity, core, _ = place_of(me_ref[0])
    high[...] = total[...].astype(BF16)
    low[...] = (total[...] - high[...].astype(F32)).astype(BF16)
    aux = total.shape[0]
    half, quarter = aux // 2, aux // 4
    plane = packed.shape[0] // 2
    square = plane - half // LANES * quarter
    for q in range(0, aux, BLOCK):
        rows = q + BLOCK
        slab = own_s[q:q + BLOCK, :]
        block = lax.dot_general(high[:rows, :], slab, NT, preferred_element_type=F32)
        block += lax.dot_general(low[:rows, :], slab, NT, preferred_element_type=F32)
        for c in range(q, q + BLOCK, LANES):
            column = block[:, c - q:c - q + LANES]
            base, side = (half, 1) if c >= half else (0, 0)
            k = (c - base) // LANES
            at = side * plane + k * (k + 1) // 2 * LANES
            packed[at:at + (k + 1) * LANES, :] = column[base:c + LANES, :]
            if side:
                for s in range(2):
                    at = s * plane + square + k * quarter
                    packed[at:at + quarter, :] = column[s * quarter:(s + 1) * quarter, :]
    size = plane // 2

    def part(side, which):
        return rows_of(packed, side * plane, plane, which)

    keep[...] = part(parity, core)
    away[...] = part(1 - parity, core)
    given = [part(1 - parity, 1 - core), part(parity, 1 - core)]
    piece = size // 4
    for send, x in zip(sends, given):
        for t in range(4):
            encode(x[t * piece:(t + 1) * piece, :], send, t * (piece + PAD))


def half_kernel(plan, names, step, side, me_ref, own_t, levels, weights, total_in, *rest):
    refs = dict(zip(names, rest))
    total, other, amp = rest[len(names):]
    add_half(plan, refs, step, side, me_ref[0], own_t, levels, weights, total, other, amp)


def add_half(plan, refs, step, side, me, own_t, levels, weights, total, other, amp, halves=None, near=None):
    virt = other.shape[1]
    columns = slice(side * virt, (side + 1) * virt)
    count = fetch([plan[side]], step, me, refs, other, side)
    weight = weights[step:step + 1, columns] - count
    level = levels[step:step + 1, columns]
    add_pair(own_t, other, amp, total, levels[...].T, level, weight, False, halves, near)


def mirrored(high, low, own_s, first, n, q):
    rows, columns = pl.ds(pl.multiple_of(first, 16), n), pl.ds(pl.multiple_of(q, 16), BLOCK)
    pairs = ((high, own_s), (low, own_s), (own_s, high), (own_s, low))
    return sum(lax.dot_general(a[rows, :], b[columns, :], NT, preferred_element_type=F32) for a, b in pairs)


def last_kernel(plan, names, step, me_ref, own_t, levels, weights, total_in, own_s, near, *rest):
    refs = dict(zip(names, rest))
    total, residual, keep, send, high, low, sem, other, amp, packed = rest[len(names):]
    me = me_ref[0]
    parity, core, _ = place_of(me)
    aux, wide = total.shape
    virt = wide // 2
    add_half(plan, refs, step, 1, me, own_t, levels, weights, total, other, amp, (high, low), near)
    copies = begin([(total.at[:, pl.ds(j * virt, virt)], residual.at[j]) for j in range(2)], sem)
    half = aux // 2

    def both(first, n, q):
        return mirrored(high, low, own_s, first, n, q)

    at = 0
    for q in range(0, half, BLOCK):
        block = both(parity * half, q + BLOCK, parity * half + q)
        for c in range(0, BLOCK, LANES):
            upper = q + c + LANES
            packed[at:at + upper, :] = block[:upper, c:c + LANES]
            at += upper
    share(packed, core, keep, send)
    finish(copies)


def share(packed, core, keep, send):
    size = keep.shape[0]
    keep[...] = packed[pl.ds(pl.multiple_of(core * size, 16), size), :]
    send[...] = packed[pl.ds(pl.multiple_of((1 - core) * size, 16), size), :]


def corner_kernel(me_ref, high, low, own_s, keep, send, packed):
    parity, core, _ = place_of(me_ref[0])
    aux = own_s.shape[0]
    half, quarter = aux // 2, aux // 4
    at = 0
    for q in range(half, aux, BLOCK):
        block = mirrored(high, low, own_s, parity * quarter, quarter, q)
        for c in range(0, BLOCK, LANES):
            packed[at:at + quarter, :] = block[:, c:c + LANES]
            at += quarter
    share(packed, core, keep, send)


def powers(exponent):
    first = jnp.clip(exponent, -100.0, 100.0)
    return jnp.exp2(first), jnp.exp2(exponent - first)


def encode(x, out, row):
    rows = x.shape[0]
    groups = x.reshape(rows // GROUP, GROUP, LANES)
    largest = jnp.max(jnp.abs(groups), axis=1)
    power = jnp.floor(jnp.log2(jnp.maximum(largest, 1e-37))) + 1.0
    a, b = powers(BITS - power)
    for g in range(rows // GROUP):
        whole = jnp.round(groups[g] * a[g:g + 1, :] * b[g:g + 1, :]).astype(I32)
        out[pl.ds(row + g * GROUP, GROUP), :] = whole.astype(I16)
    pad = jnp.zeros((PAD - rows // GROUP, LANES), F32)
    out[pl.ds(row + rows, PAD), :] = jnp.concatenate([power, pad]).astype(I32).astype(I16)


def decode(coded):
    rows = coded.shape[0] - PAD
    wide = coded.astype(I32).astype(F32)
    a, b = powers(wide[rows:] - BITS)
    return jnp.concatenate(
        [wide[g * GROUP:(g + 1) * GROUP] * a[g:g + 1, :] * b[g:g + 1, :] for g in range(rows // GROUP)]
    )


def chip_kernel(keep_in, away, got_away, got_keep, keep, send):
    piece = keep.shape[0] // 4
    for t in range(4):
        at, coded = pl.ds(t * piece, piece), pl.ds(t * (piece + PAD), piece + PAD)
        encode(away[at, :] + decode(got_away[coded, :]), send, t * (piece + PAD))
        keep[at, :] = keep_in[at, :] + decode(got_keep[coded, :])


def column_kernel(first, me_ref, mine, theirs, near, across, keep, *sends):
    _, _, z = place_of(me_ref[0])
    piece = keep.shape[0]
    away = across.shape[0] // 4
    far = jnp.concatenate([decode(across[i * away:(i + 1) * away, :]) for i in range(4)])
    for i in range(4):
        at = slice(i * piece, (i + 1) * piece)
        inner = slice(first + i * piece, first + (i + 1) * piece)
        value = (mine[at, :] + theirs[at, :]) + (near[inner, :] + far[inner, :])

        @pl.when(z == i)
        def _():
            keep[...] = value

        for t in (1, 2, 3):
            pl.when((z ^ t) == i)(functools.partial(encode, value, sends[t - 1], 0))


def sum_of(parts):
    return jnp.concatenate([sum((decode(x[...]) for x in others), mine[...]) for mine, *others in (parts[:4], parts[4:])])


def sum_kernel(*rest):
    rest[-1][...] = sum_of(rest[:-1])


def code_kernel(scale, x, out):
    encode(x[...] * scale, out, 0)


def sum_code_kernel(scale, *rest):
    encode(sum_of(rest[:-1]) * scale, rest[-1], 0)


def unpack(src, which, side, z, packed):
    plane = packed.shape[0] // 2
    for t in range(4):
        value = decode(src[t])
        used = 0
        for first, n in ((which * (plane // 18) * 5, plane // 18 * 5), (plane // 18 * (10 + which * 4), plane // 18 * 4)):
            piece = n // 4
            row = side * plane + first + (z ^ t) * piece
            packed[pl.ds(pl.multiple_of(row, 16), piece), :] = value[used:used + piece, :]
            used += piece


def lay_corner(side, packed, square):
    aux = square.shape[0]
    half, quarter = aux // 2, aux // 4
    at = (side + 1) * (packed.shape[0] // 2) - half // LANES * quarter
    first = side * quarter
    for c in range(half, aux, LANES):
        square[first:first + quarter, c:c + LANES] = packed[at:at + quarter, :]
        for r in range(0, quarter, LANES):
            square[c:c + LANES, first + r:first + r + LANES] = packed[at + r:at + r + LANES, :].T
        at += quarter


def lay_triangle(side, packed, square, after=None):
    aux = square.shape[0]
    half, quarter = aux // 2, aux // 4
    at = (side + 1) * (packed.shape[0] // 2) - half // LANES * quarter
    base = side * half
    for c in range(half - LANES, -1, -LANES):
        at -= c + LANES
        columns = slice(base + c, base + c + LANES)
        square[base:base + c + LANES, columns] = packed[at:at + c + LANES, :]
        for r in range(0, c, LANES):
            square[columns, base + r:base + r + LANES] = packed[at + r:at + r + LANES, :].T
        if after is not None:
            after(base + c)


def write_plane(side, packed, square, out, sem):
    aux = square.shape[0]
    half, quarter = aux // 2, aux // 4
    first, base = side * quarter, side * half

    def copy(at, row, rows, column, columns):
        where = (pl.ds(row, rows), pl.ds(column, columns))
        started = pltpu.make_async_copy(square.at[where], out.at[where], sem.at[at])
        started.start()
        return started

    lay_corner(side, packed, square)
    copies = [copy(0, first, quarter, half, half), copy(1, half, half, first, quarter)]
    lay_triangle(
        side, packed, square, lambda row: copies.append(copy(2 + (row - base) // LANES, row, LANES, base, half))
    )
    finish(copies)


def unpack_kernel(me_ref, a, b, sib_a, out, packed, sem, square):
    parity, core, z = place_of(me_ref[0])
    for src, which, side in ((a, core, parity), (b, core, 1 - parity), (sib_a, 1 - core, parity)):
        unpack(src, which, side, z, packed)
    for side in range(2):
        pl.when(parity == side)(functools.partial(write_plane, side, packed, square, out, sem))


def spread_kernel(me_ref, out_in, packed_in, sib_b, out, packed, sem, square):
    parity, core, z = place_of(me_ref[0])
    unpack(sib_b, 1 - core, 1 - parity, z, packed)
    for side in range(2):
        pl.when(parity != side)(functools.partial(write_plane, side, packed, square, out, sem))


def shards(slabs, pair_blocks, occ_energy, virt_energy, domain_map):
    blocks = lax.axis_size("dom")
    me = lax.axis_index("dom").astype(I32)[None]
    own = slabs[0]
    orbitals, aux, virt = own.shape
    wide = orbitals * virt
    upper = aux * (aux + LANES) // 2 // LANES
    piece = upper // 16

    hbm = pl.BlockSpec(memory_space=pl.ANY)
    vmem = pl.BlockSpec(memory_space=pltpu.VMEM)
    smem = pl.BlockSpec(memory_space=pltpu.SMEM)
    slab_s = pltpu.VMEM((aux, wide), BF16)
    amp_s = pltpu.VMEM((wide, wide), BF16)
    total_t = jax.ShapeDtypeStruct((aux, wide), F32)

    def kernel(body, name, ins, outs, out_specs, scratch=(), limit=SMALL_LIMIT, aliases={}, flops=1):
        return pl.pallas_call(
            body,
            out_shape=outs,
            in_specs=ins,
            out_specs=out_specs,
            scratch_shapes=scratch,
            compiler_params=pltpu.CompilerParams(vmem_limit_bytes=limit),
            cost_estimate=pl.CostEstimate(flops=flops, bytes_accessed=1, transcendentals=0),
            input_output_aliases=aliases,
            name=name,
        )

    def dma(n):
        return pltpu.SemaphoreType.DMA((n,))

    def coded(n):
        return jax.ShapeDtypeStruct((n, LANES), I16)

    def plain(n):
        return jax.ShapeDtypeStruct((n, LANES), F32)

    flat = own.reshape(orbitals * aux, virt)
    cuts = [sum(PARTS[:i]) for i in range(len(PARTS) + 1)]
    count, early = len(PARTS), len(PARTS) - 2
    part = flat[:PARTS[0]]
    y = [swapped(part, 2)]
    sib_pairs = swapped(pair_blocks, 1)
    gives_y = ((me[0] >> 1) ^ me[0]) & 1 == 0
    later, part, gives_y = lax.optimization_barrier((flat, part, gives_y))
    sib = swapped(later, 1)
    parts = [None, *kernel(
        functools.partial(split_kernel, cuts[1:-1]), "split", [smem, smem, hbm],
        [jax.ShapeDtypeStruct((n + (0 if i else PAD), virt), BF16) for i, n in enumerate(PARTS[1:])],
        [vmem] * (count - 1), [dma(count - 1)],
    )(me, pair_blocks, later)]

    small = jax.ShapeDtypeStruct((8, wide), F32)
    energy = virt_energy.reshape(-1, LANES)
    levels, weights = kernel(
        functools.partial(prep_kernel, blocks), "prep", [smem] * 3 + [hbm] * 3, (small, small), (vmem, vmem),
        [dma(3), pltpu.VMEM((orbitals, blocks), F32), pltpu.VMEM(energy.shape, F32), pltpu.VMEM(domain_map.shape, I32)],
    )(me, pair_blocks, sib_pairs, occ_energy.T, energy, domain_map)
    sib, near_own = lax.optimization_barrier((sib, flat))
    own_t, own_s, total = kernel(
        own_kernel, "own", [hbm, vmem, vmem],
        (jax.ShapeDtypeStruct((wide, aux), BF16), jax.ShapeDtypeStruct((aux, wide), BF16), total_t), (vmem,) * 3,
        [dma(2), amp_s], LARGE_LIMIT, flops=int(2e10),
    )(near_own, levels, weights)
    sib, part = lax.optimization_barrier((sib, parts[1]))
    y.append(swapped(part, 2))
    y[0], total, own_t, sib, part = lax.optimization_barrier((y[0], total, own_t, sib, parts[2]))
    y.append(swapped(part, 2))
    z = [forwarded(y[0])]
    total = kernel(
        sib_kernel, "sib", [vmem, vmem, hbm, vmem, vmem], total_t, vmem, [dma(2), slab_s, amp_s], LARGE_LIMIT, {1: 0},
        int(1e10),
    )(own_t, total, sib, levels, weights)
    y[1], total, part = lax.optimization_barrier((y[1], total, parts[3]))
    y.append(swapped(part, 2))
    z.append(forwarded(y[1]))
    for i in range(4, count):
        y[i - 2], part, _ = lax.optimization_barrier((y[i - 2], parts[i], y[i - 3]))
        y.append(swapped(part, 2))
        z.append(forwarded(y[i - 2]))
    y[-3], near = lax.optimization_barrier((y[-3], total))
    keep, away, *sends = kernel(
        near_metric_kernel, "near_metric", [smem, vmem, vmem], (plain(upper // 4),) * 2 + (coded(4 * (piece + PAD)),) * 2,
        (vmem,) * 4, [slab_s, slab_s, pltpu.VMEM((upper, LANES), F32)], LARGE_LIMIT, flops=int(1e10),
    )(me, near, own_s)
    y[-2], z[0], keep = lax.optimization_barrier((y[-2], z[0], keep))
    z.append(forwarded(y[-2]))
    got = [swapped(send, 1) for send in sends]
    y[-1], *got = lax.optimization_barrier((y[-1], *got))
    z.append(forwarded(y[-1]))
    y[-1], keep, away = lax.optimization_barrier((y[-1], keep, away))
    keep, send = kernel(
        chip_kernel, "chip", [vmem] * 4, (plain(upper // 4), coded(4 * (piece + PAD))), (vmem, vmem),
    )(keep, away, *got)
    across = swapped(send, 2)
    (y[-1], own_t, keep), z[early:-1] = lax.optimization_barrier(((y[-1], own_t, keep), z[early:-1]))

    def given(rows_y, rows_z):
        return swapped(jnp.where(gives_y, jnp.concatenate(rows_y), jnp.concatenate(rows_z)), 1)

    arrays = {f"y{i}": part for i, part in enumerate(y)}
    arrays |= {f"z{i}": part for i, part in enumerate(z)}
    arrays["x0"] = given(y[:early], z[:early])

    def half_of(which, j):
        name = "y" if which == Y else "z"
        rows = []
        for i, (a, b) in enumerate(zip(cuts, cuts[1:])):
            first, last = max(a, j * aux), min(b, (j + 1) * aux)
            if first >= last:
                continue
            to = first - j * aux
            if which != X:
                rows.append((f"{name}{i}", first - a, last - first, to))
            elif i < early:
                rows.append(("x0", first + (PAD if i > 1 else 0), last - first, to))
            elif i == early:
                n = (b - a) // 2
                rows += [("x1", 0, n, to), ("x2", 0, b - a - n, to + n)]
            else:
                rows.append(("x3", 0, b - a, to))
        return rows, ("x0", cuts[2]) if which == X else (f"{name}1", PARTS[1])

    def pair_step(body, name, step, before=(), outs=(), out_specs=(), scratch=(), flops=1, side=None):
        plan = [half_of(*half) for half in STEPS[step]]
        used = plan if side is None else [plan[side]]
        names = list(dict.fromkeys(n for rows, (at, _) in used for n in [r[0] for r in rows] + [at]))
        return kernel(
            functools.partial(body, plan, names, step), name,
            [smem] + [vmem] * (3 + len(before) + len(names)),
            (total_t, *outs), (vmem, *out_specs), scratch, LARGE_LIMIT, {4: 0} if before else {}, flops,
        )(me, own_t, levels, weights, *before, *[arrays[n] for n in names])

    (total,) = pair_step(first_far_kernel, "far2", 2, scratch=[slab_s, amp_s], flops=int(1e10))
    (total,) = pair_step(far_kernel, "far3", 3, (total,), scratch=[slab_s, amp_s], flops=1)
    total, *late = lax.optimization_barrier((total, y[-2], z[-2]))
    late = jnp.where(gives_y, *late)
    middle = late.shape[0] // 2
    arrays["x1"], arrays["x2"] = swapped(late[:middle], 1), swapped(late[middle:], 1)
    z[-1], total, arrays["x1"], arrays["x2"], across = lax.optimization_barrier(
        (z[-1], total, arrays["x1"], arrays["x2"], across)
    )
    arrays[f"z{count - 1}"] = z[-1]
    arrays["x3"] = given(y[-1:], z[-1:])
    half_s = [pltpu.VMEM((aux, virt), BF16), pltpu.VMEM((wide, virt), BF16)]
    (total,) = pair_step(
        lambda *a: half_kernel(*a[:3], 0, *a[3:]), "half", 4, (total,), scratch=half_s, flops=int(1e9), side=0
    )
    plane = upper // 2
    (_, square), (_, corner) = segments(plane, 0)
    slab_t = jax.ShapeDtypeStruct((aux, wide), BF16)
    _, residual, mine, send, high, low = pair_step(
        last_kernel, "last", 4, (total, own_s, near),
        (jax.ShapeDtypeStruct(own.shape, F32), plain(square), plain(square), slab_t, slab_t), (hbm,) + (vmem,) * 4,
        [dma(2), *half_s, pltpu.VMEM((2 * square, LANES), F32)], side=1,
    )

    def column(first, size, mine, got):
        n = size // 4
        return kernel(
            functools.partial(column_kernel, first), "column", [smem] + [vmem] * 4, (plain(n),) + (coded(n + PAD),) * 3,
            (vmem,) * 4,
        )(me, mine, got, keep, across)

    got = swapped(send, 1)
    mine_b, send_b = kernel(
        corner_kernel, "corner", [smem] + [vmem] * 3, (plain(corner), plain(corner)), (vmem, vmem),
        [pltpu.VMEM((2 * corner, LANES), F32)], LARGE_LIMIT, flops=int(2e9),
    )(me, high, low, own_s)
    got, send_b = lax.optimization_barrier((got, send_b))
    got_b = swapped(send_b, 1)
    keep_a, *sends_a = column(0, square, mine, got)
    summed = [keep_a] + [swapped(sends_a[t - 1], 4 * t) for t in (3, 2, 1)]
    keep_b, *sends_b = column(square, corner, mine_b, got_b)
    summed += [keep_b] + [swapped(sends_b[t - 1], 4 * t) for t in (3, 2, 1)]
    if blocks == 16:
        mine = kernel(
            functools.partial(sum_code_kernel, 1.0 / blocks), "sum_code", [vmem] * 8, coded(piece + PAD), vmem,
        )(*summed)
    else:
        value = kernel(sum_kernel, "sum", [vmem] * 8, plain(piece), vmem)(*summed)
        bit = 16
        while bit < blocks:
            value = value + swapped(value, bit)
            bit *= 2
        mine = kernel(functools.partial(code_kernel, 1.0 / blocks), "code", [vmem], coded(piece + PAD), vmem)(value)

    column = [mine] + [swapped(mine, 4 * t) for t in (1, 2, 3)]
    across = [swapped(c, 2) for c in column]
    a, b = jnp.stack(column), jnp.stack(across)
    sib_a, sib_b = swapped(a, 1), swapped(b, 1)
    whole = jax.ShapeDtypeStruct((aux, aux), F32)
    scratch = [dma(2 + aux // 2 // LANES), pltpu.VMEM((aux, aux), F32)]
    gradient, packed = kernel(
        unpack_kernel, "unpack", [smem] + [vmem] * 3, (whole, plain(upper)), (hbm, vmem), scratch, flops=int(1e9),
    )(me, a, b, sib_a)
    gradient, _ = kernel(
        spread_kernel, "spread", [smem, hbm, vmem, vmem], (whole, plain(upper)), (hbm, vmem), scratch,
        aliases={1: 0, 2: 1},
    )(me, gradient, packed, sib_b)
    return residual[None], gradient


def solution(mesh):
    return jax.shard_map(
        shards,
        mesh=mesh,
        in_specs=(
            P(("grp", "dom"), None, None, None),
            P(("grp", "dom"), None),
            P("grp", None),
            P("grp"),
            P("grp", None),
        ),
        out_specs=(P(("grp", "dom"), None, None, None), P("grp", None)),
        check_vma=False,
    )
```

```python
import functools

import jax
import jax.numpy as jnp
from jax import lax
from jax.experimental import pallas as pl
from jax.experimental.pallas import tpu as pltpu
from jax.sharding import PartitionSpec as P

LARGE_LIMIT = 16 * 1024 * 1024
SMALL_LIMIT = 8 * 1024 * 1024
LANES = 128
BLOCK = 256
PAD = 16
PARTS = (416, 368, 432, 416, 416)
GROUP = 32
BITS = 14
NT = (((1,), (1,)), ((), ()))
TN = (((0,), (0,)), ((), ()))
F32, BF16, I16, I32 = jnp.float32, jnp.bfloat16, jnp.int16, jnp.int32


def move(x, pairs):
    return lax.ppermute(x, "dom", pairs)


def swapped(x, bits):
    return move(x, [(d, d ^ bits) for d in range(lax.axis_size("dom"))])


def forwarded(x):
    devices = range(lax.axis_size("dom"))
    route = [(d, d - 4 if d & 2 else d + 4) for d in devices]
    return move(x, [(a, b) for a, b in route if b in devices])


def begin(copies, sem, at=0):
    started = [pltpu.make_async_copy(a, b, sem.at[at + i]) for i, (a, b) in enumerate(copies)]
    for copy in started:
        copy.start()
    return started


def finish(copies):
    for copy in copies:
        copy.wait()


def place_of(me):
    return (me >> 1) & 1, me & 1, (me >> 2) & 3


def offsets_of(me):
    parity, core, _ = place_of(me)
    return 0, 1 - 2 * core, 2 - 4 * parity, 4 * parity - 2, 2 * core - 1


OWN, SIB, Y, Z, X = range(5)
STEPS = (((OWN, 0), (OWN, 1)), ((SIB, 0), (SIB, 1)), ((Y, 0), (Y, 1)), ((Z, 0), (X, 0)), ((Z, 1), (X, 1)))


def prep_kernel(blocks, me_ref, pairs, sib_pairs, occ_in, energy_in, maps_in, levels, weights, sem, occ, energy, maps):
    copies = begin([(occ_in, occ), (energy_in, energy), (maps_in, maps)], sem)
    me = me_ref[0]
    virt = maps.shape[1]
    finish(copies)
    table = energy[...]
    parts = []
    for _ in range(3):
        part = table.astype(BF16)
        parts.append(part)
        table = table - part.astype(F32)
    block_major = lax.broadcasted_iota(I32, occ.shape, 1)
    row_major = lax.broadcasted_iota(I32, (energy.shape[0], virt), 0)
    lane_major = lax.broadcasted_iota(I32, (LANES, virt), 0)
    for block, offset in enumerate(offsets_of(me)):
        other = me + offset
        who = jnp.clip(other, 0, blocks - 1)
        count = 0
        for s in range(pairs.shape[1]):
            count = count + (pairs[0, s] == other).astype(I32)
            if block in (OWN, SIB):
                count = count + ((pairs, sib_pairs)[block][0, s] == me).astype(I32)
        occupied = jnp.sum(jnp.where(block_major == who, occ[...], 0.0), axis=1, keepdims=True)
        index = maps[pl.ds(who, 1), :]
        pick = (row_major == index // LANES).astype(F32).astype(BF16)
        rows = sum(lax.dot_general(p, pick, TN, preferred_element_type=F32) for p in parts)
        chosen = jnp.sum(jnp.where(lane_major == index % LANES, rows, 0.0), axis=0, keepdims=True)
        for step, halves in enumerate(STEPS):
            for side, (which, j) in enumerate(halves):
                if which == block:
                    at = pl.ds(side * virt, virt)
                    levels[step:step + 1, at] = chosen - occupied[j:j + 1, :]
                    weights[step:step + 1, at] = jnp.full((1, virt), -count.astype(F32), F32)


def add_pair(own_t, other, amp, total, own_level, level, weight, first, halves=None, near=None):
    wide = own_t.shape[0]
    for t in range(0, wide, BLOCK):
        s = pl.ds(t, BLOCK)
        integrals = jnp.dot(own_t[s, :], other[...], preferred_element_type=F32)
        amp[s, :] = (integrals * weight / (own_level[t:t + BLOCK, 0:1] + level)).astype(BF16)
    for t in range(0, wide, BLOCK):
        s = pl.ds(t, BLOCK)
        part = lax.dot_general(other[...], amp[s, :], NT, preferred_element_type=F32)
        value = part if first else total[:, s] + part
        total[:, s] = value if near is None else value + near[:, s]
        if halves is not None:
            high = value.astype(BF16)
            halves[0][:, s] = high
            halves[1][:, s] = (value - high.astype(F32)).astype(BF16)


def split_kernel(cuts, me_ref, pairs, own, *rest):
    parts, sem = rest[:-1], rest[-1]
    copies = begin(
        [(own.at[pl.ds(a, b)], part.at[pl.ds(0, b)]) for a, b, part in zip(cuts, PARTS[1:], parts)], sem
    )
    rows, virt = parts[0].shape[0] - PAD, parts[0].shape[1]
    lane = lax.broadcasted_iota(I32, (PAD, virt), 1)
    listed = jnp.full((PAD, virt), 100, I32)
    for s in range(pairs.shape[1]):
        listed = jnp.where(lane == s, pairs[0, s] - me_ref[0], listed)
    parts[0][rows:, :] = listed.astype(F32).astype(BF16)
    finish(copies)


def own_kernel(own, levels, weights, own_t, own_s, total, sem, amp):
    aux, virt = own.shape[0] // 2, own.shape[1]
    copies = begin([(own.at[pl.ds(j * aux, aux)], own_s.at[:, pl.ds(j * virt, virt)]) for j in range(2)], sem)
    level = levels[...].T
    finish(copies)
    own_t[...] = own_s[...].T
    add_pair(own_t, own_s, amp, total, level, levels[0:1, :], weights[0:1, :], True)


def sib_kernel(own_t, total_in, sib, levels, weights, total, sem, other, amp):
    aux, virt = sib.shape[0] // 2, sib.shape[1]
    copies = begin([(sib.at[pl.ds(j * aux, aux)], other.at[:, pl.ds(j * virt, virt)]) for j in range(2)], sem)
    level = levels[...].T
    finish(copies)
    add_pair(own_t, other, amp, total, level, levels[1:2, :], weights[1:2, :], False)


def fetch(plan, step, me, refs, other, skip=0):
    counts = []
    for side, (rows, (name, at)) in enumerate(plan):
        virt = other.shape[1] // len(plan)
        for source, first, n, to in rows:
            other[to:to + n, side * virt:(side + 1) * virt] = refs[source][first:first + n, :]
        wanted = -offsets_of(me)[STEPS[step][side + skip][0]]
        hits = jnp.where(refs[name][at:at + PAD, :].astype(F32)[0:1, :] == wanted.astype(F32), 1.0, 0.0)
        counts.append(jnp.broadcast_to(jnp.sum(hits, axis=1, keepdims=True), (1, virt)))
    return jnp.concatenate(counts, axis=1) if len(counts) > 1 else counts[0]


def first_far_kernel(plan, names, step, me_ref, own_t, levels, weights, *rest):
    refs = dict(zip(names, rest))
    total, other, amp = rest[len(names):]
    weight = weights[step:step + 1, :] - fetch(plan, step, me_ref[0], refs, other)
    add_pair(own_t, other, amp, total, levels[...].T, levels[step:step + 1, :], weight, True)


def far_kernel(plan, names, step, me_ref, own_t, levels, weights, total_in, *rest):
    refs = dict(zip(names, rest))
    total, other, amp = rest[len(names):]
    weight = weights[step:step + 1, :] - fetch(plan, step, me_ref[0], refs, other)
    add_pair(own_t, other, amp, total, levels[...].T, levels[step:step + 1, :], weight, False)


def segments(plane, which):
    side = plane // 18
    return (which * side * 5, side * 5), (side * 10 + which * side * 4, side * 4)


def rows_of(packed, base, plane, which):
    return jnp.concatenate(
        [packed[pl.ds(pl.multiple_of(base + a, 16), n), :] for a, n in segments(plane, which)]
    )


def near_metric_kernel(me_ref, total, own_s, keep, away, *rest):
    *sends, high, low, packed = rest
    parity, core, _ = place_of(me_ref[0])
    high[...] = total[...].astype(BF16)
    low[...] = (total[...] - high[...].astype(F32)).astype(BF16)
    aux = total.shape[0]
    half, quarter = aux // 2, aux // 4
    plane = packed.shape[0] // 2
    square = plane - half // LANES * quarter
    for q in range(0, aux, BLOCK):
        rows = q + BLOCK
        slab = own_s[q:q + BLOCK, :]
        block = lax.dot_general(high[:rows, :], slab, NT, preferred_element_type=F32)
        block += lax.dot_general(low[:rows, :], slab, NT, preferred_element_type=F32)
        for c in range(q, q + BLOCK, LANES):
            column = block[:, c - q:c - q + LANES]
            base, side = (half, 1) if c >= half else (0, 0)
            k = (c - base) // LANES
            at = side * plane + k * (k + 1) // 2 * LANES
            packed[at:at + (k + 1) * LANES, :] = column[base:c + LANES, :]
            if side:
                for s in range(2):
                    at = s * plane + square + k * quarter
                    packed[at:at + quarter, :] = column[s * quarter:(s + 1) * quarter, :]
    size = plane // 2

    def part(side, which):
        return rows_of(packed, side * plane, plane, which)

    keep[...] = part(parity, core)
    away[...] = part(1 - parity, core)
    given = [part(1 - parity, 1 - core), part(parity, 1 - core)]
    piece = size // 4
    for send, x in zip(sends, given):
        for t in range(4):
            encode(x[t * piece:(t + 1) * piece, :], send, t * (piece + PAD))


def half_kernel(plan, names, step, side, me_ref, own_t, levels, weights, total_in, *rest):
    refs = dict(zip(names, rest))
    total, other, amp = rest[len(names):]
    add_half(plan, refs, step, side, me_ref[0], own_t, levels, weights, total, other, amp)


def add_half(plan, refs, step, side, me, own_t, levels, weights, total, other, amp, halves=None, near=None):
    virt = other.shape[1]
    columns = slice(side * virt, (side + 1) * virt)
    count = fetch([plan[side]], step, me, refs, other, side)
    weight = weights[step:step + 1, columns] - count
    level = levels[step:step + 1, columns]
    add_pair(own_t, other, amp, total, levels[...].T, level, weight, False, halves, near)


def mirrored(high, low, own_s, first, n, q):
    rows, columns = pl.ds(pl.multiple_of(first, 16), n), pl.ds(pl.multiple_of(q, 16), BLOCK)
    pairs = ((high, own_s), (low, own_s), (own_s, high), (own_s, low))
    return sum(lax.dot_general(a[rows, :], b[columns, :], NT, preferred_element_type=F32) for a, b in pairs)


def last_kernel(plan, names, step, me_ref, own_t, levels, weights, total_in, own_s, near, *rest):
    refs = dict(zip(names, rest))
    total, residual, keep, send, high, low, sem, other, amp, packed = rest[len(names):]
    me = me_ref[0]
    parity, core, _ = place_of(me)
    aux, wide = total.shape
    virt = wide // 2
    add_half(plan, refs, step, 1, me, own_t, levels, weights, total, other, amp, (high, low), near)
    copies = begin([(total.at[:, pl.ds(j * virt, virt)], residual.at[j]) for j in range(2)], sem)
    half = aux // 2

    def both(first, n, q):
        return mirrored(high, low, own_s, first, n, q)

    at = 0
    for q in range(0, half, BLOCK):
        block = both(parity * half, q + BLOCK, parity * half + q)
        for c in range(0, BLOCK, LANES):
            upper = q + c + LANES
            packed[at:at + upper, :] = block[:upper, c:c + LANES]
            at += upper
    share(packed, core, keep, send)
    finish(copies)


def share(packed, core, keep, send):
    size = keep.shape[0]
    keep[...] = packed[pl.ds(pl.multiple_of(core * size, 16), size), :]
    send[...] = packed[pl.ds(pl.multiple_of((1 - core) * size, 16), size), :]


def corner_kernel(me_ref, high, low, own_s, keep, send, packed):
    parity, core, _ = place_of(me_ref[0])
    aux = own_s.shape[0]
    half, quarter = aux // 2, aux // 4
    at = 0
    for q in range(half, aux, BLOCK):
        block = mirrored(high, low, own_s, parity * quarter, quarter, q)
        for c in range(0, BLOCK, LANES):
            packed[at:at + quarter, :] = block[:, c:c + LANES]
            at += quarter
    share(packed, core, keep, send)


def powers(exponent):
    first = jnp.clip(exponent, -100.0, 100.0)
    return jnp.exp2(first), jnp.exp2(exponent - first)


def quantize(x, out, row):
    rows = x.shape[0]
    groups = x.reshape(rows // GROUP, GROUP, LANES)
    largest = jnp.max(jnp.abs(groups), axis=1)
    power = jnp.floor(jnp.log2(jnp.maximum(largest, 1e-37))) + 1.0
    a, b = powers(BITS - power)
    for g in range(rows // GROUP):
        whole = jnp.round(groups[g] * a[g:g + 1, :] * b[g:g + 1, :]).astype(I32)
        out[pl.ds(row + g * GROUP, GROUP), :] = whole.astype(I16)
    return power


def padded(power):
    return jnp.concatenate([power, jnp.zeros((PAD - power.shape[0], LANES), F32)])


def encode(x, out, row):
    power = quantize(x, out, row)
    out[pl.ds(row + x.shape[0], PAD), :] = padded(power).astype(I32).astype(I16)


def restore(coded, power):
    wide = coded.astype(I32).astype(F32)
    a, b = powers(power - BITS)
    return jnp.concatenate([
        wide[g * GROUP:(g + 1) * GROUP] * a[g:g + 1, :] * b[g:g + 1, :] for g in range(wide.shape[0] // GROUP)
    ])


def decode(coded):
    rows = coded.shape[0] - PAD
    return restore(coded[:rows], coded[rows:].astype(I32).astype(F32))


def chip_kernel(keep_in, away, got_away, got_keep, keep, send):
    piece = keep.shape[0] // 4
    for t in range(4):
        at, coded = pl.ds(t * piece, piece), pl.ds(t * (piece + PAD), piece + PAD)
        encode(away[at, :] + decode(got_away[coded, :]), send, t * (piece + PAD))
        keep[at, :] = keep_in[at, :] + decode(got_keep[coded, :])


def column_kernel(first, me_ref, mine, theirs, near, across, *rest):
    *given, keep, s1, s2, s3 = rest[:5] if first else rest[:4]
    sends = (s1, s2, s3)
    apart = None if first else rest[4]
    _, _, z = place_of(me_ref[0])

    def send(value, t):
        out = sends[t - 1]
        power = quantize(value, out, 0)
        if apart is not None:
            apart[t - 1] = padded(power)
        else:
            early = given[0][t - 1][:first // 4 // GROUP, :]
            both = padded(jnp.concatenate([early, power]))
            out[value.shape[0]:, :] = both.astype(I32).astype(I16)

    piece = keep.shape[0]
    away = across.shape[0] // 4
    far = jnp.concatenate([decode(across[i * away:(i + 1) * away, :]) for i in range(4)])
    for i in range(4):
        at = slice(i * piece, (i + 1) * piece)
        inner = slice(first + i * piece, first + (i + 1) * piece)
        value = (mine[at, :] + theirs[at, :]) + (near[inner, :] + far[inner, :])

        @pl.when(z == i)
        def _():
            keep[...] = value

        for t in (1, 2, 3):
            pl.when((z ^ t) == i)(functools.partial(send, value, t))


def sum_of(parts):
    (keep_a, *early), (keep_b, *late) = parts[:4], parts[4:]
    rows_a, rows_b = keep_a.shape[0], keep_b.shape[0]
    cut = rows_a // GROUP
    total_a, total_b = keep_a[...], keep_b[...]
    for a, b in zip(early, late):
        power = b[rows_b:, :].astype(I32).astype(F32)
        total_a += restore(a[...], power)
        total_b += restore(b[:rows_b, :], power[cut:, :])
    return jnp.concatenate([total_a, total_b])


def sum_kernel(*rest):
    rest[-1][...] = sum_of(rest[:-1])


def code_kernel(scale, x, out):
    encode(x[...] * scale, out, 0)


def sum_code_kernel(scale, *rest):
    encode(sum_of(rest[:-1]) * scale, rest[-1], 0)


def unpack(src, which, side, z, packed):
    plane = packed.shape[0] // 2
    for t in range(4):
        value = decode(src[t])
        used = 0
        for first, n in ((which * (plane // 18) * 5, plane // 18 * 5), (plane // 18 * (10 + which * 4), plane // 18 * 4)):
            piece = n // 4
            row = side * plane + first + (z ^ t) * piece
            packed[pl.ds(pl.multiple_of(row, 16), piece), :] = value[used:used + piece, :]
            used += piece


def lay_corner(side, packed, square):
    aux = square.shape[0]
    half, quarter = aux // 2, aux // 4
    at = (side + 1) * (packed.shape[0] // 2) - half // LANES * quarter
    first = side * quarter
    for c in range(half, aux, LANES):
        square[first:first + quarter, c:c + LANES] = packed[at:at + quarter, :]
        for r in range(0, quarter, LANES):
            square[c:c + LANES, first + r:first + r + LANES] = packed[at + r:at + r + LANES, :].T
        at += quarter


def lay_triangle(side, packed, square, after=None):
    aux = square.shape[0]
    half, quarter = aux // 2, aux // 4
    at = (side + 1) * (packed.shape[0] // 2) - half // LANES * quarter
    base = side * half
    for c in range(half - LANES, -1, -LANES):
        at -= c + LANES
        columns = slice(base + c, base + c + LANES)
        square[base:base + c + LANES, columns] = packed[at:at + c + LANES, :]
        for r in range(0, c, LANES):
            square[columns, base + r:base + r + LANES] = packed[at + r:at + r + LANES, :].T
        if after is not None:
            after(base + c)


def write_plane(side, packed, square, out, sem):
    aux = square.shape[0]
    half, quarter = aux // 2, aux // 4
    first, base = side * quarter, side * half

    def copy(at, row, rows, column, columns):
        where = (pl.ds(row, rows), pl.ds(column, columns))
        started = pltpu.make_async_copy(square.at[where], out.at[where], sem.at[at])
        started.start()
        return started

    lay_corner(side, packed, square)
    copies = [copy(0, first, quarter, half, half), copy(1, half, half, first, quarter)]
    lay_triangle(
        side, packed, square, lambda row: copies.append(copy(2 + (row - base) // LANES, row, LANES, base, half))
    )
    finish(copies)


def unpack_kernel(me_ref, a, b, sib_a, out, packed, sem, square):
    parity, core, z = place_of(me_ref[0])
    for src, which, side in ((a, core, parity), (b, core, 1 - parity), (sib_a, 1 - core, parity)):
        unpack(src, which, side, z, packed)
    for side in range(2):
        pl.when(parity == side)(functools.partial(write_plane, side, packed, square, out, sem))


def spread_kernel(me_ref, out_in, packed_in, sib_b, out, packed, sem, square):
    parity, core, z = place_of(me_ref[0])
    unpack(sib_b, 1 - core, 1 - parity, z, packed)
    for side in range(2):
        pl.when(parity != side)(functools.partial(write_plane, side, packed, square, out, sem))


def shards(slabs, pair_blocks, occ_energy, virt_energy, domain_map):
    blocks = lax.axis_size("dom")
    me = lax.axis_index("dom").astype(I32)[None]
    own = slabs[0]
    orbitals, aux, virt = own.shape
    wide = orbitals * virt
    upper = aux * (aux + LANES) // 2 // LANES
    piece = upper // 16

    hbm = pl.BlockSpec(memory_space=pl.ANY)
    vmem = pl.BlockSpec(memory_space=pltpu.VMEM)
    smem = pl.BlockSpec(memory_space=pltpu.SMEM)
    slab_s = pltpu.VMEM((aux, wide), BF16)
    amp_s = pltpu.VMEM((wide, wide), BF16)
    total_t = jax.ShapeDtypeStruct((aux, wide), F32)

    def kernel(body, name, ins, outs, out_specs, scratch=(), limit=SMALL_LIMIT, aliases={}, flops=1):
        return pl.pallas_call(
            body,
            out_shape=outs,
            in_specs=ins,
            out_specs=out_specs,
            scratch_shapes=scratch,
            compiler_params=pltpu.CompilerParams(vmem_limit_bytes=limit),
            cost_estimate=pl.CostEstimate(flops=flops, bytes_accessed=1, transcendentals=0),
            input_output_aliases=aliases,
            name=name,
        )

    def dma(n):
        return pltpu.SemaphoreType.DMA((n,))

    def coded(n):
        return jax.ShapeDtypeStruct((n, LANES), I16)

    def plain(n):
        return jax.ShapeDtypeStruct((n, LANES), F32)

    flat = own.reshape(orbitals * aux, virt)
    cuts = [sum(PARTS[:i]) for i in range(len(PARTS) + 1)]
    count, early = len(PARTS), len(PARTS) - 2
    part = flat[:PARTS[0]]
    y = [swapped(part, 2)]
    sib_pairs = swapped(pair_blocks, 1)
    gives_y = ((me[0] >> 1) ^ me[0]) & 1 == 0
    later, part, gives_y = lax.optimization_barrier((flat, part, gives_y))
    sib = swapped(later, 1)
    parts = [None, *kernel(
        functools.partial(split_kernel, cuts[1:-1]), "split", [smem, smem, hbm],
        [jax.ShapeDtypeStruct((n + (0 if i else PAD), virt), BF16) for i, n in enumerate(PARTS[1:])],
        [vmem] * (count - 1), [dma(count - 1)],
    )(me, pair_blocks, later)]

    small = jax.ShapeDtypeStruct((8, wide), F32)
    energy = virt_energy.reshape(-1, LANES)
    levels, weights = kernel(
        functools.partial(prep_kernel, blocks), "prep", [smem] * 3 + [hbm] * 3, (small, small), (vmem, vmem),
        [dma(3), pltpu.VMEM((orbitals, blocks), F32), pltpu.VMEM(energy.shape, F32), pltpu.VMEM(domain_map.shape, I32)],
    )(me, pair_blocks, sib_pairs, occ_energy.T, energy, domain_map)
    sib, near_own = lax.optimization_barrier((sib, flat))
    own_t, own_s, total = kernel(
        own_kernel, "own", [hbm, vmem, vmem],
        (jax.ShapeDtypeStruct((wide, aux), BF16), jax.ShapeDtypeStruct((aux, wide), BF16), total_t), (vmem,) * 3,
        [dma(2), amp_s], LARGE_LIMIT, flops=int(2e10),
    )(near_own, levels, weights)
    sib, part = lax.optimization_barrier((sib, parts[1]))
    y.append(swapped(part, 2))
    y[0], total, own_t, sib, part = lax.optimization_barrier((y[0], total, own_t, sib, parts[2]))
    y.append(swapped(part, 2))
    z = [forwarded(y[0])]
    total = kernel(
        sib_kernel, "sib", [vmem, vmem, hbm, vmem, vmem], total_t, vmem, [dma(2), slab_s, amp_s], LARGE_LIMIT, {1: 0},
        int(1e10),
    )(own_t, total, sib, levels, weights)
    y[1], total, part = lax.optimization_barrier((y[1], total, parts[3]))
    y.append(swapped(part, 2))
    z.append(forwarded(y[1]))
    for i in range(4, count):
        y[i - 2], part, _ = lax.optimization_barrier((y[i - 2], parts[i], y[i - 3]))
        y.append(swapped(part, 2))
        z.append(forwarded(y[i - 2]))
    y[-3], near = lax.optimization_barrier((y[-3], total))
    keep, away, *sends = kernel(
        near_metric_kernel, "near_metric", [smem, vmem, vmem], (plain(upper // 4),) * 2 + (coded(4 * (piece + PAD)),) * 2,
        (vmem,) * 4, [slab_s, slab_s, pltpu.VMEM((upper, LANES), F32)], LARGE_LIMIT, flops=int(1e10),
    )(me, near, own_s)
    y[-2], z[0], keep = lax.optimization_barrier((y[-2], z[0], keep))
    z.append(forwarded(y[-2]))
    got = [swapped(send, 1) for send in sends]
    y[-1], *got = lax.optimization_barrier((y[-1], *got))
    z.append(forwarded(y[-1]))
    y[-1], keep, away = lax.optimization_barrier((y[-1], keep, away))
    keep, send = kernel(
        chip_kernel, "chip", [vmem] * 4, (plain(upper // 4), coded(4 * (piece + PAD))), (vmem, vmem),
    )(keep, away, *got)
    across = swapped(send, 2)
    (y[-1], own_t, keep), z[early:-1] = lax.optimization_barrier(((y[-1], own_t, keep), z[early:-1]))

    def given(rows_y, rows_z):
        return swapped(jnp.where(gives_y, jnp.concatenate(rows_y), jnp.concatenate(rows_z)), 1)

    arrays = {f"y{i}": part for i, part in enumerate(y)}
    arrays |= {f"z{i}": part for i, part in enumerate(z)}
    arrays["x0"] = given(y[:early], z[:early])

    def half_of(which, j):
        name = "y" if which == Y else "z"
        rows = []
        for i, (a, b) in enumerate(zip(cuts, cuts[1:])):
            first, last = max(a, j * aux), min(b, (j + 1) * aux)
            if first >= last:
                continue
            to = first - j * aux
            if which != X:
                rows.append((f"{name}{i}", first - a, last - first, to))
            elif i < early:
                rows.append(("x0", first + (PAD if i > 1 else 0), last - first, to))
            elif i == early:
                n = (b - a) // 2
                rows += [("x1", 0, n, to), ("x2", 0, b - a - n, to + n)]
            else:
                rows.append(("x3", 0, b - a, to))
        return rows, ("x0", cuts[2]) if which == X else (f"{name}1", PARTS[1])

    def pair_step(body, name, step, before=(), outs=(), out_specs=(), scratch=(), flops=1, side=None):
        plan = [half_of(*half) for half in STEPS[step]]
        used = plan if side is None else [plan[side]]
        names = list(dict.fromkeys(n for rows, (at, _) in used for n in [r[0] for r in rows] + [at]))
        return kernel(
            functools.partial(body, plan, names, step), name,
            [smem] + [vmem] * (3 + len(before) + len(names)),
            (total_t, *outs), (vmem, *out_specs), scratch, LARGE_LIMIT, {4: 0} if before else {}, flops,
        )(me, own_t, levels, weights, *before, *[arrays[n] for n in names])

    (total,) = pair_step(first_far_kernel, "far2", 2, scratch=[slab_s, amp_s], flops=int(1e10))
    (total,) = pair_step(far_kernel, "far3", 3, (total,), scratch=[slab_s, amp_s], flops=1)
    total, *late = lax.optimization_barrier((total, y[-2], z[-2]))
    late = jnp.where(gives_y, *late)
    middle = late.shape[0] // 2
    arrays["x1"], arrays["x2"] = swapped(late[:middle], 1), swapped(late[middle:], 1)
    z[-1], total, arrays["x1"], arrays["x2"], across = lax.optimization_barrier(
        (z[-1], total, arrays["x1"], arrays["x2"], across)
    )
    arrays[f"z{count - 1}"] = z[-1]
    arrays["x3"] = given(y[-1:], z[-1:])
    half_s = [pltpu.VMEM((aux, virt), BF16), pltpu.VMEM((wide, virt), BF16)]
    (total,) = pair_step(
        lambda *a: half_kernel(*a[:3], 0, *a[3:]), "half", 4, (total,), scratch=half_s, flops=int(1e9), side=0
    )
    plane = upper // 2
    (_, square), (_, corner) = segments(plane, 0)
    slab_t = jax.ShapeDtypeStruct((aux, wide), BF16)
    _, residual, mine, send, high, low = pair_step(
        last_kernel, "last", 4, (total, own_s, near),
        (jax.ShapeDtypeStruct(own.shape, F32), plain(square), plain(square), slab_t, slab_t), (hbm,) + (vmem,) * 4,
        [dma(2), *half_s, pltpu.VMEM((2 * square, LANES), F32)], side=1,
    )

    def column(first, size, mine, got, *given):
        n = size // 4
        apart = () if given else (jax.ShapeDtypeStruct((3, PAD, LANES), F32),)
        outs = (plain(n),) + (coded(n + (PAD if given else 0)),) * 3 + apart
        return kernel(
            functools.partial(column_kernel, first), "column", [smem] + [vmem] * (4 + len(given)), outs,
            (vmem,) * len(outs),
        )(me, mine, got, keep, across, *given)

    got = swapped(send, 1)
    mine_b, send_b = kernel(
        corner_kernel, "corner", [smem] + [vmem] * 3, (plain(corner), plain(corner)), (vmem, vmem),
        [pltpu.VMEM((2 * corner, LANES), F32)], LARGE_LIMIT, flops=int(2e9),
    )(me, high, low, own_s)
    got, send_b = lax.optimization_barrier((got, send_b))
    got_b = swapped(send_b, 1)
    keep_a, *sends_a, apart = column(0, square, mine, got)
    summed = [keep_a] + [swapped(sends_a[t - 1], 4 * t) for t in (3, 2, 1)]
    keep_b, *sends_b = column(square, corner, mine_b, got_b, apart)
    summed += [keep_b] + [swapped(sends_b[t - 1], 4 * t) for t in (3, 2, 1)]
    if blocks == 16:
        mine = kernel(
            functools.partial(sum_code_kernel, 1.0 / blocks), "sum_code", [vmem] * 8, coded(piece + PAD), vmem,
        )(*summed)
    else:
        value = kernel(sum_kernel, "sum", [vmem] * 8, plain(piece), vmem)(*summed)
        bit = 16
        while bit < blocks:
            value = value + swapped(value, bit)
            bit *= 2
        mine = kernel(functools.partial(code_kernel, 1.0 / blocks), "code", [vmem], coded(piece + PAD), vmem)(value)

    column = [mine] + [swapped(mine, 4 * t) for t in (1, 2, 3)]
    across = [swapped(c, 2) for c in column]
    a, b = jnp.stack(column), jnp.stack(across)
    sib_a, sib_b = swapped(a, 1), swapped(b, 1)
    whole = jax.ShapeDtypeStruct((aux, aux), F32)
    scratch = [dma(2 + aux // 2 // LANES), pltpu.VMEM((aux, aux), F32)]
    gradient, packed = kernel(
        unpack_kernel, "unpack", [smem] + [vmem] * 3, (whole, plain(upper)), (hbm, vmem), scratch, flops=int(1e9),
    )(me, a, b, sib_a)
    gradient, _ = kernel(
        spread_kernel, "spread", [smem, hbm, vmem, vmem], (whole, plain(upper)), (hbm, vmem), scratch,
        aliases={1: 0, 2: 1},
    )(me, gradient, packed, sib_b)
    return residual[None], gradient


def solution(mesh):
    return jax.shard_map(
        shards,
        mesh=mesh,
        in_specs=(
            P(("grp", "dom"), None, None, None),
            P(("grp", "dom"), None),
            P("grp", None),
            P("grp"),
            P("grp", None),
        ),
        out_specs=(P(("grp", "dom"), None, None, None), P("grp", None)),
        check_vma=False,
    )
```

```python
import functools

import jax
import jax.numpy as jnp
from jax import lax
from jax.experimental import pallas as pl
from jax.experimental.pallas import tpu as pltpu
from jax.sharding import PartitionSpec as P

LARGE_LIMIT = 16 * 1024 * 1024
SMALL_LIMIT = 8 * 1024 * 1024
LANES = 128
BLOCK = 256
PAD = 16
PARTS = (416, 368, 432, 416, 416)
GROUP = 32
BITS = 14
NT = (((1,), (1,)), ((), ()))
TN = (((0,), (0,)), ((), ()))
F32, BF16, I16, I32 = jnp.float32, jnp.bfloat16, jnp.int16, jnp.int32


def move(x, pairs):
    return lax.ppermute(x, "dom", pairs)


def swapped(x, bits):
    return move(x, [(d, d ^ bits) for d in range(lax.axis_size("dom"))])


def forwarded(x):
    devices = range(lax.axis_size("dom"))
    route = [(d, d - 4 if d & 2 else d + 4) for d in devices]
    return move(x, [(a, b) for a, b in route if b in devices])


def begin(copies, sem, at=0):
    started = [pltpu.make_async_copy(a, b, sem.at[at + i]) for i, (a, b) in enumerate(copies)]
    for copy in started:
        copy.start()
    return started


def finish(copies):
    for copy in copies:
        copy.wait()


def place_of(me):
    return (me >> 1) & 1, me & 1, (me >> 2) & 3


def offsets_of(me):
    parity, core, _ = place_of(me)
    return 0, 1 - 2 * core, 2 - 4 * parity, 4 * parity - 2, 2 * core - 1


OWN, SIB, Y, Z, X = range(5)
STEPS = (((OWN, 0), (OWN, 1)), ((SIB, 0), (SIB, 1)), ((Y, 0), (Y, 1)), ((Z, 0), (X, 0)), ((Z, 1), (X, 1)))


def prep_kernel(blocks, me_ref, pairs, sib_pairs, occ_in, energy_in, maps_in, levels, weights, sem, occ, energy, maps):
    copies = begin([(occ_in, occ), (energy_in, energy), (maps_in, maps)], sem)
    me = me_ref[0]
    virt = maps.shape[1]
    finish(copies)
    table = energy[...]
    parts = []
    for _ in range(3):
        part = table.astype(BF16)
        parts.append(part)
        table = table - part.astype(F32)
    block_major = lax.broadcasted_iota(I32, occ.shape, 1)
    row_major = lax.broadcasted_iota(I32, (energy.shape[0], virt), 0)
    lane_major = lax.broadcasted_iota(I32, (LANES, virt), 0)
    for block, offset in enumerate(offsets_of(me)):
        other = me + offset
        who = jnp.clip(other, 0, blocks - 1)
        count = 0
        for s in range(pairs.shape[1]):
            count = count + (pairs[0, s] == other).astype(I32)
            if block in (OWN, SIB):
                count = count + ((pairs, sib_pairs)[block][0, s] == me).astype(I32)
        occupied = jnp.sum(jnp.where(block_major == who, occ[...], 0.0), axis=1, keepdims=True)
        index = maps[pl.ds(who, 1), :]
        pick = (row_major == index // LANES).astype(F32).astype(BF16)
        rows = sum(lax.dot_general(p, pick, TN, preferred_element_type=F32) for p in parts)
        chosen = jnp.sum(jnp.where(lane_major == index % LANES, rows, 0.0), axis=0, keepdims=True)
        for step, halves in enumerate(STEPS):
            for side, (which, j) in enumerate(halves):
                if which == block:
                    at = pl.ds(side * virt, virt)
                    levels[step:step + 1, at] = chosen - occupied[j:j + 1, :]
                    weights[step:step + 1, at] = jnp.full((1, virt), -count.astype(F32), F32)


def add_pair(own_t, other, amp, total, own_level, level, weight, first, halves=None, near=None):
    wide = own_t.shape[0]
    for t in range(0, wide, BLOCK):
        s = pl.ds(t, BLOCK)
        integrals = jnp.dot(own_t[s, :], other[...], preferred_element_type=F32)
        amp[s, :] = (integrals * weight / (own_level[t:t + BLOCK, 0:1] + level)).astype(BF16)
    for t in range(0, wide, BLOCK):
        s = pl.ds(t, BLOCK)
        part = lax.dot_general(other[...], amp[s, :], NT, preferred_element_type=F32)
        value = part if first else total[:, s] + part
        total[:, s] = value if near is None else value + near[:, s]
        if halves is not None:
            high = value.astype(BF16)
            halves[0][:, s] = high
            halves[1][:, s] = (value - high.astype(F32)).astype(BF16)


def split_kernel(cuts, me_ref, pairs, own, *rest):
    parts, sem = rest[:-1], rest[-1]
    copies = begin(
        [(own.at[pl.ds(a, b)], part.at[pl.ds(0, b)]) for a, b, part in zip(cuts, PARTS[1:], parts)], sem
    )
    rows, virt = parts[0].shape[0] - PAD, parts[0].shape[1]
    lane = lax.broadcasted_iota(I32, (PAD, virt), 1)
    listed = jnp.full((PAD, virt), 100, I32)
    for s in range(pairs.shape[1]):
        listed = jnp.where(lane == s, pairs[0, s] - me_ref[0], listed)
    parts[0][rows:, :] = listed.astype(F32).astype(BF16)
    finish(copies)


def own_kernel(own, levels, weights, own_t, own_s, total, sem, amp):
    aux, virt = own.shape[0] // 2, own.shape[1]
    copies = begin([(own.at[pl.ds(j * aux, aux)], own_s.at[:, pl.ds(j * virt, virt)]) for j in range(2)], sem)
    level = levels[...].T
    finish(copies)
    own_t[...] = own_s[...].T
    add_pair(own_t, own_s, amp, total, level, levels[0:1, :], weights[0:1, :], True)


def sib_kernel(own_t, total_in, sib, levels, weights, total, sem, other, amp):
    aux, virt = sib.shape[0] // 2, sib.shape[1]
    copies = begin([(sib.at[pl.ds(j * aux, aux)], other.at[:, pl.ds(j * virt, virt)]) for j in range(2)], sem)
    level = levels[...].T
    finish(copies)
    add_pair(own_t, other, amp, total, level, levels[1:2, :], weights[1:2, :], False)


def fetch(plan, step, me, refs, other, skip=0):
    counts = []
    for side, (rows, (name, at)) in enumerate(plan):
        virt = other.shape[1] // len(plan)
        for source, first, n, to in rows:
            other[to:to + n, side * virt:(side + 1) * virt] = refs[source][first:first + n, :]
        wanted = -offsets_of(me)[STEPS[step][side + skip][0]]
        hits = jnp.where(refs[name][at:at + PAD, :].astype(F32)[0:1, :] == wanted.astype(F32), 1.0, 0.0)
        counts.append(jnp.broadcast_to(jnp.sum(hits, axis=1, keepdims=True), (1, virt)))
    return jnp.concatenate(counts, axis=1) if len(counts) > 1 else counts[0]


def first_far_kernel(plan, names, step, me_ref, own_t, levels, weights, *rest):
    refs = dict(zip(names, rest))
    total, other, amp = rest[len(names):]
    weight = weights[step:step + 1, :] - fetch(plan, step, me_ref[0], refs, other)
    add_pair(own_t, other, amp, total, levels[...].T, levels[step:step + 1, :], weight, True)


def far_kernel(plan, names, step, me_ref, own_t, levels, weights, total_in, *rest):
    refs = dict(zip(names, rest))
    total, other, amp = rest[len(names):]
    weight = weights[step:step + 1, :] - fetch(plan, step, me_ref[0], refs, other)
    add_pair(own_t, other, amp, total, levels[...].T, levels[step:step + 1, :], weight, False)


def segments(plane, which):
    side = plane // 18
    return (which * side * 5, side * 5), (side * 10 + which * side * 4, side * 4)


def rows_of(packed, base, plane, which):
    return jnp.concatenate(
        [packed[pl.ds(pl.multiple_of(base + a, 16), n), :] for a, n in segments(plane, which)]
    )


def near_metric_kernel(me_ref, total, own_s, keep, away, *rest):
    *sends, high, low, packed = rest
    parity, core, _ = place_of(me_ref[0])
    high[...] = total[...].astype(BF16)
    low[...] = (total[...] - high[...].astype(F32)).astype(BF16)
    aux = total.shape[0]
    half, quarter = aux // 2, aux // 4
    plane = packed.shape[0] // 2
    square = plane - half // LANES * quarter
    for q in range(0, aux, BLOCK):
        rows = q + BLOCK
        slab = own_s[q:q + BLOCK, :]
        block = lax.dot_general(high[:rows, :], slab, NT, preferred_element_type=F32)
        block += lax.dot_general(low[:rows, :], slab, NT, preferred_element_type=F32)
        for c in range(q, q + BLOCK, LANES):
            column = block[:, c - q:c - q + LANES]
            base, side = (half, 1) if c >= half else (0, 0)
            k = (c - base) // LANES
            at = side * plane + k * (k + 1) // 2 * LANES
            packed[at:at + (k + 1) * LANES, :] = column[base:c + LANES, :]
            if side:
                for s in range(2):
                    at = s * plane + square + k * quarter
                    packed[at:at + quarter, :] = column[s * quarter:(s + 1) * quarter, :]
    size = plane // 2

    def part(side, which):
        return rows_of(packed, side * plane, plane, which)

    keep[...] = part(parity, core)
    away[...] = part(1 - parity, core)
    given = [part(1 - parity, 1 - core), part(parity, 1 - core)]
    piece = size // 4
    for send, x in zip(sends, given):
        for t in range(4):
            encode(x[t * piece:(t + 1) * piece, :], send, t * (piece + PAD))


def half_kernel(plan, names, step, side, me_ref, own_t, levels, weights, total_in, *rest):
    refs = dict(zip(names, rest))
    total, other, amp = rest[len(names):]
    add_half(plan, refs, step, side, me_ref[0], own_t, levels, weights, total, other, amp)


def add_half(plan, refs, step, side, me, own_t, levels, weights, total, other, amp, halves=None, near=None):
    virt = other.shape[1]
    columns = slice(side * virt, (side + 1) * virt)
    count = fetch([plan[side]], step, me, refs, other, side)
    weight = weights[step:step + 1, columns] - count
    level = levels[step:step + 1, columns]
    add_pair(own_t, other, amp, total, levels[...].T, level, weight, False, halves, near)


def mirrored(high, low, own_s, first, n, q):
    rows, columns = pl.ds(pl.multiple_of(first, 16), n), pl.ds(pl.multiple_of(q, 16), BLOCK)
    pairs = ((high, own_s), (low, own_s), (own_s, high), (own_s, low))
    return sum(lax.dot_general(a[rows, :], b[columns, :], NT, preferred_element_type=F32) for a, b in pairs)


def last_kernel(plan, names, step, me_ref, own_t, levels, weights, total_in, own_s, near, *rest):
    refs = dict(zip(names, rest))
    total, residual, keep, send, high, low, sem, other, amp, packed = rest[len(names):]
    me = me_ref[0]
    parity, core, _ = place_of(me)
    aux, wide = total.shape
    virt = wide // 2
    add_half(plan, refs, step, 1, me, own_t, levels, weights, total, other, amp, (high, low), near)
    copies = begin([(total.at[:, pl.ds(j * virt, virt)], residual.at[j]) for j in range(2)], sem)
    half = aux // 2

    def both(first, n, q):
        return mirrored(high, low, own_s, first, n, q)

    at = 0
    for q in range(0, half, BLOCK):
        block = both(parity * half, q + BLOCK, parity * half + q)
        for c in range(0, BLOCK, LANES):
            upper = q + c + LANES
            packed[at:at + upper, :] = block[:upper, c:c + LANES]
            at += upper
    share(packed, core, keep, send)
    finish(copies)


def share(packed, core, keep, send):
    size = keep.shape[0]
    keep[...] = packed[pl.ds(pl.multiple_of(core * size, 16), size), :]
    send[...] = packed[pl.ds(pl.multiple_of((1 - core) * size, 16), size), :]


def corner_kernel(me_ref, high, low, own_s, keep, send, packed):
    parity, core, _ = place_of(me_ref[0])
    aux = own_s.shape[0]
    half, quarter = aux // 2, aux // 4
    at = 0
    for q in range(half, aux, BLOCK):
        block = mirrored(high, low, own_s, parity * quarter, quarter, q)
        for c in range(0, BLOCK, LANES):
            packed[at:at + quarter, :] = block[:, c:c + LANES]
            at += quarter
    share(packed, core, keep, send)


def powers(exponent):
    first = jnp.clip(exponent, -100.0, 100.0)
    return jnp.exp2(first), jnp.exp2(exponent - first)


def encode(x, out, row):
    rows = x.shape[0]
    groups = x.reshape(rows // GROUP, GROUP, LANES)
    largest = jnp.max(jnp.abs(groups), axis=1)
    power = jnp.floor(jnp.log2(jnp.maximum(largest, 1e-37))) + 1.0
    a, b = powers(BITS - power)
    for g in range(rows // GROUP):
        whole = jnp.round(groups[g] * a[g:g + 1, :] * b[g:g + 1, :]).astype(I32)
        out[pl.ds(row + g * GROUP, GROUP), :] = whole.astype(I16)
    pad = jnp.zeros((PAD - rows // GROUP, LANES), F32)
    out[pl.ds(row + rows, PAD), :] = jnp.concatenate([power, pad]).astype(I32).astype(I16)


def decode(coded):
    rows = coded.shape[0] - PAD
    wide = coded.astype(I32).astype(F32)
    a, b = powers(wide[rows:] - BITS)
    return jnp.concatenate(
        [wide[g * GROUP:(g + 1) * GROUP] * a[g:g + 1, :] * b[g:g + 1, :] for g in range(rows // GROUP)]
    )


def chip_kernel(keep_in, away, got_away, got_keep, keep, send):
    piece = keep.shape[0] // 4
    for t in range(4):
        at, coded = pl.ds(t * piece, piece), pl.ds(t * (piece + PAD), piece + PAD)
        encode(away[at, :] + decode(got_away[coded, :]), send, t * (piece + PAD))
        keep[at, :] = keep_in[at, :] + decode(got_keep[coded, :])


def column_kernel(first, me_ref, mine, theirs, near, across, keep, *sends):
    _, _, z = place_of(me_ref[0])
    piece = keep.shape[0]
    away = across.shape[0] // 4
    far = jnp.concatenate([decode(across[i * away:(i + 1) * away, :]) for i in range(4)])
    for i in range(4):
        at = slice(i * piece, (i + 1) * piece)
        inner = slice(first + i * piece, first + (i + 1) * piece)
        value = (mine[at, :] + theirs[at, :]) + (near[inner, :] + far[inner, :])

        @pl.when(z == i)
        def _():
            keep[...] = value

        for t in (1, 2, 3):
            pl.when((z ^ t) == i)(functools.partial(encode, value, sends[t - 1], 0))


def sum_of(parts):
    return jnp.concatenate([sum((decode(x[...]) for x in others), mine[...]) for mine, *others in (parts[:4], parts[4:])])


def sum_kernel(*rest):
    rest[-1][...] = sum_of(rest[:-1])


def code_kernel(scale, x, out):
    encode(x[...] * scale, out, 0)


def sum_code_kernel(scale, *rest):
    encode(sum_of(rest[:-1]) * scale, rest[-1], 0)


def unpack(src, which, side, z, packed):
    plane = packed.shape[0] // 2
    for t in range(4):
        value = decode(src[3 - t])
        used = 0
        for first, n in ((which * (plane // 18) * 5, plane // 18 * 5), (plane // 18 * (10 + which * 4), plane // 18 * 4)):
            piece = n // 4
            row = side * plane + first + (z ^ t) * piece
            packed[pl.ds(pl.multiple_of(row, 16), piece), :] = value[used:used + piece, :]
            used += piece


def lay_corner(side, packed, square):
    aux = square.shape[0]
    half, quarter = aux // 2, aux // 4
    at = (side + 1) * (packed.shape[0] // 2) - half // LANES * quarter
    first = side * quarter
    for c in range(half, aux, LANES):
        square[first:first + quarter, c:c + LANES] = packed[at:at + quarter, :]
        for r in range(0, quarter, LANES):
            square[c:c + LANES, first + r:first + r + LANES] = packed[at + r:at + r + LANES, :].T
        at += quarter


def lay_triangle(side, packed, square, after=None):
    aux = square.shape[0]
    half, quarter = aux // 2, aux // 4
    at = (side + 1) * (packed.shape[0] // 2) - half // LANES * quarter
    base = side * half
    for c in range(half - LANES, -1, -LANES):
        at -= c + LANES
        columns = slice(base + c, base + c + LANES)
        square[base:base + c + LANES, columns] = packed[at:at + c + LANES, :]
        for r in range(0, c, LANES):
            square[columns, base + r:base + r + LANES] = packed[at + r:at + r + LANES, :].T
        if after is not None:
            after(base + c)


def write_plane(side, packed, square, out, sem):
    aux = square.shape[0]
    half, quarter = aux // 2, aux // 4
    first, base = side * quarter, side * half

    def copy(at, row, rows, column, columns):
        where = (pl.ds(row, rows), pl.ds(column, columns))
        started = pltpu.make_async_copy(square.at[where], out.at[where], sem.at[at])
        started.start()
        return started

    lay_corner(side, packed, square)
    copies = [copy(0, first, quarter, half, half), copy(1, half, half, first, quarter)]
    lay_triangle(
        side, packed, square, lambda row: copies.append(copy(2 + (row - base) // LANES, row, LANES, base, half))
    )
    finish(copies)


def unpack_kernel(me_ref, a, b, sib_a, out, packed, sem, square):
    parity, core, z = place_of(me_ref[0])
    for src, which, side in ((a, core, parity), (b, core, 1 - parity), (sib_a, 1 - core, parity)):
        unpack(src, which, side, z, packed)
    for side in range(2):
        pl.when(parity == side)(functools.partial(write_plane, side, packed, square, out, sem))


def spread_kernel(me_ref, out_in, packed_in, sib_b, out, packed, sem, square):
    parity, core, z = place_of(me_ref[0])
    unpack(sib_b, 1 - core, 1 - parity, z, packed)
    for side in range(2):
        pl.when(parity != side)(functools.partial(write_plane, side, packed, square, out, sem))


def shards(slabs, pair_blocks, occ_energy, virt_energy, domain_map):
    blocks = lax.axis_size("dom")
    me = lax.axis_index("dom").astype(I32)[None]
    own = slabs[0]
    orbitals, aux, virt = own.shape
    wide = orbitals * virt
    upper = aux * (aux + LANES) // 2 // LANES
    piece = upper // 16

    hbm = pl.BlockSpec(memory_space=pl.ANY)
    vmem = pl.BlockSpec(memory_space=pltpu.VMEM)
    smem = pl.BlockSpec(memory_space=pltpu.SMEM)
    slab_s = pltpu.VMEM((aux, wide), BF16)
    amp_s = pltpu.VMEM((wide, wide), BF16)
    total_t = jax.ShapeDtypeStruct((aux, wide), F32)

    def kernel(body, name, ins, outs, out_specs, scratch=(), limit=SMALL_LIMIT, aliases={}, flops=1):
        return pl.pallas_call(
            body,
            out_shape=outs,
            in_specs=ins,
            out_specs=out_specs,
            scratch_shapes=scratch,
            compiler_params=pltpu.CompilerParams(vmem_limit_bytes=limit),
            cost_estimate=pl.CostEstimate(flops=flops, bytes_accessed=1, transcendentals=0),
            input_output_aliases=aliases,
            name=name,
        )

    def dma(n):
        return pltpu.SemaphoreType.DMA((n,))

    def coded(n):
        return jax.ShapeDtypeStruct((n, LANES), I16)

    def plain(n):
        return jax.ShapeDtypeStruct((n, LANES), F32)

    flat = own.reshape(orbitals * aux, virt)
    cuts = [sum(PARTS[:i]) for i in range(len(PARTS) + 1)]
    count, early = len(PARTS), len(PARTS) - 2
    part = flat[:PARTS[0]]
    y = [swapped(part, 2)]
    sib_pairs = swapped(pair_blocks, 1)
    gives_y = ((me[0] >> 1) ^ me[0]) & 1 == 0
    later, part, gives_y = lax.optimization_barrier((flat, part, gives_y))
    sib = swapped(later, 1)
    parts = [None, *kernel(
        functools.partial(split_kernel, cuts[1:-1]), "split", [smem, smem, hbm],
        [jax.ShapeDtypeStruct((n + (0 if i else PAD), virt), BF16) for i, n in enumerate(PARTS[1:])],
        [vmem] * (count - 1), [dma(count - 1)],
    )(me, pair_blocks, later)]

    small = jax.ShapeDtypeStruct((8, wide), F32)
    energy = virt_energy.reshape(-1, LANES)
    levels, weights = kernel(
        functools.partial(prep_kernel, blocks), "prep", [smem] * 3 + [hbm] * 3, (small, small), (vmem, vmem),
        [dma(3), pltpu.VMEM((orbitals, blocks), F32), pltpu.VMEM(energy.shape, F32), pltpu.VMEM(domain_map.shape, I32)],
    )(me, pair_blocks, sib_pairs, occ_energy.T, energy, domain_map)
    sib, near_own = lax.optimization_barrier((sib, flat))
    own_t, own_s, total = kernel(
        own_kernel, "own", [hbm, vmem, vmem],
        (jax.ShapeDtypeStruct((wide, aux), BF16), jax.ShapeDtypeStruct((aux, wide), BF16), total_t), (vmem,) * 3,
        [dma(2), amp_s], LARGE_LIMIT, flops=int(2e10),
    )(near_own, levels, weights)
    sib, part = lax.optimization_barrier((sib, parts[1]))
    y.append(swapped(part, 2))
    y[0], total, own_t, sib, part = lax.optimization_barrier((y[0], total, own_t, sib, parts[2]))
    y.append(swapped(part, 2))
    z = [forwarded(y[0])]
    total = kernel(
        sib_kernel, "sib", [vmem, vmem, hbm, vmem, vmem], total_t, vmem, [dma(2), slab_s, amp_s], LARGE_LIMIT, {1: 0},
        int(1e10),
    )(own_t, total, sib, levels, weights)
    y[1], total, part = lax.optimization_barrier((y[1], total, parts[3]))
    y.append(swapped(part, 2))
    z.append(forwarded(y[1]))
    for i in range(4, count):
        y[i - 2], part, _ = lax.optimization_barrier((y[i - 2], parts[i], y[i - 3]))
        y.append(swapped(part, 2))
        z.append(forwarded(y[i - 2]))
    y[-3], near = lax.optimization_barrier((y[-3], total))
    keep, away, *sends = kernel(
        near_metric_kernel, "near_metric", [smem, vmem, vmem], (plain(upper // 4),) * 2 + (coded(4 * (piece + PAD)),) * 2,
        (vmem,) * 4, [slab_s, slab_s, pltpu.VMEM((upper, LANES), F32)], LARGE_LIMIT, flops=int(1e10),
    )(me, near, own_s)
    y[-2], z[0], keep = lax.optimization_barrier((y[-2], z[0], keep))
    z.append(forwarded(y[-2]))
    got = [swapped(send, 1) for send in sends]
    y[-1], *got = lax.optimization_barrier((y[-1], *got))
    z.append(forwarded(y[-1]))
    y[-1], keep, away = lax.optimization_barrier((y[-1], keep, away))
    keep, send = kernel(
        chip_kernel, "chip", [vmem] * 4, (plain(upper // 4), coded(4 * (piece + PAD))), (vmem, vmem),
    )(keep, away, *got)
    across = swapped(send, 2)
    (y[-1], own_t, keep), z[early:-1] = lax.optimization_barrier(((y[-1], own_t, keep), z[early:-1]))

    def given(rows_y, rows_z):
        return swapped(jnp.where(gives_y, jnp.concatenate(rows_y), jnp.concatenate(rows_z)), 1)

    arrays = {f"y{i}": part for i, part in enumerate(y)}
    arrays |= {f"z{i}": part for i, part in enumerate(z)}
    arrays["x0"] = given(y[:early], z[:early])

    def half_of(which, j):
        name = "y" if which == Y else "z"
        rows = []
        for i, (a, b) in enumerate(zip(cuts, cuts[1:])):
            first, last = max(a, j * aux), min(b, (j + 1) * aux)
            if first >= last:
                continue
            to = first - j * aux
            if which != X:
                rows.append((f"{name}{i}", first - a, last - first, to))
            elif i < early:
                rows.append(("x0", first + (PAD if i > 1 else 0), last - first, to))
            elif i == early:
                n = (b - a) // 2
                rows += [("x1", 0, n, to), ("x2", 0, b - a - n, to + n)]
            else:
                rows.append(("x3", 0, b - a, to))
        return rows, ("x0", cuts[2]) if which == X else (f"{name}1", PARTS[1])

    def pair_step(body, name, step, before=(), outs=(), out_specs=(), scratch=(), flops=1, side=None):
        plan = [half_of(*half) for half in STEPS[step]]
        used = plan if side is None else [plan[side]]
        names = list(dict.fromkeys(n for rows, (at, _) in used for n in [r[0] for r in rows] + [at]))
        return kernel(
            functools.partial(body, plan, names, step), name,
            [smem] + [vmem] * (3 + len(before) + len(names)),
            (total_t, *outs), (vmem, *out_specs), scratch, LARGE_LIMIT, {4: 0} if before else {}, flops,
        )(me, own_t, levels, weights, *before, *[arrays[n] for n in names])

    (total,) = pair_step(first_far_kernel, "far2", 2, scratch=[slab_s, amp_s], flops=int(1e10))
    (total,) = pair_step(far_kernel, "far3", 3, (total,), scratch=[slab_s, amp_s], flops=1)
    total, *late = lax.optimization_barrier((total, y[-2], z[-2]))
    late = jnp.where(gives_y, *late)
    middle = late.shape[0] // 2
    arrays["x1"], arrays["x2"] = swapped(late[:middle], 1), swapped(late[middle:], 1)
    z[-1], total, arrays["x1"], arrays["x2"], across = lax.optimization_barrier(
        (z[-1], total, arrays["x1"], arrays["x2"], across)
    )
    arrays[f"z{count - 1}"] = z[-1]
    arrays["x3"] = given(y[-1:], z[-1:])
    half_s = [pltpu.VMEM((aux, virt), BF16), pltpu.VMEM((wide, virt), BF16)]
    (total,) = pair_step(
        lambda *a: half_kernel(*a[:3], 0, *a[3:]), "half", 4, (total,), scratch=half_s, flops=int(1e9), side=0
    )
    plane = upper // 2
    (_, square), (_, corner) = segments(plane, 0)
    slab_t = jax.ShapeDtypeStruct((aux, wide), BF16)
    _, residual, mine, send, high, low = pair_step(
        last_kernel, "last", 4, (total, own_s, near),
        (jax.ShapeDtypeStruct(own.shape, F32), plain(square), plain(square), slab_t, slab_t), (hbm,) + (vmem,) * 4,
        [dma(2), *half_s, pltpu.VMEM((2 * square, LANES), F32)], side=1,
    )

    def column(first, size, mine, got):
        n = size // 4
        return kernel(
            functools.partial(column_kernel, first), "column", [smem] + [vmem] * 4, (plain(n),) + (coded(n + PAD),) * 3,
            (vmem,) * 4,
        )(me, mine, got, keep, across)

    got = swapped(send, 1)
    mine_b, send_b = kernel(
        corner_kernel, "corner", [smem] + [vmem] * 3, (plain(corner), plain(corner)), (vmem, vmem),
        [pltpu.VMEM((2 * corner, LANES), F32)], LARGE_LIMIT, flops=int(2e9),
    )(me, high, low, own_s)
    got, send_b = lax.optimization_barrier((got, send_b))
    got_b = swapped(send_b, 1)
    keep_a, *sends_a = column(0, square, mine, got)
    summed = [keep_a] + [swapped(sends_a[t - 1], 4 * t) for t in (3, 2, 1)]
    keep_b, *sends_b = column(square, corner, mine_b, got_b)
    summed += [keep_b] + [swapped(sends_b[t - 1], 4 * t) for t in (3, 2, 1)]
    if blocks == 16:
        mine = kernel(
            functools.partial(sum_code_kernel, 1.0 / blocks), "sum_code", [vmem] * 8, coded(piece + PAD), vmem,
        )(*summed)
    else:
        value = kernel(sum_kernel, "sum", [vmem] * 8, plain(piece), vmem)(*summed)
        bit = 16
        while bit < blocks:
            value = value + swapped(value, bit)
            bit *= 2
        mine = kernel(functools.partial(code_kernel, 1.0 / blocks), "code", [vmem], coded(piece + PAD), vmem)(value)

    column = [mine] + [swapped(mine, 4 * t) for t in (1, 2, 3)]
    across = [swapped(c, 2) for c in column]
    a, b = jnp.stack(column[::-1]), jnp.stack(across[::-1])
    sib_a, sib_b = swapped(a, 1), swapped(b, 1)
    whole = jax.ShapeDtypeStruct((aux, aux), F32)
    scratch = [dma(2 + aux // 2 // LANES), pltpu.VMEM((aux, aux), F32)]
    gradient, packed = kernel(
        unpack_kernel, "unpack", [smem] + [vmem] * 3, (whole, plain(upper)), (hbm, vmem), scratch, flops=int(1e9),
    )(me, a, b, sib_a)
    gradient, _ = kernel(
        spread_kernel, "spread", [smem, hbm, vmem, vmem], (whole, plain(upper)), (hbm, vmem), scratch,
        aliases={1: 0, 2: 1},
    )(me, gradient, packed, sib_b)
    return residual[None], gradient


def solution(mesh):
    return jax.shard_map(
        shards,
        mesh=mesh,
        in_specs=(
            P(("grp", "dom"), None, None, None),
            P(("grp", "dom"), None),
            P("grp", None),
            P("grp"),
            P("grp", None),
        ),
        out_specs=(P(("grp", "dom"), None, None, None), P("grp", None)),
        check_vma=False,
    )
```

```python
import functools

import jax
import jax.numpy as jnp
from jax import lax
from jax.experimental import pallas as pl
from jax.experimental.pallas import tpu as pltpu
from jax.sharding import PartitionSpec as P

LARGE_LIMIT = 16 * 1024 * 1024
SMALL_LIMIT = 8 * 1024 * 1024
LANES = 128
BLOCK = 256
PAD = 16
PARTS = (416, 368, 432, 416, 416)
GROUP = 32
BITS = 14
NT = (((1,), (1,)), ((), ()))
TN = (((0,), (0,)), ((), ()))
F32, BF16, I16, I32 = jnp.float32, jnp.bfloat16, jnp.int16, jnp.int32


def move(x, pairs):
    return lax.ppermute(x, "dom", pairs)


def swapped(x, bits):
    return move(x, [(d, d ^ bits) for d in range(lax.axis_size("dom"))])


def forwarded(x):
    devices = range(lax.axis_size("dom"))
    route = [(d, d - 4 if d & 2 else d + 4) for d in devices]
    return move(x, [(a, b) for a, b in route if b in devices])


def begin(copies, sem, at=0):
    started = [pltpu.make_async_copy(a, b, sem.at[at + i]) for i, (a, b) in enumerate(copies)]
    for copy in started:
        copy.start()
    return started


def finish(copies):
    for copy in copies:
        copy.wait()


def place_of(me):
    return (me >> 1) & 1, me & 1, (me >> 2) & 3


def offsets_of(me):
    parity, core, _ = place_of(me)
    return 0, 1 - 2 * core, 2 - 4 * parity, 4 * parity - 2, 2 * core - 1


OWN, SIB, Y, Z, X = range(5)
STEPS = (((OWN, 0), (OWN, 1)), ((SIB, 0), (SIB, 1)), ((Y, 0), (Y, 1)), ((Z, 0), (X, 0)), ((Z, 1), (X, 1)))


def prep_kernel(blocks, me_ref, pairs, sib_pairs, occ_in, energy_in, maps_in, levels, weights, sem, occ, energy, maps):
    copies = begin([(occ_in, occ), (energy_in, energy), (maps_in, maps)], sem)
    me = me_ref[0]
    virt = maps.shape[1]
    finish(copies)
    table = energy[...]
    parts = []
    for _ in range(3):
        part = table.astype(BF16)
        parts.append(part)
        table = table - part.astype(F32)
    block_major = lax.broadcasted_iota(I32, occ.shape, 1)
    row_major = lax.broadcasted_iota(I32, (energy.shape[0], virt), 0)
    lane_major = lax.broadcasted_iota(I32, (LANES, virt), 0)
    for block, offset in enumerate(offsets_of(me)):
        other = me + offset
        who = jnp.clip(other, 0, blocks - 1)
        count = 0
        for s in range(pairs.shape[1]):
            count = count + (pairs[0, s] == other).astype(I32)
            if block in (OWN, SIB):
                count = count + ((pairs, sib_pairs)[block][0, s] == me).astype(I32)
        occupied = jnp.sum(jnp.where(block_major == who, occ[...], 0.0), axis=1, keepdims=True)
        index = maps[pl.ds(who, 1), :]
        pick = (row_major == index // LANES).astype(F32).astype(BF16)
        rows = sum(lax.dot_general(p, pick, TN, preferred_element_type=F32) for p in parts)
        chosen = jnp.sum(jnp.where(lane_major == index % LANES, rows, 0.0), axis=0, keepdims=True)
        for step, halves in enumerate(STEPS):
            for side, (which, j) in enumerate(halves):
                if which == block:
                    at = pl.ds(side * virt, virt)
                    levels[step:step + 1, at] = chosen - occupied[j:j + 1, :]
                    weights[step:step + 1, at] = jnp.full((1, virt), -count.astype(F32), F32)


def add_pair(own_t, other, amp, total, own_level, level, weight, first, halves=None, near=None):
    wide = own_t.shape[0]
    for t in range(0, wide, BLOCK):
        s = pl.ds(t, BLOCK)
        integrals = jnp.dot(own_t[s, :], other[...], preferred_element_type=F32)
        amp[s, :] = (integrals * weight / (own_level[t:t + BLOCK, 0:1] + level)).astype(BF16)
    for t in range(0, wide, BLOCK):
        s = pl.ds(t, BLOCK)
        part = lax.dot_general(other[...], amp[s, :], NT, preferred_element_type=F32)
        value = part if first else total[:, s] + part
        total[:, s] = value if near is None else value + near[:, s]
        if halves is not None:
            high = value.astype(BF16)
            halves[0][:, s] = high
            halves[1][:, s] = (value - high.astype(F32)).astype(BF16)


def split_kernel(cuts, me_ref, pairs, own, *rest):
    parts, sem = rest[:-1], rest[-1]
    copies = begin(
        [(own.at[pl.ds(a, b)], part.at[pl.ds(0, b)]) for a, b, part in zip(cuts, PARTS[1:], parts)], sem
    )
    rows, virt = parts[0].shape[0] - PAD, parts[0].shape[1]
    lane = lax.broadcasted_iota(I32, (PAD, virt), 1)
    listed = jnp.full((PAD, virt), 100, I32)
    for s in range(pairs.shape[1]):
        listed = jnp.where(lane == s, pairs[0, s] - me_ref[0], listed)
    parts[0][rows:, :] = listed.astype(F32).astype(BF16)
    finish(copies)


def own_kernel(own, levels, weights, own_t, own_s, total, sem, amp):
    aux, virt = own.shape[0] // 2, own.shape[1]
    copies = begin([(own.at[pl.ds(j * aux, aux)], own_s.at[:, pl.ds(j * virt, virt)]) for j in range(2)], sem)
    level = levels[...].T
    finish(copies)
    own_t[...] = own_s[...].T
    add_pair(own_t, own_s, amp, total, level, levels[0:1, :], weights[0:1, :], True)


def sib_kernel(own_t, total_in, sib, levels, weights, total, sem, other, amp):
    aux, virt = sib.shape[0] // 2, sib.shape[1]
    copies = begin([(sib.at[pl.ds(j * aux, aux)], other.at[:, pl.ds(j * virt, virt)]) for j in range(2)], sem)
    level = levels[...].T
    finish(copies)
    add_pair(own_t, other, amp, total, level, levels[1:2, :], weights[1:2, :], False)


def fetch(plan, step, me, refs, other, skip=0):
    counts = []
    for side, (rows, (name, at)) in enumerate(plan):
        virt = other.shape[1] // len(plan)
        for source, first, n, to in rows:
            other[to:to + n, side * virt:(side + 1) * virt] = refs[source][first:first + n, :]
        wanted = -offsets_of(me)[STEPS[step][side + skip][0]]
        hits = jnp.where(refs[name][at:at + PAD, :].astype(F32)[0:1, :] == wanted.astype(F32), 1.0, 0.0)
        counts.append(jnp.broadcast_to(jnp.sum(hits, axis=1, keepdims=True), (1, virt)))
    return jnp.concatenate(counts, axis=1) if len(counts) > 1 else counts[0]


def first_far_kernel(plan, names, step, me_ref, own_t, levels, weights, *rest):
    refs = dict(zip(names, rest))
    total, other, amp = rest[len(names):]
    weight = weights[step:step + 1, :] - fetch(plan, step, me_ref[0], refs, other)
    add_pair(own_t, other, amp, total, levels[...].T, levels[step:step + 1, :], weight, True)


def far_kernel(plan, names, step, me_ref, own_t, levels, weights, total_in, *rest):
    refs = dict(zip(names, rest))
    total, other, amp = rest[len(names):]
    weight = weights[step:step + 1, :] - fetch(plan, step, me_ref[0], refs, other)
    add_pair(own_t, other, amp, total, levels[...].T, levels[step:step + 1, :], weight, False)


def segments(plane, which):
    side = plane // 18
    return (which * side * 5, side * 5), (side * 10 + which * side * 4, side * 4)


def rows_of(packed, base, plane, which):
    return jnp.concatenate(
        [packed[pl.ds(pl.multiple_of(base + a, 16), n), :] for a, n in segments(plane, which)]
    )


def near_metric_kernel(me_ref, total, own_s, keep, away, *rest):
    *sends, high, low, packed = rest
    parity, core, _ = place_of(me_ref[0])
    high[...] = total[...].astype(BF16)
    low[...] = (total[...] - high[...].astype(F32)).astype(BF16)
    aux = total.shape[0]
    half, quarter = aux // 2, aux // 4
    plane = packed.shape[0] // 2
    square = plane - half // LANES * quarter
    for q in range(0, aux, BLOCK):
        rows = q + BLOCK
        slab = own_s[q:q + BLOCK, :]
        block = lax.dot_general(high[:rows, :], slab, NT, preferred_element_type=F32)
        block += lax.dot_general(low[:rows, :], slab, NT, preferred_element_type=F32)
        for c in range(q, q + BLOCK, LANES):
            column = block[:, c - q:c - q + LANES]
            base, side = (half, 1) if c >= half else (0, 0)
            k = (c - base) // LANES
            at = side * plane + k * (k + 1) // 2 * LANES
            packed[at:at + (k + 1) * LANES, :] = column[base:c + LANES, :]
            if side:
                for s in range(2):
                    at = s * plane + square + k * quarter
                    packed[at:at + quarter, :] = column[s * quarter:(s + 1) * quarter, :]
    size = plane // 2

    def part(side, which):
        return rows_of(packed, side * plane, plane, which)

    keep[...] = part(parity, core)
    away[...] = part(1 - parity, core)
    given = [part(1 - parity, 1 - core), part(parity, 1 - core)]
    piece = size // 4
    for send, x in zip(sends, given):
        for t in range(4):
            encode(x[t * piece:(t + 1) * piece, :], send, t * (piece + PAD))


def half_kernel(plan, names, step, side, me_ref, own_t, levels, weights, total_in, *rest):
    refs = dict(zip(names, rest))
    total, other, amp = rest[len(names):]
    add_half(plan, refs, step, side, me_ref[0], own_t, levels, weights, total, other, amp)


def add_half(plan, refs, step, side, me, own_t, levels, weights, total, other, amp, halves=None, near=None):
    virt = other.shape[1]
    columns = slice(side * virt, (side + 1) * virt)
    count = fetch([plan[side]], step, me, refs, other, side)
    weight = weights[step:step + 1, columns] - count
    level = levels[step:step + 1, columns]
    add_pair(own_t, other, amp, total, levels[...].T, level, weight, False, halves, near)


def mirrored(high, low, own_s, first, n, q):
    rows, columns = pl.ds(pl.multiple_of(first, 16), n), pl.ds(pl.multiple_of(q, 16), BLOCK)
    pairs = ((high, own_s), (low, own_s), (own_s, high), (own_s, low))
    return sum(lax.dot_general(a[rows, :], b[columns, :], NT, preferred_element_type=F32) for a, b in pairs)


def last_kernel(plan, names, step, me_ref, own_t, levels, weights, total_in, own_s, near, *rest):
    refs = dict(zip(names, rest))
    total, residual, keep, send, high, low, sem, other, amp, packed = rest[len(names):]
    me = me_ref[0]
    parity, core, _ = place_of(me)
    aux, wide = total.shape
    virt = wide // 2
    add_half(plan, refs, step, 1, me, own_t, levels, weights, total, other, amp, (high, low), near)
    copies = begin([(total.at[:, pl.ds(j * virt, virt)], residual.at[j]) for j in range(2)], sem)
    half = aux // 2

    def both(first, n, q):
        return mirrored(high, low, own_s, first, n, q)

    at = 0
    for q in range(0, half, BLOCK):
        block = both(parity * half, q + BLOCK, parity * half + q)
        for c in range(0, BLOCK, LANES):
            upper = q + c + LANES
            packed[at:at + upper, :] = block[:upper, c:c + LANES]
            at += upper
    share(packed, core, keep, send)
    finish(copies)


def share(packed, core, keep, send):
    size = keep.shape[0]
    keep[...] = packed[pl.ds(pl.multiple_of(core * size, 16), size), :]
    send[...] = packed[pl.ds(pl.multiple_of((1 - core) * size, 16), size), :]


def corner_kernel(me_ref, high, low, own_s, keep, send, packed):
    parity, core, _ = place_of(me_ref[0])
    aux = own_s.shape[0]
    half, quarter = aux // 2, aux // 4
    at = 0
    for q in range(half, aux, BLOCK):
        block = mirrored(high, low, own_s, parity * quarter, quarter, q)
        for c in range(0, BLOCK, LANES):
            packed[at:at + quarter, :] = block[:, c:c + LANES]
            at += quarter
    share(packed, core, keep, send)


def powers(exponent):
    first = jnp.clip(exponent, -100.0, 100.0)
    return jnp.exp2(first), jnp.exp2(exponent - first)


def quantize(x, out, row):
    rows = x.shape[0]
    groups = x.reshape(rows // GROUP, GROUP, LANES)
    largest = jnp.max(jnp.abs(groups), axis=1)
    power = jnp.floor(jnp.log2(jnp.maximum(largest, 1e-37))) + 1.0
    a, b = powers(BITS - power)
    for g in range(rows // GROUP):
        whole = jnp.round(groups[g] * a[g:g + 1, :] * b[g:g + 1, :]).astype(I32)
        out[pl.ds(row + g * GROUP, GROUP), :] = whole.astype(I16)
    return power


def padded(power):
    return jnp.concatenate([power, jnp.zeros((PAD - power.shape[0], LANES), F32)])


def encode(x, out, row):
    power = quantize(x, out, row)
    out[pl.ds(row + x.shape[0], PAD), :] = padded(power).astype(I32).astype(I16)


def restore(coded, power):
    wide = coded.astype(I32).astype(F32)
    a, b = powers(power - BITS)
    return jnp.concatenate([
        wide[g * GROUP:(g + 1) * GROUP] * a[g:g + 1, :] * b[g:g + 1, :] for g in range(wide.shape[0] // GROUP)
    ])


def decode(coded):
    rows = coded.shape[0] - PAD
    return restore(coded[:rows], coded[rows:].astype(I32).astype(F32))


def chip_kernel(keep_in, away, got_away, got_keep, keep, send):
    piece = keep.shape[0] // 4
    for t in range(4):
        at, coded = pl.ds(t * piece, piece), pl.ds(t * (piece + PAD), piece + PAD)
        encode(away[at, :] + decode(got_away[coded, :]), send, t * (piece + PAD))
        keep[at, :] = keep_in[at, :] + decode(got_keep[coded, :])


def column_kernel(first, me_ref, mine, theirs, near, across, *rest):
    *given, keep, s1, s2, s3 = rest[:5] if first else rest[:4]
    sends = (s1, s2, s3)
    apart = None if first else rest[4]
    _, _, z = place_of(me_ref[0])

    def send(value, t):
        out = sends[t - 1]
        power = quantize(value, out, 0)
        if apart is not None:
            apart[t - 1] = padded(power)
        else:
            early = given[0][t - 1][:first // 4 // GROUP, :]
            both = padded(jnp.concatenate([early, power]))
            out[value.shape[0]:, :] = both.astype(I32).astype(I16)

    piece = keep.shape[0]
    away = across.shape[0] // 4
    far = jnp.concatenate([decode(across[i * away:(i + 1) * away, :]) for i in range(4)])
    for i in range(4):
        at = slice(i * piece, (i + 1) * piece)
        inner = slice(first + i * piece, first + (i + 1) * piece)
        value = (mine[at, :] + theirs[at, :]) + (near[inner, :] + far[inner, :])

        @pl.when(z == i)
        def _():
            keep[...] = value

        for t in (1, 2, 3):
            pl.when((z ^ t) == i)(functools.partial(send, value, t))


def sum_of(parts):
    (keep_a, *early), (keep_b, *late) = parts[:4], parts[4:]
    rows_a, rows_b = keep_a.shape[0], keep_b.shape[0]
    cut = rows_a // GROUP
    total_a, total_b = keep_a[...], keep_b[...]
    for a, b in zip(early, late):
        power = b[rows_b:, :].astype(I32).astype(F32)
        total_a += restore(a[...], power)
        total_b += restore(b[:rows_b, :], power[cut:, :])
    return jnp.concatenate([total_a, total_b])


def sum_kernel(*rest):
    rest[-1][...] = sum_of(rest[:-1])


def code_kernel(scale, x, out):
    encode(x[...] * scale, out, 0)


def sum_code_kernel(scale, *rest):
    encode(sum_of(rest[:-1]) * scale, rest[-1], 0)


def unpack(src, which, side, z, packed):
    plane = packed.shape[0] // 2
    for t in range(4):
        value = decode(src[3 - t])
        used = 0
        for first, n in ((which * (plane // 18) * 5, plane // 18 * 5), (plane // 18 * (10 + which * 4), plane // 18 * 4)):
            piece = n // 4
            row = side * plane + first + (z ^ t) * piece
            packed[pl.ds(pl.multiple_of(row, 16), piece), :] = value[used:used + piece, :]
            used += piece


def lay_corner(side, packed, square):
    aux = square.shape[0]
    half, quarter = aux // 2, aux // 4
    at = (side + 1) * (packed.shape[0] // 2) - half // LANES * quarter
    first = side * quarter
    for c in range(half, aux, LANES):
        square[first:first + quarter, c:c + LANES] = packed[at:at + quarter, :]
        for r in range(0, quarter, LANES):
            square[c:c + LANES, first + r:first + r + LANES] = packed[at + r:at + r + LANES, :].T
        at += quarter


def lay_triangle(side, packed, square, after=None):
    aux = square.shape[0]
    half, quarter = aux // 2, aux // 4
    at = (side + 1) * (packed.shape[0] // 2) - half // LANES * quarter
    base = side * half
    for c in range(half - LANES, -1, -LANES):
        at -= c + LANES
        columns = slice(base + c, base + c + LANES)
        square[base:base + c + LANES, columns] = packed[at:at + c + LANES, :]
        for r in range(0, c, LANES):
            square[columns, base + r:base + r + LANES] = packed[at + r:at + r + LANES, :].T
        if after is not None:
            after(base + c)


def write_plane(side, packed, square, out, sem):
    aux = square.shape[0]
    half, quarter = aux // 2, aux // 4
    first, base = side * quarter, side * half

    def copy(at, row, rows, column, columns):
        where = (pl.ds(row, rows), pl.ds(column, columns))
        started = pltpu.make_async_copy(square.at[where], out.at[where], sem.at[at])
        started.start()
        return started

    lay_corner(side, packed, square)
    copies = [copy(0, first, quarter, half, half), copy(1, half, half, first, quarter)]
    lay_triangle(
        side, packed, square, lambda row: copies.append(copy(2 + (row - base) // LANES, row, LANES, base, half))
    )
    finish(copies)


def unpack_kernel(me_ref, a, b, sib_a, out, packed, sem, square):
    parity, core, z = place_of(me_ref[0])
    for src, which, side in ((a, core, parity), (b, core, 1 - parity), (sib_a, 1 - core, parity)):
        unpack(src, which, side, z, packed)
    for side in range(2):
        pl.when(parity == side)(functools.partial(write_plane, side, packed, square, out, sem))


def spread_kernel(me_ref, out_in, packed_in, sib_b, out, packed, sem, square):
    parity, core, z = place_of(me_ref[0])
    unpack(sib_b, 1 - core, 1 - parity, z, packed)
    for side in range(2):
        pl.when(parity != side)(functools.partial(write_plane, side, packed, square, out, sem))


def shards(slabs, pair_blocks, occ_energy, virt_energy, domain_map):
    blocks = lax.axis_size("dom")
    me = lax.axis_index("dom").astype(I32)[None]
    own = slabs[0]
    orbitals, aux, virt = own.shape
    wide = orbitals * virt
    upper = aux * (aux + LANES) // 2 // LANES
    piece = upper // 16

    hbm = pl.BlockSpec(memory_space=pl.ANY)
    vmem = pl.BlockSpec(memory_space=pltpu.VMEM)
    smem = pl.BlockSpec(memory_space=pltpu.SMEM)
    slab_s = pltpu.VMEM((aux, wide), BF16)
    amp_s = pltpu.VMEM((wide, wide), BF16)
    total_t = jax.ShapeDtypeStruct((aux, wide), F32)

    def kernel(body, name, ins, outs, out_specs, scratch=(), limit=SMALL_LIMIT, aliases={}, flops=1):
        return pl.pallas_call(
            body,
            out_shape=outs,
            in_specs=ins,
            out_specs=out_specs,
            scratch_shapes=scratch,
            compiler_params=pltpu.CompilerParams(vmem_limit_bytes=limit),
            cost_estimate=pl.CostEstimate(flops=flops, bytes_accessed=1, transcendentals=0),
            input_output_aliases=aliases,
            name=name,
        )

    def dma(n):
        return pltpu.SemaphoreType.DMA((n,))

    def coded(n):
        return jax.ShapeDtypeStruct((n, LANES), I16)

    def plain(n):
        return jax.ShapeDtypeStruct((n, LANES), F32)

    flat = own.reshape(orbitals * aux, virt)
    cuts = [sum(PARTS[:i]) for i in range(len(PARTS) + 1)]
    count, early = len(PARTS), len(PARTS) - 2
    part = flat[:PARTS[0]]
    y = [swapped(part, 2)]
    sib_pairs = swapped(pair_blocks, 1)
    gives_y = ((me[0] >> 1) ^ me[0]) & 1 == 0
    later, part, gives_y = lax.optimization_barrier((flat, part, gives_y))
    sib = swapped(later, 1)
    parts = [None, *kernel(
        functools.partial(split_kernel, cuts[1:-1]), "split", [smem, smem, hbm],
        [jax.ShapeDtypeStruct((n + (0 if i else PAD), virt), BF16) for i, n in enumerate(PARTS[1:])],
        [vmem] * (count - 1), [dma(count - 1)],
    )(me, pair_blocks, later)]

    small = jax.ShapeDtypeStruct((8, wide), F32)
    energy = virt_energy.reshape(-1, LANES)
    levels, weights = kernel(
        functools.partial(prep_kernel, blocks), "prep", [smem] * 3 + [hbm] * 3, (small, small), (vmem, vmem),
        [dma(3), pltpu.VMEM((orbitals, blocks), F32), pltpu.VMEM(energy.shape, F32), pltpu.VMEM(domain_map.shape, I32)],
    )(me, pair_blocks, sib_pairs, occ_energy.T, energy, domain_map)
    sib, near_own = lax.optimization_barrier((sib, flat))
    own_t, own_s, total = kernel(
        own_kernel, "own", [hbm, vmem, vmem],
        (jax.ShapeDtypeStruct((wide, aux), BF16), jax.ShapeDtypeStruct((aux, wide), BF16), total_t), (vmem,) * 3,
        [dma(2), amp_s], LARGE_LIMIT, flops=int(2e10),
    )(near_own, levels, weights)
    sib, part = lax.optimization_barrier((sib, parts[1]))
    y.append(swapped(part, 2))
    y[0], total, own_t, sib, part = lax.optimization_barrier((y[0], total, own_t, sib, parts[2]))
    y.append(swapped(part, 2))
    z = [forwarded(y[0])]
    total = kernel(
        sib_kernel, "sib", [vmem, vmem, hbm, vmem, vmem], total_t, vmem, [dma(2), slab_s, amp_s], LARGE_LIMIT, {1: 0},
        int(1e10),
    )(own_t, total, sib, levels, weights)
    y[1], total, part = lax.optimization_barrier((y[1], total, parts[3]))
    y.append(swapped(part, 2))
    z.append(forwarded(y[1]))
    for i in range(4, count):
        y[i - 2], part, _ = lax.optimization_barrier((y[i - 2], parts[i], y[i - 3]))
        y.append(swapped(part, 2))
        z.append(forwarded(y[i - 2]))
    y[-3], near = lax.optimization_barrier((y[-3], total))
    keep, away, *sends = kernel(
        near_metric_kernel, "near_metric", [smem, vmem, vmem], (plain(upper // 4),) * 2 + (coded(4 * (piece + PAD)),) * 2,
        (vmem,) * 4, [slab_s, slab_s, pltpu.VMEM((upper, LANES), F32)], LARGE_LIMIT, flops=int(1e10),
    )(me, near, own_s)
    y[-2], z[0], keep = lax.optimization_barrier((y[-2], z[0], keep))
    z.append(forwarded(y[-2]))
    got = [swapped(send, 1) for send in sends]
    y[-1], *got = lax.optimization_barrier((y[-1], *got))
    z.append(forwarded(y[-1]))
    y[-1], keep, away = lax.optimization_barrier((y[-1], keep, away))
    keep, send = kernel(
        chip_kernel, "chip", [vmem] * 4, (plain(upper // 4), coded(4 * (piece + PAD))), (vmem, vmem),
    )(keep, away, *got)
    across = swapped(send, 2)
    (y[-1], own_t, keep), z[early:-1] = lax.optimization_barrier(((y[-1], own_t, keep), z[early:-1]))

    def given(rows_y, rows_z):
        return swapped(jnp.where(gives_y, jnp.concatenate(rows_y), jnp.concatenate(rows_z)), 1)

    arrays = {f"y{i}": part for i, part in enumerate(y)}
    arrays |= {f"z{i}": part for i, part in enumerate(z)}
    arrays["x0"] = given(y[:early], z[:early])

    def half_of(which, j):
        name = "y" if which == Y else "z"
        rows = []
        for i, (a, b) in enumerate(zip(cuts, cuts[1:])):
            first, last = max(a, j * aux), min(b, (j + 1) * aux)
            if first >= last:
                continue
            to = first - j * aux
            if which != X:
                rows.append((f"{name}{i}", first - a, last - first, to))
            elif i < early:
                rows.append(("x0", first + (PAD if i > 1 else 0), last - first, to))
            elif i == early:
                n = (b - a) // 2
                rows += [("x1", 0, n, to), ("x2", 0, b - a - n, to + n)]
            else:
                rows.append(("x3", 0, b - a, to))
        return rows, ("x0", cuts[2]) if which == X else (f"{name}1", PARTS[1])

    def pair_step(body, name, step, before=(), outs=(), out_specs=(), scratch=(), flops=1, side=None):
        plan = [half_of(*half) for half in STEPS[step]]
        used = plan if side is None else [plan[side]]
        names = list(dict.fromkeys(n for rows, (at, _) in used for n in [r[0] for r in rows] + [at]))
        return kernel(
            functools.partial(body, plan, names, step), name,
            [smem] + [vmem] * (3 + len(before) + len(names)),
            (total_t, *outs), (vmem, *out_specs), scratch, LARGE_LIMIT, {4: 0} if before else {}, flops,
        )(me, own_t, levels, weights, *before, *[arrays[n] for n in names])

    (total,) = pair_step(first_far_kernel, "far2", 2, scratch=[slab_s, amp_s], flops=int(1e10))
    (total,) = pair_step(far_kernel, "far3", 3, (total,), scratch=[slab_s, amp_s], flops=1)
    total, *late = lax.optimization_barrier((total, y[-2], z[-2]))
    late = jnp.where(gives_y, *late)
    middle = late.shape[0] // 2
    arrays["x1"], arrays["x2"] = swapped(late[:middle], 1), swapped(late[middle:], 1)
    z[-1], total, arrays["x1"], arrays["x2"], across = lax.optimization_barrier(
        (z[-1], total, arrays["x1"], arrays["x2"], across)
    )
    arrays[f"z{count - 1}"] = z[-1]
    arrays["x3"] = given(y[-1:], z[-1:])
    half_s = [pltpu.VMEM((aux, virt), BF16), pltpu.VMEM((wide, virt), BF16)]
    (total,) = pair_step(
        lambda *a: half_kernel(*a[:3], 0, *a[3:]), "half", 4, (total,), scratch=half_s, flops=int(1e9), side=0
    )
    plane = upper // 2
    (_, square), (_, corner) = segments(plane, 0)
    slab_t = jax.ShapeDtypeStruct((aux, wide), BF16)
    _, residual, mine, send, high, low = pair_step(
        last_kernel, "last", 4, (total, own_s, near),
        (jax.ShapeDtypeStruct(own.shape, F32), plain(square), plain(square), slab_t, slab_t), (hbm,) + (vmem,) * 4,
        [dma(2), *half_s, pltpu.VMEM((2 * square, LANES), F32)], side=1,
    )

    def column(first, size, mine, got, *given):
        n = size // 4
        apart = () if given else (jax.ShapeDtypeStruct((3, PAD, LANES), F32),)
        outs = (plain(n),) + (coded(n + (PAD if given else 0)),) * 3 + apart
        return kernel(
            functools.partial(column_kernel, first), "column", [smem] + [vmem] * (4 + len(given)), outs,
            (vmem,) * len(outs),
        )(me, mine, got, keep, across, *given)

    got = swapped(send, 1)
    mine_b, send_b = kernel(
        corner_kernel, "corner", [smem] + [vmem] * 3, (plain(corner), plain(corner)), (vmem, vmem),
        [pltpu.VMEM((2 * corner, LANES), F32)], LARGE_LIMIT, flops=int(2e9),
    )(me, high, low, own_s)
    got, send_b = lax.optimization_barrier((got, send_b))
    got_b = swapped(send_b, 1)
    keep_a, *sends_a, apart = column(0, square, mine, got)
    summed = [keep_a] + [swapped(sends_a[t - 1], 4 * t) for t in (3, 2, 1)]
    keep_b, *sends_b = column(square, corner, mine_b, got_b, apart)
    summed += [keep_b] + [swapped(sends_b[t - 1], 4 * t) for t in (3, 2, 1)]
    if blocks == 16:
        mine = kernel(
            functools.partial(sum_code_kernel, 1.0 / blocks), "sum_code", [vmem] * 8, coded(piece + PAD), vmem,
        )(*summed)
    else:
        value = kernel(sum_kernel, "sum", [vmem] * 8, plain(piece), vmem)(*summed)
        bit = 16
        while bit < blocks:
            value = value + swapped(value, bit)
            bit *= 2
        mine = kernel(functools.partial(code_kernel, 1.0 / blocks), "code", [vmem], coded(piece + PAD), vmem)(value)

    column = [mine] + [swapped(mine, 4 * t) for t in (1, 2, 3)]
    across = [swapped(c, 2) for c in column]
    a, b = jnp.stack(column[::-1]), jnp.stack(across[::-1])
    sib_a, sib_b = swapped(a, 1), swapped(b, 1)
    whole = jax.ShapeDtypeStruct((aux, aux), F32)
    scratch = [dma(2 + aux // 2 // LANES), pltpu.VMEM((aux, aux), F32)]
    gradient, packed = kernel(
        unpack_kernel, "unpack", [smem] + [vmem] * 3, (whole, plain(upper)), (hbm, vmem), scratch, flops=int(1e9),
    )(me, a, b, sib_a)
    gradient, _ = kernel(
        spread_kernel, "spread", [smem, hbm, vmem, vmem], (whole, plain(upper)), (hbm, vmem), scratch,
        aliases={1: 0, 2: 1},
    )(me, gradient, packed, sib_b)
    return residual[None], gradient


def solution(mesh):
    return jax.shard_map(
        shards,
        mesh=mesh,
        in_specs=(
            P(("grp", "dom"), None, None, None),
            P(("grp", "dom"), None),
            P("grp", None),
            P("grp"),
            P("grp", None),
        ),
        out_specs=(P(("grp", "dom"), None, None, None), P("grp", None)),
        check_vma=False,
    )
```
